32 devices in a mesh: seq: 4 (over x, core), blk: 8 (over z, y).
Axes of the slice: x: 2, y: 2, z: 4, core: 2. Of those that a mesh axis runs over, the one named last changes fastest.
Arguments:
- tokens: bfloat16 [4, 4096, 576], P('seq', 'blk'), may hold values from -6 to 6
- positions: int32 [4, 4096], P('seq', 'blk'), may hold values from 0 to 4095, as said below
- groups: int32 [4, 4096], P('seq', 'blk'), may hold values from 0 to 1
- keep_mask: int32 [4], P('seq'), may hold values from 0 to 1, as said below
- exit_scales: float32 [2], replicated, may hold values from 0.5 to 2
- keep_rate: float32 [1], replicated, may hold values from 1.1 to 2
- query_weight: bfloat16 [576, 576], replicated, may hold values from -0.25 to 0.25
- key_weight: bfloat16 [576, 192], replicated, may hold values from -0.25 to 0.25
- value_weight: bfloat16 [576, 192], replicated, may hold values from -0.25 to 0.25
- output_weight: bfloat16 [576, 576], replicated, may hold values from -4 to 4
- gate_weight: bfloat16 [576, 1536], replicated, may hold values from -0.25 to 0.25
- up_weight: bfloat16 [576, 1536], replicated, may hold values from -0.25 to 0.25
- down_weight: bfloat16 [1536, 576], replicated, may hold values from -0.15625 to 0.15625
- attention_gain: float32 [576], replicated, may hold values from 0.5 to 1.5
- feedforward_gain: float32 [576], replicated, may hold values from 0.5 to 1.5
- cotangent: bfloat16 [4, 4096, 576], P('seq', 'blk'), may hold values from -6 to 6
Outputs:
- layer_out: bfloat16 [4, 4096, 576], P('seq', 'blk')
- input_grad: float32 [4, 4096, 576], P('seq', 'blk')
- query_grad: float32 [576, 576], replicated
- key_grad: float32 [576, 192], replicated
- value_grad: float32 [576, 192], replicated
- output_grad: float32 [576, 576], replicated
- gate_grad: float32 [576, 1536], replicated
- up_grad: float32 [576, 1536], replicated
- down_grad: float32 [1536, 576], replicated
- attention_gain_grad: float32 [576], replicated
- feedforward_gain_grad: float32 [576], replicated
The draws below stay inside these ranges and needn't reach their ends.
Inputs may be any that keep to these rules, and one draw needn't show every extreme that they name: Within a sequence positions count up by one and fall back to 0 where a packed document begins; in one sequence, drawn from the seed, they never fall back. `keep_mask`: at least one sequence, drawn from the seed, runs the layer, and at least one other skips it.
All inputs are finite; a program needn't handle non-finite values.
Results may differ from the reference program's by a relative error of at most 0.015.
Values may be sent and summed in bfloat16 or wider, within the bound.
A program may use at most 192 MiB of HBM per device.

```python
import math
import jax
import jax.numpy as jnp
from jax import lax

D = 576
H = 9
KVH = 3
HD = 64
FF = 1536
GROUPS = 2
SPAN = 512
LENGTH = 4096
SEQUENCES = 4


def draw_positions(key, part):
    key_marks = jax.random.fold_in(key, 11)
    key_whole = jax.random.fold_in(key, 12)
    marked = jax.random.randint(key_marks, (SEQUENCES, LENGTH), 0, SPAN) == 0
    whole_seq = jax.random.randint(key_whole, (), 0, SEQUENCES)
    token_index = jnp.broadcast_to(jnp.arange(LENGTH, dtype=jnp.int32)[None, :], (SEQUENCES, LENGTH))
    seq_index = jnp.broadcast_to(jnp.arange(SEQUENCES, dtype=jnp.int32)[:, None], (SEQUENCES, LENGTH))
    starts = marked & (seq_index != whole_seq) | (token_index == 0)
    doc_first = lax.cummax(jnp.where(starts, token_index, 0), axis=1)
    return (token_index - doc_first).astype(jnp.int32)


def draw_keep_mask(key, part):
    key_bits = jax.random.fold_in(key, 21)
    key_kept = jax.random.fold_in(key, 22)
    key_skip = jax.random.fold_in(key, 23)
    random_bits = jax.random.randint(key_bits, (SEQUENCES,), 0, 2)
    kept_one = jax.random.randint(key_kept, (), 0, SEQUENCES)
    skipped_one = (kept_one + 1 + jax.random.randint(key_skip, (), 0, SEQUENCES - 1)) % SEQUENCES
    seq_index = jnp.arange(SEQUENCES, dtype=jnp.int32)
    return jnp.where(seq_index == kept_one, 1, jnp.where(seq_index == skipped_one, 0, random_bits)).astype(jnp.int32)


def set_ends(values, stream_key, smallest, top_value):
    place = [jax.random.randint(jax.random.fold_in(stream_key, axis), (), 0, length) for axis, length in enumerate(values.shape)]
    widest = values.shape.index(max(values.shape))
    beside = place[:widest] + [(place[widest] + 1) % values.shape[widest]] + place[widest + 1:]
    return values.at[tuple(place)].set(smallest).at[tuple(beside)].set(top_value)


def block_levels(rng, shape, cuts, smallest, top_value):
    level = 1.0
    for position, shards_of in cuts:
        heights = jax.random.uniform(jax.random.fold_in(jax.random.fold_in(rng, 6), position), (shards_of,), jnp.float32, smallest / len(cuts), top_value / len(cuts))
        level = level * jnp.repeat(jnp.exp(heights), shape[position] // shards_of).reshape((-1,) + (1,) * (len(shape) - 1 - position))
    return level


def normal_values(stream_key, extent, spread, bound, shards=(), kind=jnp.bfloat16):
    level = block_levels(stream_key, extent, shards, -0.22, 0.18) if shards else 1.0
    values = jax.random.normal(stream_key, extent, jnp.float32) * spread * level
    return jnp.minimum(jnp.maximum(values, -bound), bound).astype(kind)


def setup_inputs(seed: int = 0) -> dict:
    splits = jax.random.split(jax.random.key(seed), 17)
    return {
        "tokens": normal_values(splits[0], (SEQUENCES, LENGTH, D), 1.0, 6.0, ((0, 4), (1, 8))),
        "positions": draw_positions(jax.random.fold_in(splits[16], 71), 0),
        "groups": set_ends(jax.random.randint(splits[2], (SEQUENCES, LENGTH), 0, 2), jax.random.fold_in(splits[2], 1), 0, 1).astype(jnp.int32),
        "keep_mask": draw_keep_mask(jax.random.fold_in(splits[16], 71), 0),
        "exit_scales": jnp.clip(jnp.exp(jax.random.uniform(splits[4], (GROUPS,), jnp.float32, math.log(0.5), math.log(2.0))), 0.5, 2.0),
        "keep_rate": jnp.clip(jax.random.uniform(splits[5], (1,), jnp.float32, 1.1, 2.0), 1.1, 2.0),
        "query_weight": normal_values(splits[6], (D, H * HD), D ** -0.5, 0.25),
        "key_weight": normal_values(splits[7], (D, KVH * HD), D ** -0.5, 0.25),
        "value_weight": normal_values(splits[8], (D, KVH * HD), D ** -0.5, 0.25),
        "output_weight": normal_values(splits[9], (H * HD, D), 2.0 ** -0.5, 4.0),
        "gate_weight": normal_values(splits[10], (D, FF), D ** -0.5, 0.25),
        "up_weight": normal_values(splits[11], (D, FF), D ** -0.5, 0.25),
        "down_weight": normal_values(splits[12], (FF, D), FF ** -0.5, 0.15625),
        "attention_gain": jnp.clip(1.0 + 0.1 * jax.random.normal(splits[13], (D,), jnp.float32), 0.5, 1.5),
        "feedforward_gain": jnp.clip(1.0 + 0.1 * jax.random.normal(splits[14], (D,), jnp.float32), 0.5, 1.5),
        "cotangent": normal_values(splits[15], (SEQUENCES, LENGTH, D), 1.0, 6.0, ((0, 4), (1, 8))),
    }


EXACT = lax.Precision.HIGHEST
EPSILON = 1e-05
ROPE_BASE = 100000.0
MASKED = -1e+30

@jax.custom_vjp
def low(v):
    return lax.optimization_barrier(v.astype(jnp.bfloat16)).astype(jnp.float32)

@jax.custom_vjp
def low_back(v):
    return v

def low_keep(v):
    return (low(v), None)

def low_pass(kept, grad):
    return (grad,)

def back_keep(v):
    return (v, None)

def back_low(kept, grad):
    return (low(grad),)
low.defvjp(low_keep, low_pass)
low_back.defvjp(back_keep, back_low)

def rms_norm(values, gain):
    return values * lax.rsqrt(lax.optimization_barrier(jnp.mean(values * values, axis=-1, keepdims=True)) + EPSILON) * gain

def angles(positions):
    halfway = HD // 2
    frequency = 1.0 / ROPE_BASE ** (jnp.arange(halfway, dtype=jnp.float32) * (2.0 / HD))
    turned = positions.astype(jnp.float32)[:, None] * frequency[None, :]
    return (jnp.cos(turned), jnp.sin(turned))

def rotate(values, cosine, sine_vals):
    halfway = values.shape[-1] // 2
    front_half = values[..., :halfway]
    behind = values[..., halfway:]
    cos_part = cosine[:, None, :]
    sin_part = sine_vals[:, None, :]
    return jnp.concatenate([front_half * cos_part - behind * sin_part, behind * cos_part + front_half * sin_part], axis=-1)

def attention(queries, keys, values):
    group_size = H // KVH
    query_block = math.gcd(LENGTH, 512)
    block_count = LENGTH // query_block
    key_heads = keys.reshape(LENGTH, KVH, HD)
    value_heads = values.reshape(LENGTH, KVH, HD)
    key_index = jnp.arange(LENGTH, dtype=jnp.int32)

    def one_block(inputs):
        query_rows, first_row = inputs
        query_heads = query_rows.reshape(query_block, KVH, group_size, HD)
        scores = jnp.einsum('qkgd,tkd->kgqt', query_heads, key_heads, precision=EXACT) * HD ** (-0.5)
        scores = low_back(scores)
        causal = (first_row + jnp.arange(query_block, dtype=jnp.int32))[:, None] >= key_index[None, :]
        scores = jnp.where(causal, scores, MASKED)
        row_max = lax.optimization_barrier(jnp.max(scores, axis=-1, keepdims=True))
        exponent = jnp.where(causal, jnp.exp(scores - row_max), 0.0)
        probability = low(exponent / lax.optimization_barrier(jnp.sum(exponent, axis=-1, keepdims=True)))
        result = jnp.einsum('kgqt,tkd->qkgd', probability, value_heads, precision=EXACT)
        return result.reshape(query_block, H * HD)
    starts = jnp.arange(block_count, dtype=jnp.int32) * query_block
    results = lax.map(jax.checkpoint(one_block), (queries.reshape(block_count, query_block, H * HD), starts))
    return results.reshape(LENGTH, H * HD)

def block_forward(inputs, query_weight, key_weight, value_weight, output_weight, gate_weight, up_weight, down_weight, attention_gain, feedforward_gain, cosine, sine_vals, branch_scale):
    normed = low(rms_norm(inputs, attention_gain))
    query_raw = low_back(jnp.dot(normed, query_weight, precision=EXACT))
    key_raw = low_back(jnp.dot(normed, key_weight, precision=EXACT))
    value_raw = low_back(jnp.dot(normed, value_weight, precision=EXACT))
    queries = low(rotate(query_raw.reshape(LENGTH, H, HD), cosine, sine_vals).reshape(LENGTH, H * HD))
    keys = low(rotate(key_raw.reshape(LENGTH, KVH, HD), cosine, sine_vals).reshape(LENGTH, KVH * HD))
    values = low(value_raw)
    mixed = low(low_back(attention(queries, keys, values)))
    branch = low_back(jnp.dot(mixed, output_weight, precision=EXACT))
    hidden_state = inputs + branch_scale * branch
    normed2 = low(rms_norm(hidden_state, feedforward_gain))
    gate = low_back(jnp.dot(normed2, gate_weight, precision=EXACT))
    up_proj = low_back(jnp.dot(normed2, up_weight, precision=EXACT))
    act = low(jax.nn.silu(gate) * up_proj)
    down = low_back(jnp.dot(act, down_weight, precision=EXACT))
    return hidden_state + branch_scale * down

def reference(tokens, positions, groups, keep_mask, exit_scales, keep_rate, query_weight, key_weight, value_weight, output_weight, gate_weight, up_weight, down_weight, attention_gain, feedforward_gain, cotangent):
    weights = (query_weight.astype(jnp.float32), key_weight.astype(jnp.float32), value_weight.astype(jnp.float32), output_weight.astype(jnp.float32), gate_weight.astype(jnp.float32), up_weight.astype(jnp.float32), down_weight.astype(jnp.float32), attention_gain.astype(jnp.float32), feedforward_gain.astype(jnp.float32))

    def per_sequence(summed, inputs_seq):
        token_rows, position_row, group_row, keep_one, cot_rows = inputs_seq
        cosine, sine_vals = angles(position_row)
        branch_scale = keep_one.astype(jnp.float32) * keep_rate[0]

        def forward(inputs, *params):
            return block_forward(inputs, *params, cosine, sine_vals, branch_scale)
        output, pullback = jax.vjp(forward, token_rows.astype(jnp.float32), *weights)
        group_scale = jnp.where(group_row == 1, exit_scales[1], exit_scales[0])
        seed_grad = cot_rows.astype(jnp.float32) * group_scale[:, None]
        gradients = pullback(seed_grad)
        summed = tuple((left + right for left, right in zip(summed, gradients[1:])))
        return (summed, (output.astype(jnp.bfloat16), gradients[0]))
    zeros = tuple((jnp.zeros(weight.shape, jnp.float32) for weight in weights))
    summed, (outputs, input_grads) = lax.scan(per_sequence, zeros, (tokens, positions, groups, keep_mask, cotangent))
    return (outputs, input_grads, summed[0], summed[1], summed[2], summed[3], summed[4], summed[5], summed[6], summed[7], summed[8])
```

```python
import functools

import jax
import jax.numpy as jnp
from jax import lax
from jax.experimental import pallas as pl
from jax.experimental.pallas import tpu as pltpu
from jax.sharding import PartitionSpec as P

H = 9
KVH = 3
HD = 64
GROUP = H // KVH
HALF = HD // 2
PAIR = 2 * HD

EPSILON = 1e-05
ROPE_BASE = 100000.0
MASKED = -1e30
LOG2E = 1.4426950408889634
LN2 = 0.6931471805599453
F32 = jnp.float32
BF16 = jnp.bfloat16
VMEM_LIMIT = 56 * 1024 * 1024


def nn(a, b):
    return lax.dot_general(a, b, (((1,), (0,)), ((), ())), preferred_element_type=F32)


def nt(a, b):
    return lax.dot_general(a, b, (((1,), (1,)), ((), ())), preferred_element_type=F32)


def inverse_rms(values):
    return lax.rsqrt(jnp.mean(values * values, axis=-1, keepdims=True) + EPSILON)


def turn(rows, cos, sin):
    u, w = rows[:HALF], rows[HALF:]
    return jnp.concatenate([u * cos - w * sin, w * cos + u * sin], axis=0)


def project(tokens, gain, wq, wk, wv, cos, sin, queries, kv):
    x = tokens[...].astype(F32)
    normed = (x * inverse_rms(x) * gain[...]).astype(BF16)
    c, s = cos[...], sin[...]
    keys = nt(wk[...].T, normed)
    vals = nt(wv[...].T, normed)
    for g in range(KVH):
        kv[g * PAIR : g * PAIR + HD, :] = turn(keys[g * HD : (g + 1) * HD], c, s).astype(BF16)
        kv[g * PAIR + HD : (g + 1) * PAIR, :] = vals[g * HD : (g + 1) * HD].astype(BF16)
    raw = nt(wq[...].T, normed)
    factor = HD**-0.5 * LOG2E
    for h in range(H):
        turned = turn(raw[h * HD : (h + 1) * HD], c, s) * factor
        queries[h // GROUP, h % GROUP, :HD, :] = turned.astype(BF16)
        queries[h // GROUP, h % GROUP, HD:, :] = jnp.zeros((HD, x.shape[0]), BF16)


def first_block(queries, kv, out, top, total):
    rows = queries.shape[-1]
    part = rows // 2

    def one_group(g, carry):
        packed = kv[pl.ds(pl.multiple_of(g * PAIR, PAIR), PAIR), :]
        natural = packed.T
        for r in range(GROUP):
            for c in range(2):
                seen = (c + 1) * part
                cols = slice(c * part, seen)
                scores = nn(natural[:seen], queries[g, r, :, cols])
                key_at = lax.broadcasted_iota(jnp.int32, scores.shape, 0)
                query_at = lax.broadcasted_iota(jnp.int32, scores.shape, 1) + c * part
                scores = jnp.where(key_at <= query_at, scores, MASKED)
                high = jnp.max(scores, axis=0, keepdims=True)
                probs = jnp.exp2(scores - high)
                top[g, r, :, cols] = high
                total[g, r, :, cols] = jnp.sum(probs, axis=0, keepdims=True)
                out[g, r, :, cols] = nn(packed[HD:, :seen], probs.astype(BF16))
        return carry

    lax.fori_loop(0, KVH, one_group, 0)


def next_block(queries, kv, out, top, total):
    rows = queries.shape[-1]
    part = rows // 2

    def one_group(g, carry):
        packed = kv[pl.ds(pl.multiple_of(g * PAIR, PAIR), PAIR), :]
        natural = packed.T
        for r in range(GROUP):
            for c in range(2):
                cols = slice(c * part, (c + 1) * part)
                scores = nn(natural, queries[g, r, :, cols])
                old = top[g, r, :, cols]
                high = jnp.maximum(old, jnp.max(scores, axis=0, keepdims=True))
                probs = jnp.exp2(scores - high)
                fade = jnp.exp2(old - high)
                top[g, r, :, cols] = high
                total[g, r, :, cols] = total[g, r, :, cols] * fade + jnp.sum(
                    probs, axis=0, keepdims=True
                )
                out[g, r, :, cols] = out[g, r, :, cols] * fade + nn(
                    packed[HD:], probs.astype(BF16)
                )
        return carry

    lax.fori_loop(0, KVH, one_group, 0)


def finish_forward(out, top, total, mixed_t, lse):
    for h in range(H):
        g, r = h // GROUP, h % GROUP
        scaled = out[g, r] / total[g, r]
        out[g, r] = scaled
        mixed_t[h * HD : (h + 1) * HD, :] = scaled.astype(BF16)
        lse[g, r] = top[g, r] + jnp.log2(total[g, r])


def feed_forward(
    tokens, seed_scale, scale, wo, wg, wu, wd, gain2, cotangent, mixed_t, attended,
    layer_out, d_hidden, gate_grad, up_grad, down_grad, output_grad, gain2_grad,
    d_out, d_out_t, delta, d_normed2, down,
):
    bs = scale[0, 0]
    x = tokens[...].astype(F32)
    mixed = mixed_t[...].T
    hidden = x + bs * nn(mixed, wo[...])
    r2 = inverse_rms(hidden)
    normed2 = (hidden * r2 * gain2[...]).astype(BF16)
    normed2_t = normed2.T
    seed = cotangent[...].astype(F32) * seed_scale[...]
    d_down = (bs * seed).astype(BF16)
    ff = wg.shape[1]
    step = 512
    down[...] = jnp.zeros_like(down)
    d_normed2[...] = jnp.zeros_like(d_normed2)

    def chunk(f, carry):
        at = pl.ds(pl.multiple_of(f * step, step), step)
        gate = nn(normed2, wg[:, at])
        up = nn(normed2, wu[:, at])
        sig = 1.0 / (1.0 + jnp.exp(-gate))
        silu = gate * sig
        act = (silu * up).astype(BF16)
        d_act = nt(d_down, wd[at, :])
        d_gate = (d_act * up * (sig * (1.0 + gate * (1.0 - sig)))).astype(BF16)
        d_up = (d_act * silu).astype(BF16)
        down_grad[at, :] = nn(act.T, d_down).astype(down_grad.dtype)
        gate_grad[:, at] = nn(normed2_t, d_gate).astype(gate_grad.dtype)
        up_grad[:, at] = nn(normed2_t, d_up).astype(up_grad.dtype)
        down[...] += nn(act, wd[at, :])
        d_normed2[...] += nt(d_gate, wg[:, at]) + nt(d_up, wu[:, at])
        return carry

    lax.fori_loop(0, ff // step, chunk, 0)
    layer_out[...] = (hidden + bs * down[...]).astype(BF16)
    dn = d_normed2[...]
    gain2_grad[...] = jnp.sum(dn * hidden * r2, axis=0, keepdims=True)
    gained = gain2[...] * dn
    dh = seed + r2 * gained - hidden * (r2 * r2 * r2) * jnp.mean(gained * hidden, axis=-1, keepdims=True)
    d_hidden[...] = dh
    d_branch = (bs * dh).astype(BF16)
    output_grad[...] = nn(mixed_t[...], d_branch).astype(output_grad.dtype)
    d_mixed_t = nt(wo[...], d_branch).astype(BF16)
    rows = x.shape[0]
    for h in range(H):
        g, r = h // GROUP, h % GROUP
        head = d_mixed_t[h * HD : (h + 1) * HD]
        d_out_t[g, r, :HD, :] = jnp.zeros((HD, rows), BF16)
        d_out_t[g, r, HD:, :] = head
        d_out[g, r] = d_out_t[g, r].T
        delta[g, r] = jnp.sum(head.astype(F32) * attended[g, r], axis=0, keepdims=True)


def block_grads(queries, natural_q, d_out_t, d_out, lse, delta, kv, dq, store, masked):
    rows = queries.shape[-1]
    part = rows // 2

    def one_group(g, carry):
        packed = kv[pl.ds(pl.multiple_of(g * PAIR, PAIR), PAIR), :]
        natural = packed.T
        acc = None
        for r in range(GROUP):
            pieces = []
            for c in range(2):
                cols = slice(c * part, (c + 1) * part)
                scores = nn(natural, queries[g, r, :, cols])
                probs = jnp.exp2(scores - lse[g, r, :, cols])
                if masked:
                    key_at = lax.broadcasted_iota(jnp.int32, scores.shape, 0)
                    query_at = lax.broadcasted_iota(jnp.int32, scores.shape, 1) + c * part
                    probs = jnp.where(key_at <= query_at, probs, 0.0)
                d_probs = nn(natural, d_out_t[g, r, :, cols])
                d_scores = (probs * (d_probs - delta[g, r, :, cols])).astype(BF16)
                dq[g, r, :, cols] += nn(packed[:HD], d_scores)
                term = nn(probs.astype(BF16), d_out[g, r, cols, :]) + nn(
                    d_scores, natural_q[g, r, cols, :]
                )
                acc = term if acc is None else acc + term
        store(g, acc)
        return carry

    lax.fori_loop(0, KVH, one_group, 0)


def finish(
    tokens, gain, wq, wk, wv, cos, sin, dq, d_kv, d_hidden,
    input_grad, query_grad, key_grad, value_grad, gain_grad, turned,
):
    x = tokens[...].astype(F32)
    r1 = inverse_rms(x)
    normed_t = (x * r1 * gain[...]).astype(BF16).T
    c, s = cos[...], -sin[...]
    nq, nk = H * HD, KVH * HD
    for h in range(H):
        rows = dq[h // GROUP, h % GROUP] * HD**-0.5
        turned[h * HD : (h + 1) * HD, :] = turn(rows, c, s).astype(BF16)
    for g in range(KVH):
        both = d_kv[g].T
        turned[nq + g * HD : nq + (g + 1) * HD, :] = turn(both[:HD] * LN2, c, s).astype(BF16)
        turned[nq + nk + g * HD : nq + nk + (g + 1) * HD, :] = both[HD:].astype(BF16)
    d_normed_t = (
        nn(wq[...], turned[:nq, :])
        + nn(wk[...], turned[nq : nq + nk, :])
        + nn(wv[...], turned[nq + nk :, :])
    )
    query_grad[...] = nt(normed_t, turned[:nq, :]).astype(query_grad.dtype)
    key_grad[...] = nt(normed_t, turned[nq : nq + nk, :]).astype(key_grad.dtype)
    value_grad[...] = nt(normed_t, turned[nq + nk :, :]).astype(value_grad.dtype)
    d_normed = d_normed_t.T
    gain_grad[...] = jnp.sum(d_normed * x * r1, axis=0, keepdims=True)
    gained = gain[...] * d_normed
    input_grad[...] = (
        d_hidden[...] + r1 * gained - x * (r1 * r1 * r1) * jnp.mean(gained * x, axis=-1, keepdims=True)
    )


def project_kernel(tokens, gain, wq, wk, wv, cos, sin, queries, kv):
    project(tokens, gain, wq, wk, wv, cos, sin, queries, kv)


def forward_kernel(queries, kv_all, attended, mixed_t, lse, top, total):
    me = lax.axis_index("blk")
    first_block(queries, kv_all.at[me], attended, top, total)

    def step(i, carry):
        next_block(queries, kv_all.at[me - 1 - i], attended, top, total)
        return carry

    lax.fori_loop(0, me, step, 0)
    finish_forward(attended, top, total, mixed_t, lse)


def backward_kernel(queries, kv_all, d_out_t, d_out, lse, delta, dq, d_kv, natural_q):
    me = lax.axis_index("blk")
    dq[...] = jnp.zeros_like(dq)
    d_kv[...] = jnp.zeros_like(d_kv)
    for h in range(H):
        natural_q[h // GROUP, h % GROUP] = queries[h // GROUP, h % GROUP].T

    def run(j, masked):
        def store(g, value):
            d_kv[j, g] = value.astype(d_kv.dtype)

        block_grads(
            queries, natural_q, d_out_t, d_out, lse, delta, kv_all.at[j], dq, store, masked
        )

    def step(j, carry):
        run(j, False)
        return carry

    lax.fori_loop(0, me, step, 0)
    run(me, True)


def call(kernel, outs, scratch=(), smem=()):
    def run(*args):
        return pl.pallas_call(
            kernel,
            out_shape=[jax.ShapeDtypeStruct(s, t) for s, t in outs],
            in_specs=[
                pl.BlockSpec(memory_space=pltpu.SMEM if i in smem else pltpu.VMEM)
                for i in range(len(args))
            ],
            out_specs=[pl.BlockSpec(memory_space=pltpu.VMEM)] * len(outs),
            scratch_shapes=[pltpu.VMEM(s, t) for s, t in scratch],
            compiler_params=pltpu.CompilerParams(vmem_limit_bytes=VMEM_LIMIT),
        )(*args)

    return run


def body(blocks, tokens, positions, groups, keep_mask, exit_scales, keep_rate, wq, wk, wv, wo, wg, wu, wd, gain1, gain2, cotangent):
    tokens, cotangent = tokens[0], cotangent[0]
    rows, width = tokens.shape
    ff = wg.shape[1]
    nq, nk = H * HD, KVH * HD
    frequency = 1.0 / ROPE_BASE ** (jnp.arange(HALF, dtype=F32) * (2.0 / HD))
    angle = frequency[:, None] * positions[0].astype(F32)[None, :]
    cos, sin = jnp.cos(angle), jnp.sin(angle)
    seed_scale = jnp.where(groups[0] == 1, exit_scales[1], exit_scales[0])[:, None]
    scale = (keep_mask.astype(F32) * keep_rate)[None, :]
    gain1, gain2 = gain1[None, :], gain2[None, :]

    head_t = (KVH, GROUP, PAIR, rows)
    head_n = (KVH, GROUP, rows, PAIR)
    head_o = (KVH, GROUP, HD, rows)
    head_1 = (KVH, GROUP, 1, rows)
    queries, kv = call(project_kernel, [(head_t, BF16), ((KVH * PAIR, rows), BF16)])(
        tokens, gain1, wq, wk, wv, cos, sin
    )
    kv_all = lax.all_gather(kv, "blk", axis=0)
    attended, mixed_t, lse = call(
        forward_kernel,
        [(head_o, F32), ((nq, rows), BF16), (head_1, F32)],
        [(head_1, F32), (head_1, F32)],
    )(queries, kv_all)
    (layer_out, d_hidden, gate_grad, up_grad, down_grad, output_grad, gain2_grad, d_out, d_out_t, delta) = call(
        feed_forward,
        [
            ((rows, width), BF16),
            ((rows, width), F32),
            ((width, ff), BF16),
            ((width, ff), BF16),
            ((ff, width), BF16),
            ((nq, width), BF16),
            ((1, width), F32),
            (head_n, BF16),
            (head_t, BF16),
            (head_1, F32),
        ],
        [((rows, width), F32), ((rows, width), F32)],
        smem=(2,),
    )(tokens, seed_scale, scale, wo, wg, wu, wd, gain2, cotangent, mixed_t, attended)
    early = lax.psum((gate_grad, up_grad, down_grad, output_grad), ("seq", "blk"))
    dq, d_kv = call(
        backward_kernel,
        [(head_o, F32), ((blocks, KVH, rows, PAIR), BF16)],
        [(head_n, BF16)],
    )(queries, kv_all, d_out_t, d_out, lse, delta)
    d_kv = lax.psum_scatter(d_kv, "blk", scatter_dimension=0, tiled=False).astype(F32)
    input_grad, query_grad, key_grad, value_grad, gain1_grad = call(
        finish,
        [
            ((rows, width), F32),
            ((width, nq), BF16),
            ((width, nk), BF16),
            ((width, nk), BF16),
            ((1, width), F32),
        ],
        [((nq + 2 * nk, rows), BF16)],
    )(tokens, gain1, wq, wk, wv, cos, sin, dq, d_kv, d_hidden)
    late = lax.psum((query_grad, key_grad, value_grad), ("seq", "blk"))
    gains = lax.psum(jnp.concatenate([gain1_grad, gain2_grad], axis=0), ("seq", "blk"))
    return (
        layer_out[None],
        input_grad[None],
        late[0].astype(F32),
        late[1].astype(F32),
        late[2].astype(F32),
        early[3].astype(F32),
        early[0].astype(F32),
        early[1].astype(F32),
        early[2].astype(F32),
        gains[0],
        gains[1],
    )


def solution(mesh):
    local = P("seq", "blk", None)
    pair = P("seq", "blk")
    placed = (local, pair, pair, P("seq")) + (P(),) * 11 + (local,)
    return jax.shard_map(
        functools.partial(body, mesh.shape["blk"]),
        mesh=mesh,
        in_specs=placed,
        out_specs=(local, local) + (P(),) * 9,
        check_vma=False,
    )
```

```python
import functools

import jax
import jax.numpy as jnp
from jax import lax
from jax.experimental import pallas as pl
from jax.experimental.pallas import tpu as pltpu
from jax.sharding import PartitionSpec as P

H = 9
KVH = 3
HD = 64
GROUP = H // KVH
HALF = HD // 2
PAIR = 2 * HD

EPSILON = 1e-05
ROPE_BASE = 100000.0
MASKED = -1e30
LOG2E = 1.4426950408889634
LN2 = 0.6931471805599453
F32 = jnp.float32
BF16 = jnp.bfloat16
VMEM_LIMIT = 56 * 1024 * 1024
MESH = pl.DeviceIdType.MESH


def nn(a, b):
    return lax.dot_general(a, b, (((1,), (0,)), ((), ())), preferred_element_type=F32)


def nt(a, b):
    return lax.dot_general(a, b, (((1,), (1,)), ((), ())), preferred_element_type=F32)


def column(row):
    return jnp.broadcast_to(row, (8, row.shape[1])).T[:, :1]


def inverse_rms(values):
    return lax.rsqrt(jnp.mean(values * values, axis=0, keepdims=True) + EPSILON)


def turn(rows, cos, sin):
    u, w = rows[:HALF], rows[HALF:]
    return jnp.concatenate([u * cos - w * sin, w * cos + u * sin], axis=0)


def normalize(tokens, gain):
    x = tokens[...].astype(F32)
    return (x * inverse_rms(x) * column(gain[...])).astype(BF16)


def project_kv(normed, wk, wv, cos, sin, kv):
    keys = nn(wk[...], normed)
    vals = nn(wv[...], normed)
    for g in range(KVH):
        span = slice(g * HD, (g + 1) * HD)
        kv[g, :HD, :] = turn(keys[span], cos, sin).astype(BF16)
        kv[g, HD:, :] = vals[span].astype(BF16)


def project_q(normed, wq, cos, sin, queries):
    raw = nn(wq[...].T, normed)
    factor = HD**-0.5 * LOG2E
    for h in range(H):
        turned = turn(raw[h * HD : (h + 1) * HD], cos, sin) * factor
        queries[h // GROUP, h % GROUP, :HD, :] = turned.astype(BF16)
        queries[h // GROUP, h % GROUP, HD:, :] = jnp.zeros((HD, raw.shape[1]), BF16)


def values_and_ones(packed):
    ones = jnp.ones((16, packed.shape[1]), BF16)
    return jnp.concatenate([packed[HD:], ones], axis=0)


def first_unit(g, queries, packed, out, top, total):
    rows = queries.shape[-1]
    part = rows // 2
    natural = packed.T
    values = values_and_ones(packed)
    items = [(r, c) for r in range(GROUP) for c in range(2)]

    def scores_of(i):
        r, c = items[i]
        return nn(natural[: (c + 1) * part], queries[g, r, :, c * part : (c + 1) * part])

    scores = scores_of(0)
    done = []
    for i, (r, c) in enumerate(items):
        later = scores_of(i + 1) if i + 1 < len(items) else None
        key_at = lax.broadcasted_iota(jnp.int32, scores.shape, 0)
        query_at = lax.broadcasted_iota(jnp.int32, scores.shape, 1) + c * part
        scores = jnp.where(key_at <= query_at, scores, MASKED)
        high = jnp.max(scores, axis=0, keepdims=True)
        probs = jnp.exp2(scores - high)
        done.append((high, nn(values[:, : (c + 1) * part], probs.astype(BF16))))
        scores = later
    for (r, c), (high, summed) in zip(items, done):
        cols = slice(c * part, (c + 1) * part)
        top[g, r, :, cols] = high
        total[g, r, :, cols] = summed[HD : HD + 1]
        out[g, r, :, cols] = summed[:HD]


def next_unit(g, queries, packed, out, top, total):
    natural = packed.T
    values = values_and_ones(packed)
    before = [(top[g, r], total[g, r], out[g, r]) for r in range(GROUP)]
    scores = [nn(natural, queries[g, r]) for r in range(2)]
    done = []
    for r in range(GROUP):
        if r + 2 < GROUP:
            scores.append(nn(natural, queries[g, r + 2]))
        old, count, acc = before[r]
        high = jnp.maximum(old, jnp.max(scores[r], axis=0, keepdims=True))
        probs = jnp.exp2(scores[r] - high)
        fade = jnp.exp2(old - high)
        summed = nn(values, probs.astype(BF16))
        done.append((high, count * fade + summed[HD : HD + 1], acc * fade + summed[:HD]))
    for r, (high, count, acc) in enumerate(done):
        top[g, r] = high
        total[g, r] = count
        out[g, r] = acc


def finish_forward(out, top, total, mixed_t, lse):
    for h in range(H):
        g, r = h // GROUP, h % GROUP
        scaled = out[g, r] * (1.0 / total[g, r])
        out[g, r] = scaled
        mixed_t[h * HD : (h + 1) * HD, :] = scaled.astype(BF16)
        lse[g, r] = top[g, r] + jnp.log2(total[g, r])


def forward_kernel(
    blocks, tokens, gain, wq, wk, wv, cos, sin,
    queries, kv_all, attended, mixed_t, lse,
    top, total, send_sem, recv_sem,
):
    s, b = lax.axis_index("seq"), lax.axis_index("blk")
    z, y, floors = b // 2, b % 2, blocks // 2
    above, below, across = (s, b + 2), (s, b - 2), (s, b + 1 - 2 * y)
    has_above, has_below = z < floors - 1, z > 0

    barrier = pltpu.get_barrier_semaphore()
    pl.semaphore_signal(barrier, inc=1, device_id=across, device_id_type=MESH)

    @pl.when(has_above)
    def _():
        pl.semaphore_signal(barrier, inc=1, device_id=above, device_id_type=MESH)

    @pl.when(has_below)
    def _():
        pl.semaphore_signal(barrier, inc=1, device_id=below, device_id_type=MESH)

    def copy(kind, j, g):
        return pltpu.make_async_remote_copy(
            src_ref=kv_all.at[j, g],
            dst_ref=kv_all.at[j, g],
            send_sem=send_sem.at[kind, j, g],
            recv_sem=recv_sem.at[j, g],
            device_id=above if kind == 0 else across,
            device_id_type=MESH,
        )

    normed = normalize(tokens, gain)
    c, sn = cos[...], sin[...]
    project_kv(normed, wk, wv, c, sn, kv_all.at[b])
    pl.semaphore_wait(barrier, 1 + has_above.astype(jnp.int32) + has_below.astype(jnp.int32))

    def send_own(g, carry):
        @pl.when(has_above)
        def _():
            copy(0, b, g).start()

        @pl.when(y == 0)
        def _():
            copy(1, b, g).start()

        return carry

    lax.fori_loop(0, KVH, send_own, 0)
    project_q(normed, wq, c, sn, queries)

    def own(g, carry):
        first_unit(g, queries, kv_all[b, g], attended, top, total)
        return carry

    lax.fori_loop(0, KVH, own, 0)

    def level(m, carry):
        def one(g, inner):
            @pl.when(m <= z)
            def _():
                j = b - 2 * m
                copy(0, j, g).wait_recv()

                @pl.when(has_above)
                def _():
                    copy(0, j, g).start()

                copy(1, j, g).start()
                next_unit(g, queries, kv_all[j, g], attended, top, total)

            @pl.when((m >= 2) | (y == 1))
            def _():
                j = b - 2 * m + 3 - 2 * y
                copy(1, j, g).wait_recv()
                next_unit(g, queries, kv_all[j, g], attended, top, total)

            return inner

        return lax.fori_loop(0, KVH, one, carry)

    lax.fori_loop(1, z + 2, level, 0)
    finish_forward(attended, top, total, mixed_t, lse)

    def drain(m, carry):
        def one(g, inner):
            j = b - 2 * m

            @pl.when(has_above)
            def _():
                copy(0, j, g).wait_send()

            @pl.when((m >= 1) | (y == 0))
            def _():
                copy(1, j, g).wait_send()

            return inner

        return lax.fori_loop(0, KVH, one, carry)

    lax.fori_loop(0, z + 1, drain, 0)


def feed_forward(
    tokens, seed_scale, scale, wo, wg, wu, wd, gain2, cotangent, mixed_t, attended,
    layer_out, d_hidden, gate_grad, up_grad, down_grad, output_grad, gain2_grad,
    d_out, delta, d_normed2, down,
):
    bs = scale[0, 0]
    gain = column(gain2[...])
    hidden = tokens[...].astype(F32) + bs * nn(wo[...].T, mixed_t[...])
    r2 = inverse_rms(hidden)
    normed2_t = (hidden * r2 * gain).astype(BF16)
    normed2 = normed2_t.T
    seed = cotangent[...].astype(F32) * seed_scale[...]
    d_down_t = (bs * seed).astype(BF16)
    d_down = d_down_t.T
    ff = wg.shape[1]
    step = 512
    down[...] = jnp.zeros_like(down)
    d_normed2[...] = jnp.zeros_like(d_normed2)

    def chunk(f, carry):
        at = pl.ds(pl.multiple_of(f * step, step), step)
        gate = nn(normed2, wg[:, at])
        up = nn(normed2, wu[:, at])
        d_act = nn(d_down, wd[:, at])
        sig = 1.0 / (1.0 + jnp.exp(-gate))
        silu = gate * sig
        act = (silu * up).astype(BF16)
        d_gate = (d_act * up * (sig + silu * (1.0 - sig))).astype(BF16)
        d_up = (d_act * silu).astype(BF16)
        down_grad[:, at] = nn(d_down_t, act).astype(down_grad.dtype)
        gate_grad[:, at] = nn(normed2_t, d_gate).astype(gate_grad.dtype)
        up_grad[:, at] = nn(normed2_t, d_up).astype(up_grad.dtype)
        down[...] += nt(wd[:, at], act)
        d_normed2[...] += nt(wg[:, at], d_gate) + nt(wu[:, at], d_up)
        return carry

    lax.fori_loop(0, ff // step, chunk, 0)
    layer_out[...] = (hidden + bs * down[...]).astype(BF16)
    dn = d_normed2[...]
    gain2_grad[...] = jnp.sum(dn * hidden * r2, axis=1, keepdims=True)
    gained = gain * dn
    dh = seed + r2 * gained - hidden * (r2 * r2 * r2) * jnp.mean(gained * hidden, axis=0, keepdims=True)
    d_hidden[...] = dh
    d_branch = (bs * dh).astype(BF16)
    output_grad[...] = nt(mixed_t[...], d_branch).astype(output_grad.dtype)
    d_mixed = nn(wo[...], d_branch).astype(BF16)
    rows = d_mixed.shape[1]
    for h in range(H):
        g, r = h // GROUP, h % GROUP
        head = d_mixed[h * HD : (h + 1) * HD]
        d_out[g, r, :HD, :] = jnp.zeros((HD, rows), BF16)
        d_out[g, r, HD:, :] = head
        delta[g, r] = jnp.sum(head.astype(F32) * attended[g, r], axis=0, keepdims=True)


def grad_unit(g, queries, d_out, lse, delta, packed, dq, masked):
    rows = queries.shape[-1]
    natural = packed.T
    before = [dq[g, r] for r in range(GROUP)]

    def products(r):
        return nn(natural, queries[g, r]), nn(natural, d_out[g, r])

    ahead = products(0)
    done = []
    d_keys, d_vals = None, None
    for r in range(GROUP):
        scores, d_probs = ahead
        if r + 1 < GROUP:
            ahead = products(r + 1)
        probs = jnp.exp2(scores - lse[g, r])
        if masked:
            key_at = lax.broadcasted_iota(jnp.int32, scores.shape, 0)
            query_at = lax.broadcasted_iota(jnp.int32, scores.shape, 1)
            probs = jnp.where(key_at <= query_at, probs, 0.0)
        d_scores = (probs * (d_probs - delta[g, r])).astype(BF16)
        keys_term = nt(queries[g, r, :HD], d_scores)
        vals_term = nt(d_out[g, r, HD:], probs.astype(BF16))
        d_keys = keys_term if d_keys is None else d_keys + keys_term
        d_vals = vals_term if d_vals is None else d_vals + vals_term
        done.append(before[r] + nn(packed[:HD], d_scores))
    for r in range(GROUP):
        dq[g, r] = done[r]
    return d_keys * LN2, d_vals


def backward_kernel(queries, kv_all, d_out, lse, delta, dq, d_kv):
    me = lax.axis_index("blk")
    dq[...] = jnp.zeros_like(dq)
    d_kv[...] = jnp.zeros_like(d_kv)

    def run(j, masked):
        def one(g, carry):
            d_keys, d_vals = grad_unit(
                g, queries, d_out, lse, delta, kv_all[j, g], dq, masked
            )
            d_kv[j, g, :HD] = d_keys.astype(BF16)
            d_kv[j, g, HD:] = d_vals.astype(BF16)
            return carry

        lax.fori_loop(0, KVH, one, 0)

    def step(j, carry):
        run(j, False)
        return carry

    lax.fori_loop(0, me, step, 0)
    run(me, True)


def finish(
    tokens, gain, wq, wk, wv, cos, sin, dq, d_kv, d_hidden,
    input_grad, query_grad, key_grad, value_grad, gain_grad, turned,
):
    x = tokens[...].astype(F32)
    r1 = inverse_rms(x)
    weight = column(gain[...])
    normed = (x * r1 * weight).astype(BF16)
    c, s = cos[...], -sin[...]
    nq, nk = H * HD, KVH * HD
    for h in range(H):
        rows = dq[h // GROUP, h % GROUP] * HD**-0.5
        turned[h * HD : (h + 1) * HD, :] = turn(rows, c, s).astype(BF16)
    for g in range(KVH):
        turned[nq + g * HD : nq + (g + 1) * HD, :] = turn(d_kv[g, :HD], c, s).astype(BF16)
        turned[nq + nk + g * HD : nq + nk + (g + 1) * HD, :] = d_kv[g, HD:].astype(BF16)
    d_normed = (
        nn(wq[...], turned[:nq, :])
        + nn(wk[...].T, turned[nq : nq + nk, :])
        + nn(wv[...].T, turned[nq + nk :, :])
    )
    query_grad[...] = nt(normed, turned[:nq, :]).astype(query_grad.dtype)
    key_grad[...] = nt(turned[nq : nq + nk, :], normed).astype(key_grad.dtype)
    value_grad[...] = nt(turned[nq + nk :, :], normed).astype(value_grad.dtype)
    gain_grad[...] = jnp.sum(d_normed * x * r1, axis=1, keepdims=True)
    gained = weight * d_normed
    input_grad[...] = (
        d_hidden[...] + r1 * gained - x * (r1 * r1 * r1) * jnp.mean(gained * x, axis=0, keepdims=True)
    )


def call(kernel, outs, scratch=(), smem=(), **params):
    def run(*args):
        return pl.pallas_call(
            kernel,
            out_shape=[jax.ShapeDtypeStruct(s, t) for s, t in outs],
            in_specs=[
                pl.BlockSpec(memory_space=pltpu.SMEM if i in smem else pltpu.VMEM)
                for i in range(len(args))
            ],
            out_specs=[pl.BlockSpec(memory_space=pltpu.VMEM)] * len(outs),
            scratch_shapes=list(scratch),
            compiler_params=pltpu.CompilerParams(vmem_limit_bytes=VMEM_LIMIT, **params),
        )(*args)

    return run


def body(blocks, tokens, positions, groups, keep_mask, exit_scales, keep_rate, wq, wk, wv, wo, wg, wu, wd, gain1, gain2, cotangent):
    tokens, cotangent = tokens[0].T, cotangent[0].T
    wk, wv, wd = wk.T, wv.T, wd.T
    width, rows = tokens.shape
    ff = wg.shape[1]
    nq, nk = H * HD, KVH * HD
    frequency = 1.0 / ROPE_BASE ** (jnp.arange(HALF, dtype=F32) * (2.0 / HD))
    angle = frequency[:, None] * positions[0].astype(F32)[None, :]
    cos, sin = jnp.cos(angle), jnp.sin(angle)
    seed_scale = jnp.where(groups == 1, exit_scales[1], exit_scales[0])
    scale = (keep_mask.astype(F32) * keep_rate)[None, :]
    gain1, gain2 = gain1[None, :], gain2[None, :]

    head_t = (KVH, GROUP, PAIR, rows)
    head_o = (KVH, GROUP, HD, rows)
    head_1 = (KVH, GROUP, 1, rows)
    queries, kv_all, attended, mixed_t, lse = call(
        functools.partial(forward_kernel, blocks),
        [
            (head_t, BF16),
            ((blocks, KVH, PAIR, rows), BF16),
            (head_o, F32),
            ((nq, rows), BF16),
            (head_1, F32),
        ],
        [
            pltpu.VMEM(head_1, F32),
            pltpu.VMEM(head_1, F32),
            pltpu.SemaphoreType.DMA((2, blocks, KVH)),
            pltpu.SemaphoreType.DMA((blocks, KVH)),
        ],
        collective_id=0,
        has_side_effects=True,
    )(tokens, gain1, wq, wk, wv, cos, sin)
    (layer_out, d_hidden, gate_grad, up_grad, down_grad, output_grad, gain2_grad, d_out, delta) = call(
        feed_forward,
        [
            ((width, rows), BF16),
            ((width, rows), F32),
            ((width, ff), BF16),
            ((width, ff), BF16),
            ((width, ff), BF16),
            ((nq, width), BF16),
            ((width, 1), F32),
            (head_t, BF16),
            (head_1, F32),
        ],
        [pltpu.VMEM((width, rows), F32), pltpu.VMEM((width, rows), F32)],
        smem=(2,),
    )(tokens, seed_scale, scale, wo, wg, wu, wd, gain2, cotangent, mixed_t, attended)
    early = lax.psum((gate_grad, up_grad, down_grad, output_grad), ("seq", "blk"))
    dq, d_kv = call(
        backward_kernel,
        [(head_o, F32), ((blocks, KVH, PAIR, rows), BF16)],
    )(queries, kv_all, d_out, lse, delta)
    d_kv = lax.psum_scatter(d_kv, "blk", scatter_dimension=0, tiled=False).astype(F32)
    input_grad, query_grad, key_grad, value_grad, gain1_grad = call(
        finish,
        [
            ((width, rows), F32),
            ((width, nq), BF16),
            ((nk, width), BF16),
            ((nk, width), BF16),
            ((width, 1), F32),
        ],
        [pltpu.VMEM((nq + 2 * nk, rows), BF16)],
    )(tokens, gain1, wq, wk, wv, cos, sin, dq, d_kv, d_hidden)
    late = lax.psum((query_grad, key_grad, value_grad), ("seq", "blk"))
    gains = lax.psum(jnp.concatenate([gain1_grad, gain2_grad], axis=1), ("seq", "blk"))
    return (
        layer_out.T[None],
        input_grad.T[None],
        late[0].astype(F32),
        late[1].astype(F32).T,
        late[2].astype(F32).T,
        early[3].astype(F32),
        early[0].astype(F32),
        early[1].astype(F32),
        early[2].astype(F32).T,
        gains[:, 0],
        gains[:, 1],
    )


def solution(mesh):
    local = P("seq", "blk", None)
    pair = P("seq", "blk")
    placed = (local, pair, pair, P("seq")) + (P(),) * 11 + (local,)
    return jax.shard_map(
        functools.partial(body, mesh.shape["blk"]),
        mesh=mesh,
        in_specs=placed,
        out_specs=(local, local) + (P(),) * 9,
        check_vma=False,
    )
```

```python
import functools

import jax
import jax.numpy as jnp
from jax import lax
from jax.experimental import pallas as pl
from jax.experimental.pallas import tpu as pltpu
from jax.sharding import PartitionSpec as P

H = 9
KVH = 3
HD = 64
GROUP = H // KVH
HALF = HD // 2
PAIR = 2 * HD

EPSILON = 1e-05
ROPE_BASE = 100000.0
MASKED = -1e30
LOG2E = 1.4426950408889634
LN2 = 0.6931471805599453
F32 = jnp.float32
BF16 = jnp.bfloat16
VMEM_LIMIT = 61 * 1024 * 1024
MESH = pl.DeviceIdType.MESH
LANES = 128


def nn(a, b):
    return lax.dot_general(a, b, (((1,), (0,)), ((), ())), preferred_element_type=F32)


def nt(a, b):
    return lax.dot_general(a, b, (((1,), (1,)), ((), ())), preferred_element_type=F32)


def column(row):
    return jnp.broadcast_to(row, (8, row.shape[1])).T[:, :1]


def inverse_rms(values):
    return lax.rsqrt(jnp.mean(values * values, axis=0, keepdims=True) + EPSILON)


def turn(rows, cos, sin):
    u, w = rows[:HALF], rows[HALF:]
    return jnp.concatenate([u * cos - w * sin, w * cos + u * sin], axis=0)


def normalize(tokens, gain):
    x = tokens[...].astype(F32)
    return (x * inverse_rms(x) * column(gain[...])).astype(BF16)


def project_kv(normed, wk, wv, cos, sin, kv):
    keys = nn(wk[...], normed)
    vals = nn(wv[...], normed)
    for g in range(KVH):
        span = slice(g * HD, (g + 1) * HD)
        kv[g, :HD, :] = turn(keys[span], cos, sin).astype(BF16)
        kv[g, HD:, :] = vals[span].astype(BF16)


def project_q(normed, wq, cos, sin, queries):
    raw = nn(wq[...].T, normed)
    factor = HD**-0.5 * LOG2E
    for h in range(H):
        turned = turn(raw[h * HD : (h + 1) * HD], cos, sin) * factor
        queries[h // GROUP, h % GROUP, :HD, :] = turned.astype(BF16)
        queries[h // GROUP, h % GROUP, HD:, :] = jnp.zeros((HD, raw.shape[1]), BF16)


def values_and_ones(packed):
    ones = jnp.ones((16, packed.shape[1]), BF16)
    return jnp.concatenate([packed[HD:], ones], axis=0)


def first_unit(g, queries, packed, out, top, total):
    rows = queries.shape[-1]
    part = rows // 2
    natural = packed.T
    values = values_and_ones(packed)
    items = [(r, c) for r in range(GROUP) for c in range(2)]

    def scores_of(i):
        r, c = items[i]
        return nn(natural[: (c + 1) * part], queries[g, r, :, c * part : (c + 1) * part])

    scores = scores_of(0)
    done = []
    for i, (r, c) in enumerate(items):
        later = scores_of(i + 1) if i + 1 < len(items) else None
        key_at = lax.broadcasted_iota(jnp.int32, scores.shape, 0)
        query_at = lax.broadcasted_iota(jnp.int32, scores.shape, 1) + c * part
        scores = jnp.where(key_at <= query_at, scores, MASKED)
        high = jnp.max(scores, axis=0, keepdims=True)
        probs = jnp.exp2(scores - high)
        done.append((high, nn(values[:, : (c + 1) * part], probs.astype(BF16))))
        scores = later
    for (r, c), (high, summed) in zip(items, done):
        cols = slice(c * part, (c + 1) * part)
        top[g, r, :, cols] = high
        total[g, r, :, cols] = summed[HD : HD + 1]
        out[g, r, :, cols] = summed[:HD]


def next_unit(g, queries, packed, out, top, total):
    natural = packed.T
    values = values_and_ones(packed)
    before = [(top[g, r], total[g, r], out[g, r]) for r in range(GROUP)]
    scores = [nn(natural, queries[g, r]) for r in range(2)]
    done = []
    for r in range(GROUP):
        if r + 2 < GROUP:
            scores.append(nn(natural, queries[g, r + 2]))
        old, count, acc = before[r]
        high = jnp.maximum(old, jnp.max(scores[r], axis=0, keepdims=True))
        probs = jnp.exp2(scores[r] - high)
        fade = jnp.exp2(old - high)
        summed = nn(values, probs.astype(BF16))
        done.append((high, count * fade + summed[HD : HD + 1], acc * fade + summed[:HD]))
    for r, (high, count, acc) in enumerate(done):
        top[g, r] = high
        total[g, r] = count
        out[g, r] = acc


def finish_forward(out, top, total, mixed_t, lse):
    for h in range(H):
        g, r = h // GROUP, h % GROUP
        scaled = out[g, r] * (1.0 / total[g, r])
        out[g, r] = scaled
        mixed_t[h * HD : (h + 1) * HD, :] = scaled.astype(BF16)
        lse[g, r] = top[g, r] + jnp.log2(total[g, r])


def grad_unit(g, queries, d_out, lse, delta, packed, dq, masked):
    rows = queries.shape[-1]
    natural = packed.T

    def d_head(r, first=0):
        start = pl.multiple_of((g * GROUP + r) * PAIR + first, HD)
        return d_out[pl.ds(start, PAIR - first)]

    before = [dq[g, r] for r in range(GROUP)]

    def products(r):
        return nn(natural, queries[g, r]), nn(natural, d_head(r))

    ahead = products(0)
    done = []
    d_keys, d_vals = None, None
    for r in range(GROUP):
        scores, d_probs = ahead
        if r + 1 < GROUP:
            ahead = products(r + 1)
        probs = jnp.exp2(scores - lse[g, r])
        if masked:
            key_at = lax.broadcasted_iota(jnp.int32, scores.shape, 0)
            query_at = lax.broadcasted_iota(jnp.int32, scores.shape, 1)
            probs = jnp.where(key_at <= query_at, probs, 0.0)
        d_scores = (probs * (d_probs - delta[g, r])).astype(BF16)
        keys_term = nt(queries[g, r, :HD], d_scores)
        vals_term = nt(d_head(r, HD), probs.astype(BF16))
        d_keys = keys_term if d_keys is None else d_keys + keys_term
        d_vals = vals_term if d_vals is None else d_vals + vals_term
        done.append(before[r] + nn(packed[:HD], d_scores))
    for r in range(GROUP):
        dq[g, r] = done[r]
    return d_keys * LN2, d_vals


def log2(n):
    return n.bit_length() - 1


class Cube:
    def __init__(self, s, b, sizes, send_sem, recv_sem, credit):
        seqs, blocks = sizes
        self.send_sem, self.recv_sem, self.credit = send_sem, recv_sem, credit
        self.partners, self.bits = [], []
        for bit in range(log2(seqs)):
            mine = (s // 2**bit) % 2
            self.bits.append(mine)
            self.partners.append((s + 2**bit * (1 - 2 * mine), b))
        for bit in range(log2(blocks)):
            mine = (b // 2**bit) % 2
            self.bits.append(mine)
            self.partners.append((s, b + 2**bit * (1 - 2 * mine)))
        self.depth = len(self.bits)

    def span(self, rows, d):
        lo, size = 0, rows
        for e in range(1, d + 1):
            size = size // 2
            lo = lo + self.bits[e] * size
        return lo, size

    def remote(self, src, dst, sem, d):
        i, k = sem
        return pltpu.make_async_remote_copy(
            src_ref=src,
            dst_ref=dst,
            send_sem=self.send_sem.at[i, k],
            recv_sem=self.recv_sem.at[i, k],
            device_id=self.partners[d],
            device_id_type=MESH,
        )

    def scatter(self, part, landing, i, d):
        mine = self.bits[0]
        if d == 0:
            src = part.at[1 - mine]
        else:
            before, _ = self.span(part.shape[1], d - 1)
            _, size = self.span(part.shape[1], d)
            start = pl.multiple_of(before + (1 - self.bits[d]) * size, 16)
            src = part.at[mine, pl.ds(start, size)]
        return self.remote(src, landing[d], (i, d), d)

    def gather(self, part, i, d):
        lo, size = self.span(part.shape[1], d)
        ref = part.at[self.bits[0], pl.ds(pl.multiple_of(lo, 16), size)]
        return self.remote(ref, ref, (i, self.depth + d), d)

    def add(self, part, landing, d):
        lo, size = self.span(part.shape[1], d)
        rows = pl.ds(pl.multiple_of(lo, 16), size)
        mine = self.bits[0]
        part[mine, rows] = (part[mine, rows].astype(F32) + landing[d][...].astype(F32)).astype(BF16)

    def step(self, part, landing, i, k):
        n = self.depth
        if k < n:
            sent = self.scatter(part, landing, i, k)
            sent.wait_send()
            pl.semaphore_signal(
                self.credit.at[i, k], inc=1, device_id=self.partners[k], device_id_type=MESH
            )
            sent.wait_recv()
            self.add(part, landing, k)
            if k + 1 < n:
                self.scatter(part, landing, i, k + 1).start()
            else:
                self.send_back(part, i, n - 1)
        else:
            d = 2 * n - 1 - k
            self.gather(part, i, d).wait_recv()
            if d > 0:
                self.send_back(part, i, d - 1)

    def send_back(self, part, i, d):
        pl.semaphore_wait(self.credit.at[i, d], 1)
        self.gather(part, i, d).start()

    def drain(self, part, i):
        for d in range(self.depth):
            self.gather(part, i, d).wait_send()


def padded_rows(rows, depth):
    unit = 16 * 2 ** (depth - 1)
    return (rows + unit - 1) // unit * unit


def mega_kernel(
    sizes,
    keep_mask, keep_rate, exit_scales,
    tokens, groups, gain1, gain2, wk, wv, wq, cos, sin,
    wo_hbm, wg_hbm, wu_hbm, wd_hbm, cot_hbm,
    layer_out, input_grad, parts, tail,
    wo, stream, cotangent,
    queries, kv_all, attended, mixed_t, top, total,
    d_normed2, d_out,
    chain, cross,
    load_sem, stream_sem, send_sem, recv_sem, cube_send, cube_recv, credit, kv_send, chain_recv, cross_recv,
    *landings,
):
    seqs, blocks = sizes
    s, b = lax.axis_index("seq"), lax.axis_index("blk")
    z, y, floors = b // 2, b % 2, blocks // 2
    above, below, across = (s, b + 2), (s, b - 2), (s, b + 1 - 2 * y)
    has_above, has_below = z < floors - 1, z > 0
    cube = Cube(s, b, sizes, cube_send, cube_recv, credit)
    depth = cube.depth
    count = parts.shape[0]
    main_landing, tail_landing = landings[:depth], landings[depth:]

    loads = [
        pltpu.make_async_copy(src, dst, load_sem.at[i])
        for i, (src, dst) in enumerate(
            [(wo_hbm, wo), (cot_hbm, cotangent)]
        )
    ]
    step = 2 * LANES
    chunks = wg_hbm.shape[1] // step

    def weights(f):
        at = pl.ds(pl.multiple_of(f * step, step), step)
        return [
            pltpu.make_async_copy(ref.at[:, at], stream.at[f % 2, k], stream_sem.at[f % 2, k])
            for k, ref in enumerate((wg_hbm, wu_hbm, wd_hbm))
        ]

    for load in loads + weights(0):
        load.start()

    barrier = pltpu.get_barrier_semaphore()

    def greet(device):
        pl.semaphore_signal(barrier, inc=1, device_id=device, device_id_type=MESH)

    for device in cube.partners:
        greet(device)
    odd = z % 2
    extra_below = has_below & (odd == 0)
    extra_above = has_above & (odd == 1)

    @pl.when(extra_below)
    def _():
        greet(below)

    @pl.when(extra_above)
    def _():
        greet(above)

    extra = extra_below.astype(jnp.int32) + extra_above.astype(jnp.int32)

    def copy(kind, j, g):
        return pltpu.make_async_remote_copy(
            src_ref=kv_all.at[j, g],
            dst_ref=kv_all.at[j, g],
            send_sem=send_sem.at[kind, j, g],
            recv_sem=recv_sem.at[j, g],
            device_id=above if kind == 0 else across,
            device_id_type=MESH,
        )

    normed = normalize(tokens, gain1)
    c, sn = cos[...], sin[...]
    project_kv(normed, wk, wv, c, sn, kv_all.at[b])
    pl.semaphore_wait(barrier, depth + extra)

    def send_own(g, carry):
        @pl.when(has_above)
        def _():
            copy(0, b, g).start()

        @pl.when(y == 0)
        def _():
            copy(1, b, g).start()

        return carry

    lax.fori_loop(0, KVH, send_own, 0)
    project_q(normed, wq, c, sn, queries)

    def own(g, carry):
        first_unit(g, queries, kv_all[b, g], attended, top, total)
        return carry

    lax.fori_loop(0, KVH, own, 0)

    def level(m, carry):
        def one(g, inner):
            @pl.when(m <= z)
            def _():
                j = b - 2 * m
                copy(0, j, g).wait_recv()

                @pl.when(has_above)
                def _():
                    copy(0, j, g).start()

                copy(1, j, g).start()
                next_unit(g, queries, kv_all[j, g], attended, top, total)

            @pl.when((m >= 2) | (y == 1))
            def _():
                j = b - 2 * m + 3 - 2 * y
                copy(1, j, g).wait_recv()
                next_unit(g, queries, kv_all[j, g], attended, top, total)

            return inner

        return lax.fori_loop(0, KVH, one, carry)

    lax.fori_loop(1, z + 2, level, 0)
    lse = top
    finish_forward(attended, top, total, mixed_t, lse)

    def drain_forward(m, carry):
        def one(g, inner):
            j = b - 2 * m

            @pl.when(has_above)
            def _():
                copy(0, j, g).wait_send()

            @pl.when((m >= 1) | (y == 0))
            def _():
                copy(1, j, g).wait_send()

            return inner

        return lax.fori_loop(0, KVH, one, carry)

    lax.fori_loop(0, z + 1, drain_forward, 0)

    lead = count + 1
    start, stride = [1 - lead], [1]
    for d in range(1, depth):
        start.append(2 * d - 7)
        stride.append(2)
    for d in range(depth - 1, 1, -1):
        start.append(start[-1] + 2)
        stride.append(2)
    start += [start[-1] + 3, start[-1] + 4]
    stride += [2, 2]
    slots = max(KVH * blocks + 2 * floors + 2, start[-1] + 2 * count)
    shift = 2 * lead + 2 * depth

    def serve(n):
        for k in range(2 * depth - 1, -1, -1):
            at = n - start[k] + 2 * shift
            i = at // stride[k] - 2 * shift // stride[k]
            due = (at % stride[k] == 0) & (i >= 0) & (i < count)

            @pl.when(due)
            def _(i=i, k=k):
                cube.step(parts.at[i], [r.at[i] for r in main_landing], i, k)

    for load in loads:
        load.wait()
    bs = keep_mask[0].astype(F32) * keep_rate[0]
    gain = column(gain2[...])
    hidden = tokens[...].astype(F32) + bs * nn(wo[...].T, mixed_t[...])
    r2 = inverse_rms(hidden)
    normed2_t = (hidden * r2 * gain).astype(BF16)
    normed2 = normed2_t.T

    def seed():
        by_group = jnp.where(groups[...] == 1, exit_scales[1], exit_scales[0])
        return cotangent[...].astype(F32) * by_group

    d_down_t = (bs * seed()).astype(BF16)
    d_down = d_down_t.T
    width, rows = hidden.shape
    for i in range(count):
        filled = 3 * width if i < chunks else 5 * width // 2
        for half in range(2):
            parts[i, half, filled:] = jnp.zeros((parts.shape[2] - filled, LANES), BF16)
    down = d_hidden = input_grad
    down[...] = jnp.zeros_like(down)
    d_normed2[...] = jnp.zeros_like(d_normed2)

    def chunk(f, carry):
        for load in weights(f):
            load.wait()

        @pl.when(f + 1 < chunks)
        def _():
            for load in weights(f + 1):
                load.start()

        wg, wu, wd = (stream.at[f % 2, k] for k in range(3))
        gate = nn(normed2, wg[...])
        up = nn(normed2, wu[...])
        d_act = nn(d_down, wd[...])
        sig = 1.0 / (1.0 + jnp.exp(-gate))
        silu = gate * sig
        act = (silu * up).astype(BF16)
        d_gate = (d_act * up * (sig + silu * (1.0 - sig))).astype(BF16)
        d_up = (d_act * silu).astype(BF16)
        grads = (nn(normed2_t, d_gate), nn(normed2_t, d_up), nn(d_down_t, act))
        for k, value in enumerate(grads):
            for half in range(2):
                parts[f, half, k * width : (k + 1) * width] = value[
                    :, half * LANES : (half + 1) * LANES
                ].astype(BF16)
        down[...] += nt(wd[...], act)
        d_normed2[...] += nt(wg[...], d_gate) + nt(wu[...], d_up)
        cube.scatter(parts.at[f], [r.at[f] for r in main_landing], f, 0).start()
        serve(f - lead)
        return carry

    lax.fori_loop(0, chunks, chunk, 0)
    layer_out[...] = (hidden + bs * down[...]).astype(BF16)
    dn = d_normed2[...]
    gain2_grad = jnp.sum(dn * hidden * r2, axis=1, keepdims=True)
    gained = gain * dn
    dh = seed() + r2 * gained - hidden * (r2 * r2 * r2) * jnp.mean(gained * hidden, axis=0, keepdims=True)
    d_hidden[...] = dh
    d_branch = (bs * dh).astype(BF16)
    out_grad = nt(mixed_t[...], d_branch)
    half_rows = width // 2
    last = parts.at[chunks]
    last[0, :width] = out_grad[:, :LANES].astype(BF16)
    last[0, width : 2 * width] = out_grad[:, LANES : 2 * LANES].astype(BF16)
    middle = out_grad[:, 2 * LANES : 3 * LANES].astype(BF16)
    last[0, 2 * width : 2 * width + half_rows] = middle[:half_rows]
    last[1, :half_rows] = middle[half_rows:]
    last[1, half_rows : half_rows + width] = out_grad[:, 3 * LANES : 4 * LANES].astype(BF16)
    last[1, half_rows + width : half_rows + 2 * width] = with_gain(out_grad, gain2_grad)
    cube.scatter(last, [r.at[chunks] for r in main_landing], chunks, 0).start()
    serve(-2)
    d_mixed = nn(wo[...], d_branch).astype(BF16)
    delta = total
    for h in range(H):
        g, r = h // GROUP, h % GROUP
        head = d_mixed[h * HD : (h + 1) * HD]
        d_out[h * PAIR : h * PAIR + HD] = jnp.zeros((HD, rows), BF16)
        d_out[h * PAIR + HD : (h + 1) * PAIR] = head
        delta[g, r] = jnp.sum(head.astype(F32) * attended[g, r], axis=0, keepdims=True)
    dq = attended
    dq[...] = jnp.zeros_like(dq)
    serve(-1)

    def kv_down(j, g):
        return pltpu.make_async_remote_copy(
            src_ref=kv_all.at[j, g],
            dst_ref=chain.at[j // 2, g],
            send_sem=kv_send.at[j, g],
            recv_sem=chain_recv.at[j // 2, g],
            device_id=below,
            device_id_type=MESH,
        )

    def kv_across(j, g):
        return pltpu.make_async_remote_copy(
            src_ref=kv_all.at[j, g],
            dst_ref=cross.at[j // 2, g],
            send_sem=kv_send.at[j, g],
            recv_sem=cross_recv.at[j // 2, g],
            device_id=across,
            device_id_type=MESH,
        )

    d_kv = d_normed2
    lag = 2 + 2 * (floors - 1 - z)

    def slot(n, carry):
        j, g = n // KVH, n % KVH

        def unit(masked):
            d_keys, d_vals = grad_unit(g, queries, d_out, lse, delta, kv_all[j, g], dq, masked)
            kv_all[j, g, :HD] = d_keys.astype(BF16)
            kv_all[j, g, HD:] = d_vals.astype(BF16)

        @pl.when(j < b)
        def _():
            unit(False)

        @pl.when(j == b)
        def _():
            unit(True)

        @pl.when((j <= b) & (j % 2 != y))
        def _():
            kv_across(j, g).start()

        ready = n - lag + KVH * blocks
        jj, gg = ready // KVH - blocks, ready % KVH

        @pl.when((n >= lag) & (jj <= b) & (jj % 2 == y))
        def _():
            at = pl.ds(pl.multiple_of(gg * PAIR, PAIR), PAIR)
            mine = kv_all[jj, gg].astype(F32)
            d_kv[at] = mine

            @pl.when((jj < b) | (y == 0))
            def _():
                kv_across(jj, gg).wait_recv()
                d_kv[at] = d_kv[at] + cross[jj // 2, gg].astype(F32)

            @pl.when(has_above)
            def _():
                kv_down(jj, gg).wait_recv()
                d_kv[at] = d_kv[at] + chain[jj // 2, gg].astype(F32)

            @pl.when(jj < b)
            def _():
                kv_all[jj, gg] = d_kv[at].astype(BF16)
                kv_down(jj, gg).start()

        serve(n)
        return carry

    lax.fori_loop(0, slots, slot, 0)

    def drain_backward(n, carry):
        j, g = n // KVH, n % KVH

        @pl.when(j % 2 != y)
        def _():
            kv_across(j, g).wait_send()

        @pl.when((j % 2 == y) & (j < b))
        def _():
            kv_down(j, g).wait_send()

        return carry

    lax.fori_loop(0, KVH * (b + 1), drain_backward, 0)

    x = tokens[...].astype(F32)
    r1 = inverse_rms(x)
    weight = column(gain1[...])
    normed = (x * r1 * weight).astype(BF16)
    c, sn = cos[...], -sin[...]
    nq, nk = H * HD, KVH * HD
    turned = d_out
    for h in range(H):
        piece = dq[h // GROUP, h % GROUP] * HD**-0.5
        turned[h * HD : (h + 1) * HD, :] = turn(piece, c, sn).astype(BF16)
    for g in range(KVH):
        turned[nq + g * HD : nq + (g + 1) * HD, :] = turn(d_kv[g * PAIR : g * PAIR + HD], c, sn).astype(BF16)
        turned[nq + nk + g * HD : nq + nk + (g + 1) * HD, :] = d_kv[g * PAIR + HD : (g + 1) * PAIR].astype(BF16)
    d_normed = (
        nn(wq[...], turned[:nq, :])
        + nn(wk[...].T, turned[nq : nq + nk, :])
        + nn(wv[...].T, turned[nq + nk : nq + 2 * nk, :])
    )
    query_grad = nt(normed, turned[:nq, :])
    kv_grad = nt(turned[nq : nq + 2 * nk, :], normed)
    gain1_grad = jnp.sum(d_normed * x * r1, axis=1, keepdims=True)
    for i in range(4):
        tail[0, i * width : (i + 1) * width] = query_grad[:, i * LANES : (i + 1) * LANES].astype(BF16)
    tail[0, 4 * width :] = jnp.zeros((tail.shape[1] - 4 * width, LANES), BF16)
    tail[1, :width] = with_gain(query_grad, gain1_grad)
    for i in range(5):
        first = width + i * 2 * nk
        left = kv_grad[:, i * LANES : (i + 1) * LANES].astype(BF16)
        if left.shape[1] < LANES:
            left = jnp.concatenate([left, jnp.zeros_like(left)], axis=1)
        tail[1, first : first + 2 * nk] = left
    filled = width + 10 * nk
    tail[1, filled:] = jnp.zeros((tail.shape[1] - filled, LANES), BF16)
    cube.scatter(tail, tail_landing, count, 0).start()
    gained = weight * d_normed
    input_grad[...] = (
        d_hidden[...] + r1 * gained - x * (r1 * r1 * r1) * jnp.mean(gained * x, axis=0, keepdims=True)
    )
    for k in range(2 * depth):
        cube.step(tail, tail_landing, count, k)
    for i in range(count):
        cube.drain(parts.at[i], i)
    cube.drain(tail, count)


def unpack_kernel(
    chunks, parts, tail, gate, up, down, output, query, key, value, gain1, gain2
):
    i = pl.program_id(0)
    width = gate.shape[0]

    @pl.when(i < chunks)
    def _():
        for k, out in enumerate((gate, up, down)):
            for half in range(2):
                piece = parts[0, half, k * width : (k + 1) * width]
                out[:, half * LANES : (half + 1) * LANES] = piece.astype(F32)

    @pl.when(i == chunks)
    def _():
        half = width // 2
        output[:, :LANES] = parts[0, 0, :width].astype(F32)
        output[:, LANES : 2 * LANES] = parts[0, 0, width : 2 * width].astype(F32)
        output[:half, 2 * LANES : 3 * LANES] = parts[0, 0, 2 * width : 2 * width + half].astype(F32)
        output[half:, 2 * LANES : 3 * LANES] = parts[0, 1, :half].astype(F32)
        output[:, 3 * LANES : 4 * LANES] = parts[0, 1, half : half + width].astype(F32)
        end = parts[0, 1, half + width : half + 2 * width].astype(F32)
        output[:, 4 * LANES :] = end[:, :HD]
        gain2[...] = end.T[HD : HD + 1]
        for k in range(4):
            query[:, k * LANES : (k + 1) * LANES] = tail[0, k * width : (k + 1) * width].astype(F32)
        end = tail[1, :width].astype(F32)
        query[:, 4 * LANES :] = end[:, :HD]
        gain1[...] = end.T[HD : HD + 1]
        nk = key.shape[0]
        for k in range(5):
            size = min(LANES, width - k * LANES)
            lanes = slice(k * LANES, k * LANES + size)
            first = width + 2 * k * nk
            key[:, lanes] = tail[1, first : first + nk].astype(F32)[:, :size]
            value[:, lanes] = tail[1, first + nk : first + 2 * nk].astype(F32)[:, :size]


def with_gain(grad, gain):
    rows = grad.shape[0]
    return jnp.concatenate(
        [grad[:, 4 * LANES :], gain, jnp.zeros((rows, LANES - HD - 1), F32)], axis=1
    ).astype(BF16)


def body(sizes, tokens, positions, groups, keep_mask, exit_scales, keep_rate, wq, wk, wv, wo, wg, wu, wd, gain1, gain2, cotangent):
    seqs, blocks = sizes
    depth = log2(seqs) + log2(blocks)
    tokens, cotangent = tokens[0].T, cotangent[0].T
    wk, wv, wd = wk.T, wv.T, wd.T
    width, rows = tokens.shape
    ff = wg.shape[1]
    nq, nk = H * HD, KVH * HD
    frequency = 1.0 / ROPE_BASE ** (jnp.arange(HALF, dtype=F32) * (2.0 / HD))
    angle = frequency[:, None] * positions[0].astype(F32)[None, :]
    cos, sin = jnp.cos(angle), jnp.sin(angle)

    chunks = ff // (2 * LANES)
    count = chunks + 1
    part_rows = padded_rows(3 * width, depth)
    tail_rows = padded_rows(max(4 * width, width + 10 * nk), depth)
    vmem, smem, hbm = (pl.BlockSpec(memory_space=m) for m in (pltpu.VMEM, pltpu.SMEM, pl.ANY))
    head_t = (KVH, GROUP, PAIR, rows)
    head_o = (KVH, GROUP, HD, rows)
    head_1 = (KVH, GROUP, 1, rows)
    dma = pltpu.SemaphoreType.DMA
    scratch = [
        pltpu.VMEM(wo.shape, BF16),
        pltpu.VMEM((2, 3, width, 2 * LANES), BF16),
        pltpu.VMEM(cotangent.shape, BF16),
        pltpu.VMEM(head_t, BF16),
        pltpu.VMEM((blocks, KVH, PAIR, rows), BF16),
        pltpu.VMEM(head_o, F32),
        pltpu.VMEM((nq, rows), BF16),
        pltpu.VMEM(head_1, F32),
        pltpu.VMEM(head_1, F32),
        pltpu.VMEM((width, rows), F32),
        pltpu.VMEM((H * PAIR, rows), BF16),
        pltpu.VMEM((blocks // 2, KVH, PAIR, rows), BF16),
        pltpu.VMEM((blocks // 2, KVH, PAIR, rows), BF16),
        dma((2,)),
        dma((2, 3)),
        dma((2, blocks, KVH)),
        dma((blocks, KVH)),
        dma((count + 1, 2 * depth)),
        dma((count + 1, 2 * depth)),
        pltpu.SemaphoreType.REGULAR((count + 1, depth)),
        dma((blocks, KVH)),
        dma((blocks // 2, KVH)),
        dma((blocks // 2, KVH)),
    ]
    scratch += [pltpu.VMEM((count, part_rows >> d, LANES), BF16) for d in range(depth)]
    scratch += [pltpu.VMEM((tail_rows >> d, LANES), BF16) for d in range(depth)]
    layer_out, input_grad, parts, tail = pl.pallas_call(
        functools.partial(mega_kernel, sizes),
        out_shape=[
            jax.ShapeDtypeStruct((width, rows), BF16),
            jax.ShapeDtypeStruct((width, rows), F32),
            jax.ShapeDtypeStruct((count, 2, part_rows, LANES), BF16),
            jax.ShapeDtypeStruct((2, tail_rows, LANES), BF16),
        ],
        in_specs=[smem] * 3 + [vmem] * 9 + [hbm] * 5,
        out_specs=[vmem] * 4,
        scratch_shapes=scratch,
        compiler_params=pltpu.CompilerParams(
            vmem_limit_bytes=VMEM_LIMIT, collective_id=0, has_side_effects=True
        ),
    )(
        keep_mask, keep_rate, exit_scales,
        tokens, groups, gain1[None, :], gain2[None, :], wk, wv, wq, cos, sin,
        wo, wg, wu, wd, cotangent,
    )

    wide = pl.BlockSpec((width, 2 * LANES), lambda i: (0, jnp.minimum(i, chunks - 1)))
    small = [(nq, width), (width, nq), (nk, width), (nk, width), (1, width), (1, width)]
    gate_grad, up_grad, down_grad, output_grad, query_grad, key_grad, value_grad, gain1_grad, gain2_grad = pl.pallas_call(
        functools.partial(unpack_kernel, chunks),
        grid=(count,),
        out_shape=[jax.ShapeDtypeStruct((width, ff), F32)] * 3
        + [jax.ShapeDtypeStruct(shape, F32) for shape in small],
        in_specs=[
            pl.BlockSpec((1, 2, part_rows, LANES), lambda i: (i, 0, 0, 0)),
            pl.BlockSpec(tail.shape, lambda i: (0, 0, 0)),
        ],
        out_specs=[wide] * 3 + [pl.BlockSpec(shape, lambda i: (0, 0)) for shape in small],
        compiler_params=pltpu.CompilerParams(vmem_limit_bytes=VMEM_LIMIT),
    )(parts, tail)
    return (
        layer_out.T[None],
        input_grad.T[None],
        query_grad,
        key_grad.T,
        value_grad.T,
        output_grad,
        gate_grad,
        up_grad,
        down_grad.T,
        gain1_grad[0],
        gain2_grad[0],
    )


def solution(mesh):
    local = P("seq", "blk", None)
    pair = P("seq", "blk")
    placed = (local, pair, pair, P("seq")) + (P(),) * 11 + (local,)
    return jax.shard_map(
        functools.partial(body, (mesh.shape["seq"], mesh.shape["blk"])),
        mesh=mesh,
        in_specs=placed,
        out_specs=(local, local) + (P(),) * 9,
        check_vma=False,
    )
```

```python
import functools

import jax
import jax.numpy as jnp
from jax import lax
from jax.experimental import pallas as pl
from jax.experimental.pallas import tpu as pltpu
from jax.sharding import PartitionSpec as P

H = 9
KVH = 3
HD = 64
GROUP = H // KVH
HALF = HD // 2
PAIR = 2 * HD

EPSILON = 1e-05
ROPE_BASE = 100000.0
MASKED = -1e30
LOG2E = 1.4426950408889634
LN2 = 0.6931471805599453
F32 = jnp.float32
BF16 = jnp.bfloat16
VMEM_LIMIT = 61 * 1024 * 1024
MESH = pl.DeviceIdType.MESH
LANES = 128


def nn(a, b):
    return lax.dot_general(a, b, (((1,), (0,)), ((), ())), preferred_element_type=F32)


def nt(a, b):
    return lax.dot_general(a, b, (((1,), (1,)), ((), ())), preferred_element_type=F32)


def column(values):
    return jnp.broadcast_to(values[None, :], (8, values.shape[0])).T[:, :1]


def as_row(values):
    return jnp.broadcast_to(values, (values.shape[0], 8)).T[:1]


def inverse_rms(values):
    return lax.rsqrt(jnp.mean(values * values, axis=0, keepdims=True) + EPSILON)


def turn(rows, cos, sin):
    u, w = rows[:HALF], rows[HALF:]
    return jnp.concatenate([u * cos - w * sin, w * cos + u * sin], axis=0)


def normalize(tokens, gain):
    x = tokens[...].astype(F32)
    return (x * inverse_rms(x) * column(gain[...])).astype(BF16)


def project_kv(normed, wk, wv, cos, sin, kv):
    keys = nn(wk[...], normed)
    vals = nn(wv[...], normed)
    for g in range(KVH):
        span = slice(g * HD, (g + 1) * HD)
        kv[g, :HD, :] = turn(keys[span], cos, sin).astype(BF16)
        kv[g, HD:, :] = vals[span].astype(BF16)


def project_q(normed, wq, cos, sin, queries):
    raw = nn(wq[...].T, normed)
    factor = HD**-0.5 * LOG2E
    for h in range(H):
        turned = turn(raw[h * HD : (h + 1) * HD], cos, sin) * factor
        queries[h // GROUP, h % GROUP, :HD, :] = turned.astype(BF16)
        queries[h // GROUP, h % GROUP, HD:, :] = jnp.zeros((HD, raw.shape[1]), BF16)


def values_and_ones(packed):
    ones = jnp.ones((16, packed.shape[1]), BF16)
    return jnp.concatenate([packed[HD:], ones], axis=0)


def first_unit(g, queries, packed, out, top, total):
    rows = queries.shape[-1]
    part = rows // 2
    natural = packed.T
    values = values_and_ones(packed)
    items = [(r, c) for r in range(GROUP) for c in range(2)]

    def scores_of(i):
        r, c = items[i]
        return nn(natural[: (c + 1) * part], queries[g, r, :, c * part : (c + 1) * part])

    scores = scores_of(0)
    done = []
    for i, (r, c) in enumerate(items):
        later = scores_of(i + 1) if i + 1 < len(items) else None
        key_at = lax.broadcasted_iota(jnp.int32, scores.shape, 0)
        query_at = lax.broadcasted_iota(jnp.int32, scores.shape, 1) + c * part
        scores = jnp.where(key_at <= query_at, scores, MASKED)
        high = jnp.max(scores, axis=0, keepdims=True)
        probs = jnp.exp2(scores - high)
        done.append((high, nn(values[:, : (c + 1) * part], probs.astype(BF16))))
        scores = later
    for (r, c), (high, summed) in zip(items, done):
        cols = slice(c * part, (c + 1) * part)
        top[g, r, :, cols] = high
        total[g, r, :, cols] = summed[HD : HD + 1]
        out[g, r, :, cols] = summed[:HD]


def next_unit(g, queries, packed, out, top, total):
    natural = packed.T
    values = values_and_ones(packed)
    before = [(top[g, r], total[g, r], out[g, r]) for r in range(GROUP)]
    scores = [nn(natural, queries[g, r]) for r in range(2)]
    done = []
    for r in range(GROUP):
        if r + 2 < GROUP:
            scores.append(nn(natural, queries[g, r + 2]))
        old, count, acc = before[r]
        high = jnp.maximum(old, jnp.max(scores[r], axis=0, keepdims=True))
        probs = jnp.exp2(scores[r] - high)
        fade = jnp.exp2(old - high)
        summed = nn(values, probs.astype(BF16))
        done.append((high, count * fade + summed[HD : HD + 1], acc * fade + summed[:HD]))
    for r, (high, count, acc) in enumerate(done):
        top[g, r] = high
        total[g, r] = count
        out[g, r] = acc


def finish_forward(out, top, total, mixed_t, lse):
    for h in range(H):
        g, r = h // GROUP, h % GROUP
        scaled = out[g, r] * (1.0 / total[g, r])
        out[g, r] = scaled
        mixed_t[h * HD : (h + 1) * HD, :] = scaled.astype(BF16)
        lse[g, r] = top[g, r] + jnp.log2(total[g, r])


def grad_unit(g, queries, d_out, lse, delta, packed, dq, masked):
    rows = queries.shape[-1]
    natural = packed.T

    def d_head(r, first=0):
        start = pl.multiple_of((g * GROUP + r) * PAIR + first, HD)
        return d_out[pl.ds(start, PAIR - first)]

    before = [dq[g, r] for r in range(GROUP)]

    def products(r):
        return nn(natural, queries[g, r]), nn(natural, d_head(r))

    ahead = products(0)
    done = []
    d_keys, d_vals = None, None
    for r in range(GROUP):
        scores, d_probs = ahead
        if r + 1 < GROUP:
            ahead = products(r + 1)
        probs = jnp.exp2(scores - lse[g, r])
        if masked:
            key_at = lax.broadcasted_iota(jnp.int32, scores.shape, 0)
            query_at = lax.broadcasted_iota(jnp.int32, scores.shape, 1)
            probs = jnp.where(key_at <= query_at, probs, 0.0)
        d_scores = (probs * (d_probs - delta[g, r])).astype(BF16)
        keys_term = nt(queries[g, r, :HD], d_scores)
        vals_term = nt(d_head(r, HD), probs.astype(BF16))
        d_keys = keys_term if d_keys is None else d_keys + keys_term
        d_vals = vals_term if d_vals is None else d_vals + vals_term
        done.append(before[r] + nn(packed[:HD], d_scores))
    for r in range(GROUP):
        dq[g, r] = done[r]
    return d_keys * LN2, d_vals


def log2(n):
    return n.bit_length() - 1


HALVINGS = 3


class Cube:
    def __init__(self, links, send_sem, recv_sem, credit):
        self.send_sem, self.recv_sem, self.credit = send_sem, recv_sem, credit
        self.bits = [bit for bit, _ in links]
        self.partners = [partner for _, partner in links]
        self.depth = len(links)
        self.steps = self.depth + HALVINGS

    def span(self, rows, d):
        lo, size = 0, rows
        for e in range(1, d + 1):
            size = size // 2
            lo = lo + self.bits[e] * size
        return lo, size

    def owned(self, part, d):
        lo, size = self.span(part.shape[1], d)
        return part.at[self.bits[0], pl.ds(pl.multiple_of(lo, 16), size)]

    def transfer(self, part, landing, i, k):
        mine, d = self.bits[0], k
        if k == 0:
            src, dst = part.at[1 - mine], landing[0]
        elif k < HALVINGS:
            before, _ = self.span(part.shape[1], k - 1)
            _, size = self.span(part.shape[1], k)
            start = pl.multiple_of(before + (1 - self.bits[k]) * size, 16)
            src, dst = part.at[mine, pl.ds(start, size)], landing[k]
        elif k < self.depth:
            src, dst = self.owned(part, HALVINGS - 1), landing[k]
        else:
            d = self.steps - 1 - k
            src = dst = self.owned(part, d)
        return pltpu.make_async_remote_copy(
            src_ref=src,
            dst_ref=dst,
            send_sem=self.send_sem.at[i, k],
            recv_sem=self.recv_sem.at[i, k],
            device_id=self.partners[d],
            device_id_type=MESH,
        )

    def begin(self, part, landing, i, k):
        if k >= self.depth:
            pl.semaphore_wait(self.credit.at[i, self.steps - 1 - k], 1)
        self.transfer(part, landing, i, k).start()

    def step(self, part, landing, i, k):
        moved = self.transfer(part, landing, i, k)
        if k < self.depth:
            moved.wait_send()
            if k < HALVINGS:
                pl.semaphore_signal(
                    self.credit.at[i, k], inc=1, device_id=self.partners[k], device_id_type=MESH
                )
        moved.wait_recv()
        if k < self.depth:
            rows = self.owned(part, min(k, HALVINGS - 1))
            rows[...] = rows[...] + landing[k][...]
        if k + 1 < self.steps:
            self.begin(part, landing, i, k + 1)

    def drain(self, part, landing, i):
        for k in range(self.depth, self.steps):
            self.transfer(part, landing, i, k).wait_send()


MAIN_SLOTS = [
    [-7, -5, -3, -1, 1, 4, 6, 8],
    [-6, -4, -2, 0, 2, 5, 10, 12],
    [-5, -2, 0, 2, 5, 7, 9, 11],
    [-4, -1, 1, 3, 9, 11, 16, 20],
    [-3, 0, 2, 4, 8, 10, 13, 23],
    [1, 3, 7, 9, 13, 14, 17, 23],
    [-1, 6, 8, 11, 14, 16, 20, 22],
]
LATE_SLOTS = [[13, 14, 16, 17, 18, 19, 22, 23], [18, 19, 20, 21, 22, 23, 25, 28]]
LAGS = [7, 6, 3, 2]


def tables(count, depth, blocks):
    if (count, depth, blocks) == (len(MAIN_SLOTS), 5, 8):
        return MAIN_SLOTS, LATE_SLOTS, LAGS
    floors = blocks // 2
    main = []
    for i in range(count):
        row = [i - count, 2 * i - count + 2]
        row += [2 * (i + k) - count for k in range(HALVINGS - 1, depth + 1)]
        main.append(row + [row[-1] + 3 + i // 2, row[-1] + 4 + i // 2])
    waits = [1, 3, 4] + list(range(5, 2 * depth - 1, 2))
    waits += [waits[-1] + 1, waits[-1] + 3, waits[-1] + 4]
    late = [[g * blocks + blocks + 1 + w for w in waits] for g in range(KVH - 1)]
    return main, late, [2 * (floors - z) for z in range(floors)]


def rounds(slots, first, last):
    lists = []
    for i, n in enumerate(slots):
        if first <= n < last:
            for chosen in lists:
                if all(n != other for _, other in chosen):
                    chosen.append((i, n))
                    break
            else:
                lists.append([(i, n)])
    return lists


def at_slot(chosen, n):
    found = 0
    for i, slot in chosen:
        found = found + jnp.where(n == slot, i + 1, 0)
    return found


def cube_links(s, b, sizes):
    seqs, blocks = sizes
    links = []
    for bit in range(log2(seqs)):
        mine = (s // 2**bit) % 2
        links.append((mine, (s + 2**bit * (1 - 2 * mine), b)))
    for bit in range(log2(blocks)):
        mine = (b // 2**bit) % 2
        links.append((mine, (s, b + 2**bit * (1 - 2 * mine))))
    return links


def row_counts(rows, depth):
    return [rows >> min(k, HALVINGS - 1) for k in range(depth)]


def padded_rows(rows):
    return (rows + 63) // 64 * 64


def mega_kernel(
    sizes,
    keep_mask, keep_rate, exit_scales,
    tokens, groups, gain1, gain2, wk, wv, wq, cos, sin,
    wo_hbm, wg_hbm, wu_hbm, wd_hbm, cot_hbm,
    layer_out, input_grad, parts, tails, gains,
    wo, stream, cotangent,
    queries, kv_all, attended, mixed_t, top, total,
    d_normed2, d_out,
    chain, cross,
    load_sem, stream_sem, send_sem, recv_sem, cube_send, cube_recv, credit, tail_send, tail_recv, tail_credit,
    gain_send, gain_recv, kv_send, chain_recv, cross_recv, gain_landing,
    *landings,
):
    seqs, blocks = sizes
    s, b = lax.axis_index("seq"), lax.axis_index("blk")
    z, y, floors = b // 2, b % 2, blocks // 2
    above, below, across = (s, b + 2), (s, b - 2), (s, b + 1 - 2 * y)
    has_above, has_below = z < floors - 1, z > 0
    links = cube_links(s, b, sizes)
    cube = Cube(links, cube_send, cube_recv, credit)
    tail_cube = Cube(links, tail_send, tail_recv, tail_credit)
    depth = cube.depth
    count = parts.shape[0]

    def main(i):
        return parts.at[i], [r.at[i] for r in landings[:depth]], i

    def late(i):
        return tails.at[i], [r.at[i] for r in landings[depth:]], i

    loads = [
        pltpu.make_async_copy(src, dst, load_sem.at[i])
        for i, (src, dst) in enumerate(
            [(wo_hbm, wo), (cot_hbm, cotangent)]
        )
    ]
    step = 2 * LANES
    chunks = wg_hbm.shape[1] // step

    def weights(f):
        at = pl.ds(pl.multiple_of(f * step, step), step)
        return [
            pltpu.make_async_copy(ref.at[:, at], stream.at[f % 2, k], stream_sem.at[f % 2, k])
            for k, ref in enumerate((wg_hbm, wu_hbm, wd_hbm))
        ]

    for load in loads + weights(0):
        load.start()

    barrier = pltpu.get_barrier_semaphore()

    def greet(device):
        pl.semaphore_signal(barrier, inc=1, device_id=device, device_id_type=MESH)

    for device in cube.partners:
        greet(device)
    odd = z % 2
    extra_below = has_below & (odd == 0)
    extra_above = has_above & (odd == 1)

    @pl.when(extra_below)
    def _():
        greet(below)

    @pl.when(extra_above)
    def _():
        greet(above)

    extra = extra_below.astype(jnp.int32) + extra_above.astype(jnp.int32)

    def copy(kind, j, g):
        return pltpu.make_async_remote_copy(
            src_ref=kv_all.at[j, g],
            dst_ref=kv_all.at[j, g],
            send_sem=send_sem.at[kind, j, g],
            recv_sem=recv_sem.at[j, g],
            device_id=above if kind == 0 else across,
            device_id_type=MESH,
        )

    normed = normalize(tokens, gain1)
    c, sn = cos[...], sin[...]
    project_kv(normed, wk, wv, c, sn, kv_all.at[b])
    pl.semaphore_wait(barrier, depth + extra)

    def send_own(g, carry):
        @pl.when(has_above)
        def _():
            copy(0, b, g).start()

        @pl.when(y == 0)
        def _():
            copy(1, b, g).start()

        return carry

    lax.fori_loop(0, KVH, send_own, 0)
    project_q(normed, wq, c, sn, queries)

    def own(g, carry):
        first_unit(g, queries, kv_all[b, g], attended, top, total)
        return carry

    lax.fori_loop(0, KVH, own, 0)

    def level(m, carry):
        def one(g, inner):
            @pl.when(m <= z)
            def _():
                j = b - 2 * m
                copy(0, j, g).wait_recv()

                @pl.when(has_above)
                def _():
                    copy(0, j, g).start()

                copy(1, j, g).start()
                next_unit(g, queries, kv_all[j, g], attended, top, total)

            @pl.when((m >= 2) | (y == 1))
            def _():
                j = b - 2 * m + 3 - 2 * y
                copy(1, j, g).wait_recv()
                next_unit(g, queries, kv_all[j, g], attended, top, total)

            return inner

        return lax.fori_loop(0, KVH, one, carry)

    lax.fori_loop(1, z + 2, level, 0)
    lse = top
    finish_forward(attended, top, total, mixed_t, lse)

    def drain_forward(m, carry):
        def one(g, inner):
            j = b - 2 * m

            @pl.when(has_above)
            def _():
                copy(0, j, g).wait_send()

            @pl.when((m >= 1) | (y == 0))
            def _():
                copy(1, j, g).wait_send()

            return inner

        return lax.fori_loop(0, KVH, one, carry)

    lax.fori_loop(0, z + 1, drain_forward, 0)

    whole_head = 2 * floors + 1
    end = (KVH - 1) * blocks + whole_head + 2
    main_slots, late_slots, lags = tables(count, depth, blocks)
    lead = count + 1

    def serve(n, first, last):
        for k in range(cube.steps - 1, -1, -1):
            for exchange, block_of, slots in (
                (tail_cube, late, late_slots),
                (cube, main, main_slots),
            ):
                for chosen in rounds([row[k] for row in slots], first, last):
                    found = at_slot(chosen, n)

                    @pl.when(found > 0)
                    def _(exchange=exchange, block_of=block_of, k=k, found=found):
                        exchange.step(*block_of(jnp.maximum(found - 1, 0)), k)

    def serve_now(n):
        for k in range(cube.steps - 1, -1, -1):
            for exchange, block_of, slots in (
                (tail_cube, late, late_slots),
                (cube, main, main_slots),
            ):
                for i, row in enumerate(slots):
                    if row[k] == n or (n == end + cube.steps - 3 and row[k] > n):
                        exchange.step(*block_of(i), k)

    for load in loads:
        load.wait()
    bs = keep_mask[0].astype(F32) * keep_rate[0]
    gain = column(gain2[...])
    hidden = tokens[...].astype(F32) + bs * nn(wo[...].T, mixed_t[...])
    r2 = inverse_rms(hidden)
    normed2_t = (hidden * r2 * gain).astype(BF16)
    normed2 = normed2_t.T

    def seed():
        by_group = jnp.where(groups[...] == 1, exit_scales[1], exit_scales[0])
        return cotangent[...].astype(F32) * by_group

    d_down_t = (bs * seed()).astype(BF16)
    d_down = d_down_t.T
    width, rows = hidden.shape
    for i in range(count):
        filled = 3 * width if i < chunks else 5 * width // 2
        for half in range(2 if filled < parts.shape[2] else 0):
            parts[i, half, filled:] = jnp.zeros((parts.shape[2] - filled, LANES), BF16)
    down = d_hidden = input_grad
    down[...] = jnp.zeros_like(down)
    d_normed2[...] = jnp.zeros_like(d_normed2)

    def chunk(f, carry):
        for load in weights(f):
            load.wait()

        @pl.when(f + 1 < chunks)
        def _():
            for load in weights(f + 1):
                load.start()

        wg, wu, wd = (stream.at[f % 2, k] for k in range(3))
        gate = nn(normed2, wg[...])
        up = nn(normed2, wu[...])
        d_act = nn(d_down, wd[...])
        sig = 1.0 / (1.0 + jnp.exp(-gate))
        silu = gate * sig
        act = (silu * up).astype(BF16)
        d_gate = (d_act * up * (sig + silu * (1.0 - sig))).astype(BF16)
        d_up = (d_act * silu).astype(BF16)
        grads = (nn(normed2_t, d_gate), nn(normed2_t, d_up), nn(d_down_t, act))
        for k, value in enumerate(grads):
            for half in range(2):
                parts[f, half, k * width : (k + 1) * width] = value[
                    :, half * LANES : (half + 1) * LANES
                ].astype(BF16)
        down[...] += nt(wd[...], act)
        d_normed2[...] += nt(wg[...], d_gate) + nt(wu[...], d_up)
        cube.begin(*main(f), 0)
        serve(f - lead, -lead, -2)
        return carry

    lax.fori_loop(0, chunks, chunk, 0)
    layer_out[...] = (hidden + bs * down[...]).astype(BF16)
    dn = d_normed2[...]
    gain2_grad = jnp.sum(dn * hidden * r2, axis=1, keepdims=True)
    gained = gain * dn
    dh = seed() + r2 * gained - hidden * (r2 * r2 * r2) * jnp.mean(gained * hidden, axis=0, keepdims=True)
    d_hidden[...] = dh
    d_branch = (bs * dh).astype(BF16)
    out_grad = nt(mixed_t[...], d_branch)
    half_rows = width // 2
    last = parts.at[chunks]
    last[0, :width] = out_grad[:, :LANES].astype(BF16)
    last[0, width : 2 * width] = out_grad[:, LANES : 2 * LANES].astype(BF16)
    middle = out_grad[:, 2 * LANES : 3 * LANES].astype(BF16)
    last[0, 2 * width : 2 * width + half_rows] = middle[:half_rows]
    last[1, :half_rows] = middle[half_rows:]
    last[1, half_rows : half_rows + width] = out_grad[:, 3 * LANES : 4 * LANES].astype(BF16)
    last[1, half_rows + width : half_rows + 2 * width] = last_block(out_grad)
    cube.begin(*main(chunks), 0)
    serve_now(-2)
    d_mixed = nn(wo[...], d_branch).astype(BF16)
    delta = total
    for h in range(H):
        g, r = h // GROUP, h % GROUP
        head = d_mixed[h * HD : (h + 1) * HD]
        d_out[h * PAIR : h * PAIR + HD] = jnp.zeros((HD, rows), BF16)
        d_out[h * PAIR + HD : (h + 1) * PAIR] = head
        delta[g, r] = jnp.sum(head.astype(F32) * attended[g, r], axis=0, keepdims=True)
    dq = attended
    dq[...] = jnp.zeros_like(dq)
    normed_kept = mixed_t
    normed_kept[...] = normalize(tokens, gain1)
    serve_now(-1)

    def kv_down(j, g):
        return pltpu.make_async_remote_copy(
            src_ref=kv_all.at[j, g],
            dst_ref=chain.at[j // 2, g],
            send_sem=kv_send.at[j, g],
            recv_sem=chain_recv.at[j // 2, g],
            device_id=below,
            device_id_type=MESH,
        )

    def kv_across(j, g):
        return pltpu.make_async_remote_copy(
            src_ref=kv_all.at[j, g],
            dst_ref=cross.at[j // 2, g],
            send_sem=kv_send.at[j, g],
            recv_sem=cross_recv.at[j // 2, g],
            device_id=across,
            device_id_type=MESH,
        )

    d_kv = d_normed2
    lag = lags[0]
    for i in range(1, floors):
        lag = jnp.where(z == i, lags[i], lag)
    nq, nk = H * HD, KVH * HD
    span = GROUP * PAIR

    def finish_head(g):
        at = pl.multiple_of(g * span, PAIR)
        c, sn = cos[...], -sin[...]
        for r in range(GROUP):
            piece = turn(dq[g, r] * HD**-0.5, c, sn)
            d_out[pl.ds(at + r * HD, HD)] = piece.astype(BF16)
        pair = d_kv[pl.ds(pl.multiple_of(g * PAIR, PAIR), PAIR)]
        d_out[pl.ds(at + GROUP * HD, HD)] = turn(pair[:HD], c, sn).astype(BF16)
        d_out[pl.ds(at + (GROUP + 1) * HD, HD)] = pair[HD:].astype(BF16)
        high = (GROUP + 2) * HD
        grad = nt(d_out[pl.ds(at, high)], normed_kept[...]).astype(BF16)
        tails[g, 0, :high] = grad[:, :LANES]
        tails[g, 0, high : 2 * high] = grad[:, LANES : 2 * LANES]
        tails[g, 0, 2 * high : 5 * high // 2] = grad[: high // 2, 2 * LANES : 3 * LANES]
        tails[g, 1, : high // 2] = grad[high // 2 :, 2 * LANES : 3 * LANES]
        tails[g, 1, high // 2 : 3 * high // 2] = grad[:, 3 * LANES : 4 * LANES]
        tails[g, 1, 3 * high // 2 : 5 * high // 2] = jnp.concatenate(
            [grad[:, 4 * LANES :], jnp.zeros((high, HD), BF16)], axis=1
        )
        for half in range(2):
            rest = tails.shape[2] - 5 * high // 2
            tails[g, half, 5 * high // 2 :] = jnp.zeros((rest, LANES), BF16)
        tail_cube.begin(*late(g), 0)

    def slot(n, carry):
        g, j = n // blocks, n % blocks
        busy = n < KVH * blocks

        def unit(masked):
            d_keys, d_vals = grad_unit(g, queries, d_out, lse, delta, kv_all[j, g], dq, masked)
            kv_all[j, g, :HD] = d_keys.astype(BF16)
            kv_all[j, g, HD:] = d_vals.astype(BF16)

        @pl.when(busy & (j < b))
        def _():
            unit(False)

        @pl.when(busy & (j == b))
        def _():
            unit(True)

        @pl.when(busy & (j <= b) & (j % 2 != y))
        def _():
            kv_across(j, g).start()

        ready = n - lag
        at = jnp.maximum(ready, 0)
        gg, jj = at // blocks, at % blocks
        due = (ready >= 0) & (ready < KVH * blocks) & (jj % 2 == y)
        rows_of = pl.ds(pl.multiple_of(jnp.minimum(gg, KVH - 1) * PAIR, PAIR), PAIR)

        @pl.when(due & (jj < b))
        def _():
            kv_across(jj, gg).wait_recv()
            both = kv_all[jj, gg].astype(F32) + cross[jj // 2, gg].astype(F32)

            @pl.when(has_above)
            def _():
                kv_down(jj, gg).wait_recv()
                kv_all[jj, gg] = (both + chain[jj // 2, gg].astype(F32)).astype(BF16)

            @pl.when(jnp.logical_not(has_above))
            def _():
                kv_all[jj, gg] = both.astype(BF16)

            kv_down(jj, gg).start()

        @pl.when(due & (jj == b))
        def _():
            d_kv[rows_of] = kv_all[jj, gg].astype(F32)

            @pl.when(y == 0)
            def _():
                kv_across(jj, gg).wait_recv()
                d_kv[rows_of] = d_kv[rows_of] + cross[jj // 2, gg].astype(F32)

            @pl.when(has_above)
            def _():
                kv_down(jj, gg).wait_recv()
                d_kv[rows_of] = d_kv[rows_of] + chain[jj // 2, gg].astype(F32)

        settled = n - whole_head

        @pl.when((settled >= 0) & (settled % blocks == 0) & (settled // blocks < KVH))
        def _():
            finish_head(settled // blocks)

        serve(n, 0, end)

        @pl.when(n == end - 1)
        def _():
            tail_cube.step(*late(KVH - 1), 0)

        return carry

    lax.fori_loop(0, end, slot, 0)

    def drain_backward(n, carry):
        j, g = n // KVH, n % KVH

        @pl.when(j % 2 != y)
        def _():
            kv_across(j, g).wait_send()

        @pl.when((j % 2 == y) & (j < b))
        def _():
            kv_down(j, g).wait_send()

        return carry

    lax.fori_loop(0, KVH * (b + 1), drain_backward, 0)

    x = tokens[...].astype(F32)
    r1 = inverse_rms(x)
    weight = column(gain1[...])
    d_normed = jnp.zeros_like(x)
    for g in range(KVH):
        first = g * span
        middle, last_row = first + GROUP * HD, first + (GROUP + 1) * HD
        heads = slice(g * GROUP * HD, (g + 1) * GROUP * HD)
        own_head = slice(g * HD, (g + 1) * HD)
        d_normed = (
            d_normed
            + nn(wq[:, heads], d_out[first:middle])
            + nn(wk[own_head].T, d_out[middle:last_row])
            + nn(wv[own_head].T, d_out[last_row : last_row + HD])
        )
    pads = jnp.zeros((1, gains.shape[1] - width), F32)
    for i, values in enumerate((jnp.sum(d_normed * x * r1, axis=1, keepdims=True), gain2_grad)):
        gains[i : i + 1] = jnp.concatenate([as_row(values), pads], axis=1)
    gains[2:] = jnp.zeros((gains.shape[0] - 2, gains.shape[1]), F32)

    def gain_swap(d):
        return pltpu.make_async_remote_copy(
            src_ref=gains,
            dst_ref=gain_landing.at[d],
            send_sem=gain_send.at[d],
            recv_sem=gain_recv.at[d],
            device_id=cube.partners[d],
            device_id_type=MESH,
        )

    gain_swap(0).start()
    tail_cube.step(*late(KVH - 1), 1)
    gained = weight * d_normed
    input_grad[...] = (
        d_hidden[...] + r1 * gained - x * (r1 * r1 * r1) * jnp.mean(gained * x, axis=0, keepdims=True)
    )
    for k in range(2, cube.steps):
        serve_now(end + k - 2)
        if k - 2 < depth:
            gain_swap(k - 2).wait()
            gains[...] = gains[...] + gain_landing[k - 2]
            if k - 1 < depth:
                gain_swap(k - 1).start()
        tail_cube.step(*late(KVH - 1), k)
    for i in range(count):
        cube.drain(*main(i))
    for i in range(KVH):
        tail_cube.drain(*late(i))


def unpack_kernel(
    chunks, parts, tails, gains, late_out, late_grad,
    gate, up, down, output_hbm, query_hbm, key_hbm, value_hbm, gain1, gain2, layer_out, input_grad,
    output, query, key, value, sems,
):
    i = pl.program_id(0)
    width = gate.shape[0]
    layer_out[...] = late_out[...]
    input_grad[...] = late_grad[...]
    small = ((output, output_hbm), (query, query_hbm), (key, key_hbm), (value, value_hbm))
    copies = [pltpu.make_async_copy(a, b, sems.at[n]) for n, (a, b) in enumerate(small)]

    @pl.when(i > 0)
    def _():
        for k, out in enumerate((gate, up, down)):
            for half in range(2):
                piece = parts[0, half, k * width : (k + 1) * width]
                out[:, half * LANES : (half + 1) * LANES] = piece.astype(F32)

    def five(ref, at, rows):
        half = rows // 2
        yield ref[at + (0, slice(0, rows))]
        yield ref[at + (0, slice(rows, 2 * rows))]
        yield jnp.concatenate(
            [ref[at + (0, slice(2 * rows, 2 * rows + half))], ref[at + (1, slice(0, half))]], axis=0
        )
        yield ref[at + (1, slice(half, half + rows))]
        yield ref[at + (1, slice(half + rows, half + 2 * rows))]

    @pl.when(i == 0)
    def _():
        for k, block in enumerate(five(parts, (0,), width)):
            size = min(LANES, width - k * LANES)
            output[:, k * LANES : k * LANES + size] = block.astype(F32)[:, :size]
        high = GROUP * HD
        for k in range(5):
            size = min(LANES, width - k * LANES)
            lanes = slice(k * LANES, k * LANES + size)
            columns = []
            for g in range(KVH):
                block = list(five(tails, (g,), high + PAIR))[k].astype(F32)[:, :size]
                own = slice(g * HD, (g + 1) * HD)
                key[own, lanes] = block[high : high + HD]
                value[own, lanes] = block[high + HD :]
                columns.append(block[:high])
            query[lanes, :] = jnp.concatenate(columns, axis=0).T
        gain1[...] = gains[0, :width]
        gain2[...] = gains[1, :width]
        for copy in copies:
            copy.start()

    @pl.when(i == chunks)
    def _():
        for copy in copies:
            copy.wait()


def last_block(grad):
    return jnp.concatenate(
        [grad[:, 4 * LANES :], jnp.zeros((grad.shape[0], LANES - HD), F32)], axis=1
    ).astype(BF16)


def body(sizes, tokens, positions, groups, keep_mask, exit_scales, keep_rate, wq, wk, wv, wo, wg, wu, wd, gain1, gain2, cotangent):
    seqs, blocks = sizes
    depth = log2(seqs) + log2(blocks)
    tokens, cotangent = tokens[0].T, cotangent[0].T
    wk, wv, wd = wk.T, wv.T, wd.T
    width, rows = tokens.shape
    ff = wg.shape[1]
    nq, nk = H * HD, KVH * HD
    frequency = 1.0 / ROPE_BASE ** (jnp.arange(HALF, dtype=F32) * (2.0 / HD))
    angle = frequency[:, None] * positions[0].astype(F32)[None, :]
    cos, sin = jnp.cos(angle), jnp.sin(angle)

    chunks = ff // (2 * LANES)
    count = chunks + 1
    part_rows = padded_rows(3 * width)
    tail_rows = padded_rows(5 * (GROUP + 2) * HD // 2)
    gain_shape = (8, 5 * LANES)
    vmem, smem, hbm = (pl.BlockSpec(memory_space=m) for m in (pltpu.VMEM, pltpu.SMEM, pl.ANY))
    head_t = (KVH, GROUP, PAIR, rows)
    head_o = (KVH, GROUP, HD, rows)
    head_1 = (KVH, GROUP, 1, rows)
    dma = pltpu.SemaphoreType.DMA
    scratch = [
        pltpu.VMEM(wo.shape, BF16),
        pltpu.VMEM((2, 3, width, 2 * LANES), BF16),
        pltpu.VMEM(cotangent.shape, BF16),
        pltpu.VMEM(head_t, BF16),
        pltpu.VMEM((blocks, KVH, PAIR, rows), BF16),
        pltpu.VMEM(head_o, F32),
        pltpu.VMEM((nq, rows), BF16),
        pltpu.VMEM(head_1, F32),
        pltpu.VMEM(head_1, F32),
        pltpu.VMEM((width, rows), F32),
        pltpu.VMEM((H * PAIR, rows), BF16),
        pltpu.VMEM((blocks // 2, KVH, PAIR, rows), BF16),
        pltpu.VMEM((blocks // 2, KVH, PAIR, rows), BF16),
        dma((2,)),
        dma((2, 3)),
        dma((2, blocks, KVH)),
        dma((blocks, KVH)),
        dma((count, depth + HALVINGS)),
        dma((count, depth + HALVINGS)),
        pltpu.SemaphoreType.REGULAR((count, HALVINGS)),
        dma((KVH, depth + HALVINGS)),
        dma((KVH, depth + HALVINGS)),
        pltpu.SemaphoreType.REGULAR((KVH, HALVINGS)),
        dma((depth,)),
        dma((depth,)),
        dma((blocks, KVH)),
        dma((blocks // 2, KVH)),
        dma((blocks // 2, KVH)),
    ]
    scratch += [pltpu.VMEM((depth,) + gain_shape, F32)]
    scratch += [pltpu.VMEM((count, n, LANES), BF16) for n in row_counts(part_rows, depth)]
    scratch += [pltpu.VMEM((KVH, n, LANES), BF16) for n in row_counts(tail_rows, depth)]
    layer_out, input_grad, parts, tails, gains = pl.pallas_call(
        functools.partial(mega_kernel, sizes),
        out_shape=[
            jax.ShapeDtypeStruct((width, rows), BF16),
            jax.ShapeDtypeStruct((width, rows), F32),
            jax.ShapeDtypeStruct((count, 2, part_rows, LANES), BF16),
            jax.ShapeDtypeStruct((KVH, 2, tail_rows, LANES), BF16),
            jax.ShapeDtypeStruct(gain_shape, F32),
        ],
        in_specs=[smem] * 3 + [vmem] * 9 + [hbm] * 5,
        out_specs=[vmem] * 5,
        scratch_shapes=scratch,
        compiler_params=pltpu.CompilerParams(
            vmem_limit_bytes=VMEM_LIMIT, collective_id=0, has_side_effects=True
        ),
    )(
        keep_mask, keep_rate, exit_scales,
        tokens, groups, gain1, gain2, wk, wv, wq, cos, sin,
        wo, wg, wu, wd, cotangent,
    )

    wide = pl.BlockSpec((width, 2 * LANES), lambda i: (0, jnp.maximum(i - 1, 0)))
    lines = pl.BlockSpec((width // chunks, rows), lambda i: (jnp.maximum(i - 1, 0), 0))
    line = pl.BlockSpec((width,), lambda i: (0,))
    small = [(nq, width), (width, nq), (nk, width), (nk, width)]
    (gate_grad, up_grad, down_grad, output_grad, query_grad, key_grad, value_grad, gain1_grad, gain2_grad, layer_out, input_grad) = pl.pallas_call(
        functools.partial(unpack_kernel, chunks),
        grid=(count,),
        out_shape=[jax.ShapeDtypeStruct((width, ff), F32)] * 3
        + [jax.ShapeDtypeStruct(shape, F32) for shape in small + [(width,), (width,)]]
        + [jax.ShapeDtypeStruct((width, rows), t) for t in (BF16, F32)],
        in_specs=[
            pl.BlockSpec((1, 2, part_rows, LANES), lambda i: ((i + chunks) % count, 0, 0, 0)),
            pl.BlockSpec(tails.shape, lambda i: (0,) * 4),
            pl.BlockSpec(gain_shape, lambda i: (0, 0)),
            lines,
            lines,
        ],
        out_specs=[wide] * 3 + [hbm] * 4 + [line] * 2 + [lines] * 2,
        scratch_shapes=[pltpu.VMEM(shape, F32) for shape in small] + [dma((4,))],
        compiler_params=pltpu.CompilerParams(vmem_limit_bytes=VMEM_LIMIT),
    )(parts, tails, gains, layer_out, input_grad)
    return (
        layer_out.T[None],
        input_grad.T[None],
        query_grad,
        key_grad.T,
        value_grad.T,
        output_grad,
        gate_grad,
        up_grad,
        down_grad.T,
        gain1_grad,
        gain2_grad,
    )


def solution(mesh):
    local = P("seq", "blk", None)
    pair = P("seq", "blk")
    placed = (local, pair, pair, P("seq")) + (P(),) * 11 + (local,)
    return jax.shard_map(
        functools.partial(body, (mesh.shape["seq"], mesh.shape["blk"])),
        mesh=mesh,
        in_specs=placed,
        out_specs=(local, local) + (P(),) * 9,
        check_vma=False,
    )
```

```python
import functools

import jax
import jax.numpy as jnp
from jax import lax
from jax.experimental import pallas as pl
from jax.experimental.pallas import tpu as pltpu
from jax.sharding import PartitionSpec as P

H = 9
KVH = 3
HD = 64
GROUP = H // KVH
HALF = HD // 2
PAIR = 2 * HD

EPSILON = 1e-05
ROPE_BASE = 100000.0
MASKED = -1e30
LOG2E = 1.4426950408889634
LN2 = 0.6931471805599453
F32 = jnp.float32
BF16 = jnp.bfloat16
VMEM_LIMIT = 61 * 1024 * 1024
MESH = pl.DeviceIdType.MESH
LANES = 128
REROUTED = 2


def nn(a, b):
    return lax.dot_general(a, b, (((1,), (0,)), ((), ())), preferred_element_type=F32)


def nt(a, b):
    return lax.dot_general(a, b, (((1,), (1,)), ((), ())), preferred_element_type=F32)


def column(values):
    return jnp.broadcast_to(values[None, :], (8, values.shape[0])).T[:, :1]


def as_row(values):
    return jnp.broadcast_to(values, (values.shape[0], 8)).T[:1]


def inverse_rms(values):
    return lax.rsqrt(jnp.mean(values * values, axis=0, keepdims=True) + EPSILON)


def turn(rows, cos, sin):
    u, w = rows[:HALF], rows[HALF:]
    return jnp.concatenate([u * cos - w * sin, w * cos + u * sin], axis=0)


def normalize(tokens, gain):
    x = tokens[...].astype(F32)
    return (x * inverse_rms(x) * column(gain[...])).astype(BF16)


def project_kv(normed, wk, wv, cos, sin, kv):
    keys = nn(wk[...], normed)
    vals = nn(wv[...], normed)
    for g in range(KVH):
        span = slice(g * HD, (g + 1) * HD)
        kv[g, :HD, :] = turn(keys[span], cos, sin).astype(BF16)
        kv[g, HD:, :] = vals[span].astype(BF16)


def project_q(normed, wq, cos, sin, queries):
    raw = nn(wq[...].T, normed)
    factor = HD**-0.5 * LOG2E
    for h in range(H):
        turned = turn(raw[h * HD : (h + 1) * HD], cos, sin) * factor
        queries[h // GROUP, h % GROUP, :HD, :] = turned.astype(BF16)
        queries[h // GROUP, h % GROUP, HD:, :] = jnp.zeros((HD, raw.shape[1]), BF16)


def values_and_ones(packed):
    ones = jnp.ones((16, packed.shape[1]), BF16)
    return jnp.concatenate([packed[HD:], ones], axis=0)


def first_unit(g, queries, packed, out, top, total):
    rows = queries.shape[-1]
    part = rows // 2
    natural = packed.T
    values = values_and_ones(packed)
    items = [(r, c) for r in range(GROUP) for c in range(2)]

    def scores_of(i):
        r, c = items[i]
        return nn(natural[: (c + 1) * part], queries[g, r, :, c * part : (c + 1) * part])

    scores = scores_of(0)
    done = []
    for i, (r, c) in enumerate(items):
        later = scores_of(i + 1) if i + 1 < len(items) else None
        key_at = lax.broadcasted_iota(jnp.int32, scores.shape, 0)
        query_at = lax.broadcasted_iota(jnp.int32, scores.shape, 1) + c * part
        scores = jnp.where(key_at <= query_at, scores, MASKED)
        high = jnp.max(scores, axis=0, keepdims=True)
        probs = jnp.exp2(scores - high)
        done.append((high, nn(values[:, : (c + 1) * part], probs.astype(BF16))))
        scores = later
    for (r, c), (high, summed) in zip(items, done):
        cols = slice(c * part, (c + 1) * part)
        top[g, r, :, cols] = high
        total[g, r, :, cols] = summed[HD : HD + 1]
        out[g, r, :, cols] = summed[:HD]


def next_unit(g, queries, packed, out, top, total):
    natural = packed.T
    values = values_and_ones(packed)
    before = [(top[g, r], total[g, r], out[g, r]) for r in range(GROUP)]
    scores = [nn(natural, queries[g, r]) for r in range(2)]
    done = []
    for r in range(GROUP):
        if r + 2 < GROUP:
            scores.append(nn(natural, queries[g, r + 2]))
        old, count, acc = before[r]
        high = jnp.maximum(old, jnp.max(scores[r], axis=0, keepdims=True))
        probs = jnp.exp2(scores[r] - high)
        fade = jnp.exp2(old - high)
        summed = nn(values, probs.astype(BF16))
        done.append((high, count * fade + summed[HD : HD + 1], acc * fade + summed[:HD]))
    for r, (high, count, acc) in enumerate(done):
        top[g, r] = high
        total[g, r] = count
        out[g, r] = acc


def finish_forward(out, top, total, mixed_t, lse):
    for h in range(H):
        g, r = h // GROUP, h % GROUP
        scaled = out[g, r] * (1.0 / total[g, r])
        out[g, r] = scaled
        mixed_t[h * HD : (h + 1) * HD, :] = scaled.astype(BF16)
        lse[g, r] = top[g, r] + jnp.log2(total[g, r])


def grad_unit(g, queries, d_out, lse, delta, packed, dq, masked):
    rows = queries.shape[-1]
    natural = packed.T

    def d_head(r, first=0):
        start = pl.multiple_of((g * GROUP + r) * PAIR + first, HD)
        return d_out[pl.ds(start, PAIR - first)]

    before = [dq[g, r] for r in range(GROUP)]

    def products(r):
        return nn(natural, queries[g, r]), nn(natural, d_head(r))

    ahead = products(0)
    done = []
    d_keys, d_vals = None, None
    for r in range(GROUP):
        scores, d_probs = ahead
        if r + 1 < GROUP:
            ahead = products(r + 1)
        probs = jnp.exp2(scores - lse[g, r])
        if masked:
            key_at = lax.broadcasted_iota(jnp.int32, scores.shape, 0)
            query_at = lax.broadcasted_iota(jnp.int32, scores.shape, 1)
            probs = jnp.where(key_at <= query_at, probs, 0.0)
        d_scores = (probs * (d_probs - delta[g, r])).astype(BF16)
        keys_term = nt(queries[g, r, :HD], d_scores)
        vals_term = nt(d_head(r, HD), probs.astype(BF16))
        d_keys = keys_term if d_keys is None else d_keys + keys_term
        d_vals = vals_term if d_vals is None else d_vals + vals_term
        done.append(before[r] + nn(packed[:HD], d_scores))
    for r in range(GROUP):
        dq[g, r] = done[r]
    return d_keys * LN2, d_vals


def log2(n):
    return n.bit_length() - 1


HALVINGS = 3


class Cube:
    def __init__(self, links, send_sem, recv_sem, credit):
        self.send_sem, self.recv_sem, self.credit = send_sem, recv_sem, credit
        self.bits = [bit for bit, _ in links]
        self.partners = [partner for _, partner in links]
        self.depth = len(links)
        self.steps = self.depth + HALVINGS

    def span(self, rows, d):
        lo, size = 0, rows
        for e in range(1, d + 1):
            size = size // 2
            lo = lo + self.bits[e] * size
        return lo, size

    def owned(self, part, d):
        lo, size = self.span(part.shape[1], d)
        return part.at[self.bits[0], pl.ds(pl.multiple_of(lo, 16), size)]

    def transfer(self, part, landing, i, k):
        mine, d = self.bits[0], k
        if k == 0:
            src, dst = part.at[1 - mine], landing[0]
        elif k < HALVINGS:
            before, _ = self.span(part.shape[1], k - 1)
            _, size = self.span(part.shape[1], k)
            start = pl.multiple_of(before + (1 - self.bits[k]) * size, 16)
            src, dst = part.at[mine, pl.ds(start, size)], landing[k]
        elif k < self.depth:
            src, dst = self.owned(part, HALVINGS - 1), landing[k]
        else:
            d = self.steps - 1 - k
            src = dst = self.owned(part, d)
        return pltpu.make_async_remote_copy(
            src_ref=src,
            dst_ref=dst,
            send_sem=self.send_sem.at[i, k],
            recv_sem=self.recv_sem.at[i, k],
            device_id=self.partners[d],
            device_id_type=MESH,
        )

    def begin(self, part, landing, i, k):
        if k >= self.depth:
            pl.semaphore_wait(self.credit.at[i, self.steps - 1 - k], 1)
        self.transfer(part, landing, i, k).start()

    def step(self, part, landing, i, k):
        moved = self.transfer(part, landing, i, k)
        if k < self.depth:
            moved.wait_send()
            if k < HALVINGS:
                pl.semaphore_signal(
                    self.credit.at[i, k], inc=1, device_id=self.partners[k], device_id_type=MESH
                )
        moved.wait_recv()
        if k < self.depth:
            rows = self.owned(part, min(k, HALVINGS - 1))
            rows[...] = rows[...] + landing[k][...]
        if k + 1 < self.steps:
            self.begin(part, landing, i, k + 1)

    def drain(self, part, landing, i):
        for k in range(self.depth, self.steps):
            self.transfer(part, landing, i, k).wait_send()


MAIN_SLOTS = [
    [-7, -5, -4, -2, 0, 4, 15, 25],
    [-6, -4, -2, 0, 2, 4, 6, 11],
    [-5, -2, 0, 2, 6, 9, 21, 25],
    [-4, -1, 2, 6, 10, 16, 30, 31],
    [-3, 1, 2, 4, 7, 10, 13, 16],
    [-1, 2, 5, 7, 12, 17, 23, 27],
    [1, 4, 7, 12, 16, 22, 27, 30],
]
LATE_SLOTS = [[11, 14, 17, 19, 23, 24, 27, 30], [19, 21, 26, 27, 29, 30, 31, 32]]
LAGS = [8, 6, 4, 2]
Z_FIRST = [3]


def tables(count, depth, blocks):
    if (count, depth, blocks) == (len(MAIN_SLOTS), 5, 8):
        return MAIN_SLOTS, LATE_SLOTS, LAGS
    floors = blocks // 2
    main = []
    for i in range(count):
        row = [i - count, 2 * i - count + 2]
        row += [2 * (i + k) - count for k in range(HALVINGS - 1, depth + 1)]
        main.append(row + [row[-1] + 3 + i // 2, row[-1] + 4 + i // 2])
    waits = [1, 3, 4] + list(range(5, 2 * depth - 1, 2))
    waits += [waits[-1] + 1, waits[-1] + 3, waits[-1] + 4]
    late = [[g * blocks + blocks + 1 + w for w in waits] for g in range(KVH - 1)]
    return main, late, [2 * (floors - z) for z in range(floors)]


def rounds(slots, first, last):
    lists = []
    for i, n in slots:
        if first <= n < last:
            for chosen in lists:
                if all(n != other for _, other in chosen):
                    chosen.append((i, n))
                    break
            else:
                lists.append([(i, n)])
    return lists


def at_slot(chosen, n):
    found = 0
    for i, slot in chosen:
        found = found + jnp.where(n == slot, i + 1, 0)
    return found


def cube_links(s, b, sizes):
    seqs, blocks = sizes
    links = []
    for bit in range(log2(seqs)):
        mine = (s // 2**bit) % 2
        links.append((mine, (s + 2**bit * (1 - 2 * mine), b)))
    for bit in range(log2(blocks)):
        mine = (b // 2**bit) % 2
        links.append((mine, (s, b + 2**bit * (1 - 2 * mine))))
    return links


def row_counts(rows, depth):
    return [rows >> min(k, HALVINGS - 1) for k in range(depth)]


def padded_rows(rows):
    return (rows + 63) // 64 * 64


def mega_kernel(
    sizes,
    keep_mask, keep_rate, exit_scales,
    tokens, groups, gain1, gain2, wk, wv, wq, cos, sin,
    wo_hbm, wg_hbm, wu_hbm, wd_hbm, cot_hbm,
    layer_out_hbm, input_grad_hbm, parts_hbm, tails, gains,
    layer_out, input_grad, parts,
    wo, stream, cotangent,
    queries, kv_all, attended, mixed_t, top, total,
    d_normed2, d_out,
    chain, cross,
    load_sem, stream_sem, out_sem, send_sem, recv_sem, cube_send, cube_recv, credit, tail_send, tail_recv, tail_credit,
    gain_send, gain_recv, kv_send, chain_recv, cross_recv, gain_landing,
    *landings,
):
    seqs, blocks = sizes
    s, b = lax.axis_index("seq"), lax.axis_index("blk")
    z, y, floors = b // 2, b % 2, blocks // 2
    above, below, across = (s, b + 2), (s, b - 2), (s, b + 1 - 2 * y)
    has_above, has_below = z < floors - 1, z > 0
    links = cube_links(s, b, sizes)
    cube = Cube(links, cube_send, cube_recv, credit)
    z_links = links[:1] + links[3:] + links[1:3]
    z_cube = Cube(z_links, cube_send, cube_recv, credit)
    tail_cube = Cube(links, tail_send, tail_recv, tail_credit)
    depth = cube.depth
    count = parts.shape[0]

    def main(i):
        return parts.at[i], [r.at[i] for r in landings[:depth]], i

    def late(i):
        return tails.at[i], [r.at[i] for r in landings[depth:]], i

    loads = [
        pltpu.make_async_copy(src, dst, load_sem.at[i])
        for i, (src, dst) in enumerate(
            [(wo_hbm, wo), (cot_hbm, cotangent)]
        )
    ]
    step = 2 * LANES
    chunks = wg_hbm.shape[1] // step

    def weights(f):
        at = pl.ds(pl.multiple_of(f * step, step), step)
        return [
            pltpu.make_async_copy(ref.at[:, at], stream.at[f % 2, k], stream_sem.at[f % 2, k])
            for k, ref in enumerate((wg_hbm, wu_hbm, wd_hbm))
        ]

    for load in loads + weights(0):
        load.start()

    barrier = pltpu.get_barrier_semaphore()

    def greet(device):
        pl.semaphore_signal(barrier, inc=1, device_id=device, device_id_type=MESH)

    for device in cube.partners:
        greet(device)
    odd = z % 2
    extra_below = has_below & (odd == 0)
    extra_above = has_above & (odd == 1)

    @pl.when(extra_below)
    def _():
        greet(below)

    @pl.when(extra_above)
    def _():
        greet(above)

    extra = extra_below.astype(jnp.int32) + extra_above.astype(jnp.int32)

    def copy(kind, j, g):
        return pltpu.make_async_remote_copy(
            src_ref=kv_all.at[j, g],
            dst_ref=kv_all.at[j, g],
            send_sem=send_sem.at[kind, j, g],
            recv_sem=recv_sem.at[j, g],
            device_id=above if kind == 0 else across,
            device_id_type=MESH,
        )

    def rerouted(j, g):
        return (j == 0) & (g < REROUTED)

    normed = normalize(tokens, gain1)
    c, sn = cos[...], sin[...]
    project_kv(normed, wk, wv, c, sn, kv_all.at[b])
    pl.semaphore_wait(barrier, depth + extra)

    def send_own(g, carry):
        @pl.when(has_above)
        def _():
            copy(0, b, g).start()

        @pl.when(y == 0)
        def _():
            copy(1, b, g).start()

        return carry

    lax.fori_loop(0, KVH, send_own, 0)
    project_q(normed, wq, c, sn, queries)

    def own(g, carry):
        first_unit(g, queries, kv_all[b, g], attended, top, total)
        return carry

    lax.fori_loop(0, KVH, own, 0)

    def level(m, carry):
        def one(g, inner):
            @pl.when(m <= z)
            def _():
                j = b - 2 * m
                copy(0, j, g).wait_recv()

                @pl.when(has_above)
                def _():
                    copy(0, j, g).start()

                @pl.when(jnp.logical_not(rerouted(j, g)))
                def _():
                    copy(1, j, g).start()

                next_unit(g, queries, kv_all[j, g], attended, top, total)

            @pl.when((m >= 2) | (y == 1))
            def _():
                j = b - 2 * m + 3 - 2 * y
                copy(1, j, g).wait_recv()

                @pl.when(has_above & rerouted(j, g))
                def _():
                    copy(0, j, g).start()

                next_unit(g, queries, kv_all[j, g], attended, top, total)

            return inner

        return lax.fori_loop(0, KVH, one, carry)

    lax.fori_loop(1, z + 2, level, 0)
    lse = top
    finish_forward(attended, top, total, mixed_t, lse)

    def drain_forward(m, carry):
        def one(g, inner):
            j = b - 2 * m

            @pl.when(has_above)
            def _():
                copy(0, j, g).wait_send()

            @pl.when(((m >= 1) & jnp.logical_not(rerouted(j, g))) | ((m == 0) & (y == 0)))
            def _():
                copy(1, j, g).wait_send()

            return inner

        return lax.fori_loop(0, KVH, one, carry)

    lax.fori_loop(0, z + 1, drain_forward, 0)

    @pl.when(has_above & (y == 1))
    def _():
        for g in range(REROUTED):
            copy(0, 0, g).wait_send()


    whole_head = 2 * floors + 1
    end = (KVH - 1) * blocks + whole_head + 2
    main_slots, late_slots, lags = tables(count, depth, blocks)
    lead = count + 1
    rows_of_main = list(enumerate(main_slots))
    plan = (
        (tail_cube, late, list(enumerate(late_slots))),
        (cube, main, [(i, row) for i, row in rows_of_main if i not in Z_FIRST]),
        (z_cube, main, [(i, row) for i, row in rows_of_main if i in Z_FIRST]),
    )

    def part_out(i):
        return pltpu.make_async_copy(parts.at[i], parts_hbm.at[i], out_sem.at[i])


    def serve(n, first, last):
        for k in range(cube.steps - 1, -1, -1):
            for exchange, block_of, slots in plan:
                for chosen in rounds([(i, row[k]) for i, row in slots], first, last):
                    found = at_slot(chosen, n)

                    @pl.when(found > 0)
                    def _(exchange=exchange, block_of=block_of, k=k, found=found):
                        exchange.step(*block_of(jnp.maximum(found - 1, 0)), k)

    def serve_now(n):
        for k in range(cube.steps - 1, -1, -1):
            for exchange, block_of, slots in plan:
                for i, row in slots:
                    if row[k] == n or (n == end + cube.steps - 3 and row[k] > n):
                        exchange.step(*block_of(i), k)
                        if block_of is main and n >= end and k == cube.steps - 1:
                            part_out(i).start()

    for load in loads:
        load.wait()
    bs = keep_mask[0].astype(F32) * keep_rate[0]
    gain = column(gain2[...])
    hidden = tokens[...].astype(F32) + bs * nn(wo[...].T, mixed_t[...])
    r2 = inverse_rms(hidden)
    normed2_t = (hidden * r2 * gain).astype(BF16)
    normed2 = normed2_t.T

    def seed():
        by_group = jnp.where(groups[...] == 1, exit_scales[1], exit_scales[0])
        return cotangent[...].astype(F32) * by_group

    d_down_t = (bs * seed()).astype(BF16)
    d_down = d_down_t.T
    width, rows = hidden.shape
    for i in range(count):
        filled = 3 * width if i < chunks else 5 * width // 2
        for half in range(2 if filled < parts.shape[2] else 0):
            parts[i, half, filled:] = jnp.zeros((parts.shape[2] - filled, LANES), BF16)
    down = d_hidden = input_grad
    down[...] = jnp.zeros_like(down)
    d_normed2[...] = jnp.zeros_like(d_normed2)

    def chunk(f, carry):
        for load in weights(f):
            load.wait()

        @pl.when(f + 1 < chunks)
        def _():
            for load in weights(f + 1):
                load.start()

        wg, wu, wd = (stream.at[f % 2, k] for k in range(3))
        gate = nn(normed2, wg[...])
        up = nn(normed2, wu[...])
        d_act = nn(d_down, wd[...])
        sig = 1.0 / (1.0 + jnp.exp(-gate))
        silu = gate * sig
        act = (silu * up).astype(BF16)
        d_gate = (d_act * up * (sig + silu * (1.0 - sig))).astype(BF16)
        d_up = (d_act * silu).astype(BF16)
        grads = (nn(normed2_t, d_gate), nn(normed2_t, d_up), nn(d_down_t, act))
        for k, value in enumerate(grads):
            for half in range(2):
                parts[f, half, k * width : (k + 1) * width] = value[
                    :, half * LANES : (half + 1) * LANES
                ].astype(BF16)
        down[...] += nt(wd[...], act)
        d_normed2[...] += nt(wg[...], d_gate) + nt(wu[...], d_up)
        cube.begin(*main(f), 0)
        serve(f - lead, -lead, -2)
        return carry

    lax.fori_loop(0, chunks, chunk, 0)
    layer_out[...] = (hidden + bs * down[...]).astype(BF16)
    whole_out = pltpu.make_async_copy(layer_out, layer_out_hbm, out_sem.at[count])
    whole_out.start()
    dn = d_normed2[...]
    gain2_grad = jnp.sum(dn * hidden * r2, axis=1, keepdims=True)
    gained = gain * dn
    dh = seed() + r2 * gained - hidden * (r2 * r2 * r2) * jnp.mean(gained * hidden, axis=0, keepdims=True)
    d_hidden[...] = dh
    d_branch = (bs * dh).astype(BF16)
    out_grad = nt(mixed_t[...], d_branch)
    half_rows = width // 2
    last = parts.at[chunks]
    last[0, :width] = out_grad[:, :LANES].astype(BF16)
    last[0, width : 2 * width] = out_grad[:, LANES : 2 * LANES].astype(BF16)
    middle = out_grad[:, 2 * LANES : 3 * LANES].astype(BF16)
    last[0, 2 * width : 2 * width + half_rows] = middle[:half_rows]
    last[1, :half_rows] = middle[half_rows:]
    last[1, half_rows : half_rows + width] = out_grad[:, 3 * LANES : 4 * LANES].astype(BF16)
    last[1, half_rows + width : half_rows + 2 * width] = last_block(out_grad)
    cube.begin(*main(chunks), 0)
    serve_now(-2)
    d_mixed = nn(wo[...], d_branch).astype(BF16)
    delta = total
    for h in range(H):
        g, r = h // GROUP, h % GROUP
        head = d_mixed[h * HD : (h + 1) * HD]
        d_out[h * PAIR : h * PAIR + HD] = jnp.zeros((HD, rows), BF16)
        d_out[h * PAIR + HD : (h + 1) * PAIR] = head
        delta[g, r] = jnp.sum(head.astype(F32) * attended[g, r], axis=0, keepdims=True)
    dq = attended
    dq[...] = jnp.zeros_like(dq)
    normed_kept = mixed_t
    normed_kept[...] = normalize(tokens, gain1)
    serve_now(-1)

    def kv_down(j, g):
        return pltpu.make_async_remote_copy(
            src_ref=kv_all.at[j, g],
            dst_ref=chain.at[j // 2, g],
            send_sem=kv_send.at[j, g],
            recv_sem=chain_recv.at[j // 2, g],
            device_id=below,
            device_id_type=MESH,
        )

    def kv_across(j, g):
        return pltpu.make_async_remote_copy(
            src_ref=kv_all.at[j, g],
            dst_ref=cross.at[j // 2, g],
            send_sem=kv_send.at[j, g],
            recv_sem=cross_recv.at[j // 2, g],
            device_id=across,
            device_id_type=MESH,
        )

    d_kv = d_normed2
    lag = lags[0]
    for i in range(1, floors):
        lag = jnp.where(z == i, lags[i], lag)
    nq, nk = H * HD, KVH * HD
    span = GROUP * PAIR

    def finish_head(g):
        at = pl.multiple_of(g * span, PAIR)
        c, sn = cos[...], -sin[...]
        for r in range(GROUP):
            piece = turn(dq[g, r] * HD**-0.5, c, sn)
            d_out[pl.ds(at + r * HD, HD)] = piece.astype(BF16)
        pair = d_kv[pl.ds(pl.multiple_of(g * PAIR, PAIR), PAIR)]
        d_out[pl.ds(at + GROUP * HD, HD)] = turn(pair[:HD], c, sn).astype(BF16)
        d_out[pl.ds(at + (GROUP + 1) * HD, HD)] = pair[HD:].astype(BF16)
        high = (GROUP + 2) * HD
        grad = nt(d_out[pl.ds(at, high)], normed_kept[...]).astype(BF16)
        tails[g, 0, :high] = grad[:, :LANES]
        tails[g, 0, high : 2 * high] = grad[:, LANES : 2 * LANES]
        tails[g, 0, 2 * high : 5 * high // 2] = grad[: high // 2, 2 * LANES : 3 * LANES]
        tails[g, 1, : high // 2] = grad[high // 2 :, 2 * LANES : 3 * LANES]
        tails[g, 1, high // 2 : 3 * high // 2] = grad[:, 3 * LANES : 4 * LANES]
        tails[g, 1, 3 * high // 2 : 5 * high // 2] = jnp.concatenate(
            [grad[:, 4 * LANES :], jnp.zeros((high, HD), BF16)], axis=1
        )
        for half in range(2):
            rest = tails.shape[2] - 5 * high // 2
            tails[g, half, 5 * high // 2 :] = jnp.zeros((rest, LANES), BF16)
        tail_cube.begin(*late(g), 0)

    def slot(n, carry):
        g, j = n // blocks, n % blocks
        busy = n < KVH * blocks

        def unit(masked):
            d_keys, d_vals = grad_unit(g, queries, d_out, lse, delta, kv_all[j, g], dq, masked)
            kv_all[j, g, :HD] = d_keys.astype(BF16)
            kv_all[j, g, HD:] = d_vals.astype(BF16)

        @pl.when(busy & (j < b))
        def _():
            unit(False)

        @pl.when(busy & (j == b))
        def _():
            unit(True)

        @pl.when(busy & (j <= b) & (j % 2 != y))
        def _():
            kv_across(j, g).start()

        ready = n - lag
        at = jnp.maximum(ready, 0)
        gg, jj = at // blocks, at % blocks
        due = (ready >= 0) & (ready < KVH * blocks) & (jj % 2 == y)
        rows_of = pl.ds(pl.multiple_of(jnp.minimum(gg, KVH - 1) * PAIR, PAIR), PAIR)

        @pl.when(due & (jj < b))
        def _():
            kv_across(jj, gg).wait_recv()
            both = kv_all[jj, gg].astype(F32) + cross[jj // 2, gg].astype(F32)

            @pl.when(has_above)
            def _():
                kv_down(jj, gg).wait_recv()
                kv_all[jj, gg] = (both + chain[jj // 2, gg].astype(F32)).astype(BF16)

            @pl.when(jnp.logical_not(has_above))
            def _():
                kv_all[jj, gg] = both.astype(BF16)

            kv_down(jj, gg).start()

        @pl.when(due & (jj == b))
        def _():
            d_kv[rows_of] = kv_all[jj, gg].astype(F32)

            @pl.when(y == 0)
            def _():
                kv_across(jj, gg).wait_recv()
                d_kv[rows_of] = d_kv[rows_of] + cross[jj // 2, gg].astype(F32)

            @pl.when(has_above)
            def _():
                kv_down(jj, gg).wait_recv()
                d_kv[rows_of] = d_kv[rows_of] + chain[jj // 2, gg].astype(F32)

        settled = n - whole_head

        @pl.when((settled >= 0) & (settled % blocks == 0) & (settled // blocks < KVH))
        def _():
            finish_head(settled // blocks)

        serve(n, 0, end)

        @pl.when(n == end - 1)
        def _():
            tail_cube.step(*late(KVH - 1), 0)

        return carry

    lax.fori_loop(0, end, slot, 0)

    def drain_backward(n, carry):
        j, g = n // KVH, n % KVH

        @pl.when(j % 2 != y)
        def _():
            kv_across(j, g).wait_send()

        @pl.when((j % 2 == y) & (j < b))
        def _():
            kv_down(j, g).wait_send()

        return carry

    lax.fori_loop(0, KVH * (b + 1), drain_backward, 0)

    x = tokens[...].astype(F32)
    r1 = inverse_rms(x)
    weight = column(gain1[...])
    d_normed = jnp.zeros_like(x)
    for g in range(KVH):
        first = g * span
        middle, last_row = first + GROUP * HD, first + (GROUP + 1) * HD
        heads = slice(g * GROUP * HD, (g + 1) * GROUP * HD)
        own_head = slice(g * HD, (g + 1) * HD)
        d_normed = (
            d_normed
            + nn(wq[:, heads], d_out[first:middle])
            + nn(wk[own_head].T, d_out[middle:last_row])
            + nn(wv[own_head].T, d_out[last_row : last_row + HD])
        )
    pads = jnp.zeros((1, gains.shape[1] - width), F32)
    for i, values in enumerate((jnp.sum(d_normed * x * r1, axis=1, keepdims=True), gain2_grad)):
        gains[i : i + 1] = jnp.concatenate([as_row(values), pads], axis=1)
    gains[2:] = jnp.zeros((gains.shape[0] - 2, gains.shape[1]), F32)

    def gain_swap(d):
        return pltpu.make_async_remote_copy(
            src_ref=gains,
            dst_ref=gain_landing.at[d],
            send_sem=gain_send.at[d],
            recv_sem=gain_recv.at[d],
            device_id=cube.partners[d],
            device_id_type=MESH,
        )

    gain_swap(0).start()
    for i, row in rows_of_main:
        if row[-1] < end:
            part_out(i).start()
    tail_cube.step(*late(KVH - 1), 1)
    gained = weight * d_normed
    input_grad[...] = (
        d_hidden[...] + r1 * gained - x * (r1 * r1 * r1) * jnp.mean(gained * x, axis=0, keepdims=True)
    )
    grad_out = pltpu.make_async_copy(input_grad, input_grad_hbm, out_sem.at[count + 1])
    grad_out.start()
    for k in range(2, cube.steps):
        serve_now(end + k - 2)
        if k - 2 < depth:
            gain_swap(k - 2).wait()
            gains[...] = gains[...] + gain_landing[k - 2]
            if k - 1 < depth:
                gain_swap(k - 1).start()
        tail_cube.step(*late(KVH - 1), k)
    for i in range(count):
        (z_cube if i in Z_FIRST else cube).drain(*main(i))
        part_out(i).wait()
    whole_out.wait()
    grad_out.wait()
    for i in range(KVH):
        tail_cube.drain(*late(i))


def unpack_kernel(
    chunks, parts, tails, gains, late_out, late_grad,
    gate, up, down, output_hbm, query_hbm, key_hbm, value_hbm, gain1, gain2, layer_out, input_grad,
    output, query, key, value, sems,
):
    i = pl.program_id(0)
    width = gate.shape[0]
    layer_out[...] = late_out[...]
    input_grad[...] = late_grad[...]
    small = ((output, output_hbm), (query, query_hbm), (key, key_hbm), (value, value_hbm))
    copies = [pltpu.make_async_copy(a, b, sems.at[n]) for n, (a, b) in enumerate(small)]

    @pl.when(i > 0)
    def _():
        for k, out in enumerate((gate, up, down)):
            for half in range(2):
                piece = parts[0, half, k * width : (k + 1) * width]
                out[:, half * LANES : (half + 1) * LANES] = piece.astype(F32)

    def five(ref, at, rows):
        half = rows // 2
        yield ref[at + (0, slice(0, rows))]
        yield ref[at + (0, slice(rows, 2 * rows))]
        yield jnp.concatenate(
            [ref[at + (0, slice(2 * rows, 2 * rows + half))], ref[at + (1, slice(0, half))]], axis=0
        )
        yield ref[at + (1, slice(half, half + rows))]
        yield ref[at + (1, slice(half + rows, half + 2 * rows))]

    @pl.when(i == 0)
    def _():
        for k, block in enumerate(five(parts, (0,), width)):
            size = min(LANES, width - k * LANES)
            output[:, k * LANES : k * LANES + size] = block.astype(F32)[:, :size]
        high = GROUP * HD
        for k in range(5):
            size = min(LANES, width - k * LANES)
            lanes = slice(k * LANES, k * LANES + size)
            columns = []
            for g in range(KVH):
                block = list(five(tails, (g,), high + PAIR))[k].astype(F32)[:, :size]
                own = slice(g * HD, (g + 1) * HD)
                key[own, lanes] = block[high : high + HD]
                value[own, lanes] = block[high + HD :]
                columns.append(block[:high])
            query[lanes, :] = jnp.concatenate(columns, axis=0).T
        gain1[...] = gains[0, :width]
        gain2[...] = gains[1, :width]
        for copy in copies:
            copy.start()

    @pl.when(i == chunks)
    def _():
        for copy in copies:
            copy.wait()


def last_block(grad):
    return jnp.concatenate(
        [grad[:, 4 * LANES :], jnp.zeros((grad.shape[0], LANES - HD), F32)], axis=1
    ).astype(BF16)


def body(sizes, tokens, positions, groups, keep_mask, exit_scales, keep_rate, wq, wk, wv, wo, wg, wu, wd, gain1, gain2, cotangent):
    seqs, blocks = sizes
    depth = log2(seqs) + log2(blocks)
    tokens, cotangent = tokens[0].T, cotangent[0].T
    wk, wv, wd = wk.T, wv.T, wd.T
    width, rows = tokens.shape
    ff = wg.shape[1]
    nq, nk = H * HD, KVH * HD
    frequency = 1.0 / ROPE_BASE ** (jnp.arange(HALF, dtype=F32) * (2.0 / HD))
    angle = frequency[:, None] * positions[0].astype(F32)[None, :]
    cos, sin = jnp.cos(angle), jnp.sin(angle)

    chunks = ff // (2 * LANES)
    count = chunks + 1
    part_rows = padded_rows(3 * width)
    tail_rows = padded_rows(5 * (GROUP + 2) * HD // 2)
    gain_shape = (8, 5 * LANES)
    vmem, smem, hbm = (pl.BlockSpec(memory_space=m) for m in (pltpu.VMEM, pltpu.SMEM, pl.ANY))
    head_t = (KVH, GROUP, PAIR, rows)
    head_o = (KVH, GROUP, HD, rows)
    head_1 = (KVH, GROUP, 1, rows)
    dma = pltpu.SemaphoreType.DMA
    scratch = [
        pltpu.VMEM((width, rows), BF16),
        pltpu.VMEM((width, rows), F32),
        pltpu.VMEM((count, 2, part_rows, LANES), BF16),
        pltpu.VMEM(wo.shape, BF16),
        pltpu.VMEM((2, 3, width, 2 * LANES), BF16),
        pltpu.VMEM(cotangent.shape, BF16),
        pltpu.VMEM(head_t, BF16),
        pltpu.VMEM((blocks, KVH, PAIR, rows), BF16),
        pltpu.VMEM(head_o, F32),
        pltpu.VMEM((nq, rows), BF16),
        pltpu.VMEM(head_1, F32),
        pltpu.VMEM(head_1, F32),
        pltpu.VMEM((width, rows), F32),
        pltpu.VMEM((H * PAIR, rows), BF16),
        pltpu.VMEM((blocks // 2, KVH, PAIR, rows), BF16),
        pltpu.VMEM((blocks // 2, KVH, PAIR, rows), BF16),
        dma((2,)),
        dma((2, 3)),
        dma((count + 2,)),
        dma((2, blocks, KVH)),
        dma((blocks, KVH)),
        dma((count, depth + HALVINGS)),
        dma((count, depth + HALVINGS)),
        pltpu.SemaphoreType.REGULAR((count, HALVINGS)),
        dma((KVH, depth + HALVINGS)),
        dma((KVH, depth + HALVINGS)),
        pltpu.SemaphoreType.REGULAR((KVH, HALVINGS)),
        dma((depth,)),
        dma((depth,)),
        dma((blocks, KVH)),
        dma((blocks // 2, KVH)),
        dma((blocks // 2, KVH)),
    ]
    scratch += [pltpu.VMEM((depth,) + gain_shape, F32)]
    scratch += [pltpu.VMEM((count, n, LANES), BF16) for n in row_counts(part_rows, depth)]
    scratch += [pltpu.VMEM((KVH, n, LANES), BF16) for n in row_counts(tail_rows, depth)]
    layer_out, input_grad, parts, tails, gains = pl.pallas_call(
        functools.partial(mega_kernel, sizes),
        out_shape=[
            jax.ShapeDtypeStruct((width, rows), BF16),
            jax.ShapeDtypeStruct((width, rows), F32),
            jax.ShapeDtypeStruct((count, 2, part_rows, LANES), BF16),
            jax.ShapeDtypeStruct((KVH, 2, tail_rows, LANES), BF16),
            jax.ShapeDtypeStruct(gain_shape, F32),
        ],
        in_specs=[smem] * 3 + [vmem] * 9 + [hbm] * 5,
        out_specs=[hbm] * 3 + [vmem] * 2,
        scratch_shapes=scratch,
        compiler_params=pltpu.CompilerParams(
            vmem_limit_bytes=VMEM_LIMIT, collective_id=0, has_side_effects=True
        ),
    )(
        keep_mask, keep_rate, exit_scales,
        tokens, groups, gain1, gain2, wk, wv, wq, cos, sin,
        wo, wg, wu, wd, cotangent,
    )

    wide = pl.BlockSpec((width, 2 * LANES), lambda i: (0, jnp.maximum(i - 1, 0)))
    lines = pl.BlockSpec((width // chunks, rows), lambda i: (jnp.maximum(i - 1, 0), 0))
    line = pl.BlockSpec((width,), lambda i: (0,))
    small = [(nq, width), (width, nq), (nk, width), (nk, width)]
    (gate_grad, up_grad, down_grad, output_grad, query_grad, key_grad, value_grad, gain1_grad, gain2_grad, layer_out, input_grad) = pl.pallas_call(
        functools.partial(unpack_kernel, chunks),
        grid=(count,),
        out_shape=[jax.ShapeDtypeStruct((width, ff), F32)] * 3
        + [jax.ShapeDtypeStruct(shape, F32) for shape in small + [(width,), (width,)]]
        + [jax.ShapeDtypeStruct((width, rows), t) for t in (BF16, F32)],
        in_specs=[
            pl.BlockSpec((1, 2, part_rows, LANES), lambda i: ((i + chunks) % count, 0, 0, 0)),
            pl.BlockSpec(tails.shape, lambda i: (0,) * 4),
            pl.BlockSpec(gain_shape, lambda i: (0, 0)),
            lines,
            lines,
        ],
        out_specs=[wide] * 3 + [hbm] * 4 + [line] * 2 + [lines] * 2,
        scratch_shapes=[pltpu.VMEM(shape, F32) for shape in small] + [dma((4,))],
        compiler_params=pltpu.CompilerParams(vmem_limit_bytes=VMEM_LIMIT),
    )(parts, tails, gains, layer_out, input_grad)
    return (
        layer_out.T[None],
        input_grad.T[None],
        query_grad,
        key_grad.T,
        value_grad.T,
        output_grad,
        gate_grad,
        up_grad,
        down_grad.T,
        gain1_grad,
        gain2_grad,
    )


def solution(mesh):
    local = P("seq", "blk", None)
    pair = P("seq", "blk")
    placed = (local, pair, pair, P("seq")) + (P(),) * 11 + (local,)
    return jax.shard_map(
        functools.partial(body, (mesh.shape["seq"], mesh.shape["blk"])),
        mesh=mesh,
        in_specs=placed,
        out_specs=(local, local) + (P(),) * 9,
        check_vma=False,
    )
```

```python
import functools

import jax
import jax.numpy as jnp
from jax import lax
from jax.experimental import pallas as pl
from jax.experimental.pallas import tpu as pltpu
from jax.sharding import PartitionSpec as P

H = 9
KVH = 3
HD = 64
GROUP = H // KVH
HALF = HD // 2
PAIR = 2 * HD

EPSILON = 1e-05
ROPE_BASE = 100000.0
MASKED = -1e30
LOG2E = 1.4426950408889634
LN2 = 0.6931471805599453
F32 = jnp.float32
BF16 = jnp.bfloat16
VMEM_LIMIT = 61 * 1024 * 1024
MESH = pl.DeviceIdType.MESH
LANES = 128
REROUTED = 2


def nn(a, b):
    return lax.dot_general(a, b, (((1,), (0,)), ((), ())), preferred_element_type=F32)


def nt(a, b):
    return lax.dot_general(a, b, (((1,), (1,)), ((), ())), preferred_element_type=F32)


def column(values):
    return jnp.broadcast_to(values[None, :], (8, values.shape[0])).T[:, :1]


def as_row(values):
    return jnp.broadcast_to(values, (values.shape[0], 8)).T[:1]


def inverse_rms(values):
    return lax.rsqrt(jnp.mean(values * values, axis=0, keepdims=True) + EPSILON)


def turn(rows, cos, sin):
    u, w = rows[:HALF], rows[HALF:]
    return jnp.concatenate([u * cos - w * sin, w * cos + u * sin], axis=0)


def normalize(tokens, gain):
    x = tokens[...].astype(F32)
    return (x * inverse_rms(x) * column(gain[...])).astype(BF16)


def project_kv(normed, wk, wv, cos, sin, kv):
    keys = nn(wk[...], normed)
    vals = nn(wv[...], normed)
    for g in range(KVH):
        span = slice(g * HD, (g + 1) * HD)
        kv[g, :HD, :] = turn(keys[span], cos, sin).astype(BF16)
        kv[g, HD:, :] = vals[span].astype(BF16)


def project_q(normed, wq, cos, sin, queries):
    raw = nn(wq[...].T, normed)
    factor = HD**-0.5 * LOG2E
    for h in range(H):
        turned = turn(raw[h * HD : (h + 1) * HD], cos, sin) * factor
        queries[h // GROUP, h % GROUP, :HD, :] = turned.astype(BF16)
        queries[h // GROUP, h % GROUP, HD:, :] = jnp.zeros((HD, raw.shape[1]), BF16)


def values_and_ones(packed):
    ones = jnp.ones((16, packed.shape[1]), BF16)
    return jnp.concatenate([packed[HD:], ones], axis=0)


def first_unit(g, queries, packed, out, top, total):
    rows = queries.shape[-1]
    part = rows // 2
    natural = packed.T
    values = values_and_ones(packed)
    items = [(r, c) for r in range(GROUP) for c in range(2)]

    def scores_of(i):
        r, c = items[i]
        return nn(natural[: (c + 1) * part], queries[g, r, :, c * part : (c + 1) * part])

    scores = scores_of(0)
    done = []
    for i, (r, c) in enumerate(items):
        later = scores_of(i + 1) if i + 1 < len(items) else None
        key_at = lax.broadcasted_iota(jnp.int32, scores.shape, 0)
        query_at = lax.broadcasted_iota(jnp.int32, scores.shape, 1) + c * part
        scores = jnp.where(key_at <= query_at, scores, MASKED)
        high = jnp.max(scores, axis=0, keepdims=True)
        probs = jnp.exp2(scores - high)
        done.append((high, nn(values[:, : (c + 1) * part], probs.astype(BF16))))
        scores = later
    for (r, c), (high, summed) in zip(items, done):
        cols = slice(c * part, (c + 1) * part)
        top[g, r, :, cols] = high
        total[g, r, :, cols] = summed[HD : HD + 1]
        out[g, r, :, cols] = summed[:HD]


def next_unit(g, queries, packed, out, top, total):
    natural = packed.T
    values = values_and_ones(packed)
    before = [(top[g, r], total[g, r], out[g, r]) for r in range(GROUP)]
    scores = [nn(natural, queries[g, r]) for r in range(2)]
    done = []
    for r in range(GROUP):
        if r + 2 < GROUP:
            scores.append(nn(natural, queries[g, r + 2]))
        old, count, acc = before[r]
        high = jnp.maximum(old, jnp.max(scores[r], axis=0, keepdims=True))
        probs = jnp.exp2(scores[r] - high)
        fade = jnp.exp2(old - high)
        summed = nn(values, probs.astype(BF16))
        done.append((high, count * fade + summed[HD : HD + 1], acc * fade + summed[:HD]))
    for r, (high, count, acc) in enumerate(done):
        top[g, r] = high
        total[g, r] = count
        out[g, r] = acc


def finish_forward(out, top, total, mixed_t, lse):
    for h in range(H):
        g, r = h // GROUP, h % GROUP
        scaled = out[g, r] * (1.0 / total[g, r])
        out[g, r] = scaled
        mixed_t[h * HD : (h + 1) * HD, :] = scaled.astype(BF16)
        lse[g, r] = top[g, r] + jnp.log2(total[g, r])


def grad_unit(g, queries, d_out, lse, delta, packed, dq, masked):
    rows = queries.shape[-1]
    part = rows // 2
    natural = packed.T
    items = [(r, c) for r in range(GROUP) for c in range(2)]
    columns = [slice(c * part, (c + 1) * part) for c in range(2)]
    before = [dq[g, r, :, columns[c]] for r, c in items]

    def seen(c):
        return (c + 1) * part if masked else rows

    def d_head(r, c, first=0):
        start = pl.multiple_of((g * GROUP + r) * PAIR + first, HD)
        return d_out[pl.ds(start, PAIR - first), columns[c]]

    def products(r, c):
        keys = natural[: seen(c)]
        return nn(keys, queries[g, r, :, columns[c]]), nn(keys, d_head(r, c))

    ahead = products(*items[0])
    done = []
    totals = [None] * 4
    for i, (r, c) in enumerate(items):
        scores, d_probs = ahead
        if i + 1 < len(items):
            ahead = products(*items[i + 1])
        probs = jnp.exp2(scores - lse[g, r, :, columns[c]])
        if masked:
            key_at = lax.broadcasted_iota(jnp.int32, scores.shape, 0)
            query_at = lax.broadcasted_iota(jnp.int32, scores.shape, 1) + c * part
            probs = jnp.where(key_at <= query_at, probs, 0.0)
        d_scores = (probs * (d_probs - delta[g, r, :, columns[c]])).astype(BF16)
        terms = (
            nt(d_head(r, c, HD), probs.astype(BF16)),
            nt(queries[g, r, :HD, columns[c]], d_scores),
        )
        kind = c if masked else 0
        for n, term in enumerate(terms):
            at = 2 * kind + n
            totals[at] = term if totals[at] is None else totals[at] + term
        done.append(before[i] + nn(packed[:HD, : seen(c)], d_scores))
    for i, (r, c) in enumerate(items):
        dq[g, r, :, columns[c]] = done[i]
    d_vals, d_keys = totals[:2]
    if masked:
        rest = jnp.zeros((HD, rows - part), F32)
        d_vals = totals[2] + jnp.concatenate([d_vals, rest], axis=1)
        d_keys = totals[3] + jnp.concatenate([d_keys, rest], axis=1)
    return d_keys * LN2, d_vals


def log2(n):
    return n.bit_length() - 1


HALVINGS = 3


class Cube:
    def __init__(self, links, send_sem, recv_sem, credit):
        self.send_sem, self.recv_sem, self.credit = send_sem, recv_sem, credit
        self.bits = [bit for bit, _ in links]
        self.partners = [partner for _, partner in links]
        self.depth = len(links)
        self.steps = self.depth + HALVINGS

    def span(self, rows, d):
        lo, size = 0, rows
        for e in range(1, d + 1):
            size = size // 2
            lo = lo + self.bits[e] * size
        return lo, size

    def owned(self, part, d):
        lo, size = self.span(part.shape[1], d)
        return part.at[self.bits[0], pl.ds(pl.multiple_of(lo, 16), size)]

    def transfer(self, part, landing, i, k):
        mine, d = self.bits[0], k
        if k == 0:
            src, dst = part.at[1 - mine], landing[0]
        elif k < HALVINGS:
            before, _ = self.span(part.shape[1], k - 1)
            _, size = self.span(part.shape[1], k)
            start = pl.multiple_of(before + (1 - self.bits[k]) * size, 16)
            src, dst = part.at[mine, pl.ds(start, size)], landing[k]
        elif k < self.depth:
            src, dst = self.owned(part, HALVINGS - 1), landing[k]
        else:
            d = self.steps - 1 - k
            src = dst = self.owned(part, d)
        return pltpu.make_async_remote_copy(
            src_ref=src,
            dst_ref=dst,
            send_sem=self.send_sem.at[i, k],
            recv_sem=self.recv_sem.at[i, k],
            device_id=self.partners[d],
            device_id_type=MESH,
        )

    def begin(self, part, landing, i, k):
        if k >= self.depth:
            pl.semaphore_wait(self.credit.at[i, self.steps - 1 - k], 1)
        self.transfer(part, landing, i, k).start()

    def step(self, part, landing, i, k):
        moved = self.transfer(part, landing, i, k)
        if k < self.depth:
            moved.wait_send()
            if k < HALVINGS:
                pl.semaphore_signal(
                    self.credit.at[i, k], inc=1, device_id=self.partners[k], device_id_type=MESH
                )
        moved.wait_recv()
        if k < self.depth:
            rows = self.owned(part, min(k, HALVINGS - 1))
            rows[...] = rows[...] + landing[k][...]
        if k + 1 < self.steps:
            self.begin(part, landing, i, k + 1)

    def drain(self, part, landing, i):
        for k in range(self.depth, self.steps):
            self.transfer(part, landing, i, k).wait_send()


MAIN_SLOTS = [
    [-7, -5, -4, -2, 0, 7, 22, 28],
    [-6, -4, -2, 0, 2, 3, 7, 25],
    [-5, -2, 0, 2, 7, 10, 31, 32],
    [-4, -1, 2, 6, 10, 16, 25, 32],
    [-3, 1, 2, 4, 9, 12, 23, 25],
    [-1, 2, 4, 7, 14, 18, 25, 30],
    [1, 3, 6, 11, 18, 22, 27, 29],
]
LATE_SLOTS = [[12, 14, 17, 19, 23, 24, 27, 31], [21, 23, 26, 27, 29, 30, 31, 32]]
LAGS = [8, 6, 4, 2]
Z_FIRST = [3]


def tables(count, depth, blocks):
    if (count, depth, blocks) == (len(MAIN_SLOTS), 5, 8):
        return MAIN_SLOTS, LATE_SLOTS, LAGS
    floors = blocks // 2
    main = []
    for i in range(count):
        row = [i - count, 2 * i - count + 2]
        row += [2 * (i + k) - count for k in range(HALVINGS - 1, depth + 1)]
        main.append(row + [row[-1] + 3 + i // 2, row[-1] + 4 + i // 2])
    waits = [1, 3, 4] + list(range(5, 2 * depth - 1, 2))
    waits += [waits[-1] + 1, waits[-1] + 3, waits[-1] + 4]
    late = [[g * blocks + blocks + 1 + w for w in waits] for g in range(KVH - 1)]
    return main, late, [2 * (floors - z) for z in range(floors)]


def by_slot(n, first, last, act):
    if last - first == 1:
        act(first)
        return
    middle = (first + last) // 2
    for wanted, lo, hi in ((n < middle, first, middle), (n >= middle, middle, last)):
        pl.when(wanted)(functools.partial(by_slot, n, lo, hi, act))


def cube_links(s, b, sizes):
    seqs, blocks = sizes
    links = []
    for bit in range(log2(seqs)):
        mine = (s // 2**bit) % 2
        links.append((mine, (s + 2**bit * (1 - 2 * mine), b)))
    for bit in range(log2(blocks)):
        mine = (b // 2**bit) % 2
        links.append((mine, (s, b + 2**bit * (1 - 2 * mine))))
    return links


def row_counts(rows, depth):
    return [rows >> min(k, HALVINGS - 1) for k in range(depth)]


def padded_rows(rows):
    return (rows + 63) // 64 * 64


def mega_kernel(
    sizes,
    keep_mask, keep_rate, exit_scales,
    tokens, groups, gain1, gain2, wk, wv, wq, cos, sin,
    wo_hbm, wg_hbm, wu_hbm, wd_hbm, cot_hbm,
    layer_out_hbm, input_grad_hbm, parts_hbm, tails, gains,
    layer_out, input_grad, parts,
    wo, stream, cotangent,
    queries, kv_all, attended, mixed_t, top, total,
    d_normed2, d_out,
    chain, cross,
    load_sem, stream_sem, out_sem, send_sem, recv_sem, cube_send, cube_recv, credit, tail_send, tail_recv, tail_credit,
    gain_send, gain_recv, kv_send, chain_recv, cross_recv, gain_landing,
    *landings,
):
    seqs, blocks = sizes
    s, b = lax.axis_index("seq"), lax.axis_index("blk")
    z, y, floors = b // 2, b % 2, blocks // 2
    above, below, across = (s, b + 2), (s, b - 2), (s, b + 1 - 2 * y)
    has_above, has_below = z < floors - 1, z > 0
    links = cube_links(s, b, sizes)
    cube = Cube(links, cube_send, cube_recv, credit)
    z_links = links[:1] + links[3:] + links[1:3]
    z_cube = Cube(z_links, cube_send, cube_recv, credit)
    tail_cube = Cube(links, tail_send, tail_recv, tail_credit)
    depth = cube.depth
    count = parts.shape[0]

    def main(i):
        return parts.at[i], [r.at[i] for r in landings[:depth]], i

    def late(i):
        return tails.at[i], [r.at[i] for r in landings[depth:]], i

    loads = [
        pltpu.make_async_copy(src, dst, load_sem.at[i])
        for i, (src, dst) in enumerate(
            [(wo_hbm, wo), (cot_hbm, cotangent)]
        )
    ]
    step = 2 * LANES
    chunks = wg_hbm.shape[1] // step

    def weights(f):
        at = pl.ds(pl.multiple_of(f * step, step), step)
        return [
            pltpu.make_async_copy(ref.at[:, at], stream.at[f % 2, k], stream_sem.at[f % 2, k])
            for k, ref in enumerate((wg_hbm, wu_hbm, wd_hbm))
        ]

    for load in loads + weights(0):
        load.start()

    barrier = pltpu.get_barrier_semaphore()

    def greet(device):
        pl.semaphore_signal(barrier, inc=1, device_id=device, device_id_type=MESH)

    for device in cube.partners:
        greet(device)
    odd = z % 2
    extra_below = has_below & (odd == 0)
    extra_above = has_above & (odd == 1)

    @pl.when(extra_below)
    def _():
        greet(below)

    @pl.when(extra_above)
    def _():
        greet(above)

    extra = extra_below.astype(jnp.int32) + extra_above.astype(jnp.int32)

    def copy(kind, j, g):
        return pltpu.make_async_remote_copy(
            src_ref=kv_all.at[j, g],
            dst_ref=kv_all.at[j, g],
            send_sem=send_sem.at[kind, j, g],
            recv_sem=recv_sem.at[j, g],
            device_id=above if kind == 0 else across,
            device_id_type=MESH,
        )

    def rerouted(j, g):
        return (j == 0) & (g < REROUTED)

    normed = normalize(tokens, gain1)
    c, sn = cos[...], sin[...]
    project_kv(normed, wk, wv, c, sn, kv_all.at[b])
    pl.semaphore_wait(barrier, depth + extra)

    def send_own(g, carry):
        @pl.when(has_above)
        def _():
            copy(0, b, g).start()

        @pl.when(y == 0)
        def _():
            copy(1, b, g).start()

        return carry

    lax.fori_loop(0, KVH, send_own, 0)
    project_q(normed, wq, c, sn, queries)

    def own(g, carry):
        first_unit(g, queries, kv_all[b, g], attended, top, total)
        return carry

    lax.fori_loop(0, KVH, own, 0)

    def level(m, carry):
        def one(g, inner):
            @pl.when(m <= z)
            def _():
                j = b - 2 * m
                copy(0, j, g).wait_recv()

                @pl.when(has_above)
                def _():
                    copy(0, j, g).start()

                @pl.when(jnp.logical_not(rerouted(j, g)))
                def _():
                    copy(1, j, g).start()

                next_unit(g, queries, kv_all[j, g], attended, top, total)

            @pl.when((m >= 2) | (y == 1))
            def _():
                j = b - 2 * m + 3 - 2 * y
                copy(1, j, g).wait_recv()

                @pl.when(has_above & rerouted(j, g))
                def _():
                    copy(0, j, g).start()

                next_unit(g, queries, kv_all[j, g], attended, top, total)

            return inner

        return lax.fori_loop(0, KVH, one, carry)

    lax.fori_loop(1, z + 2, level, 0)
    lse = top
    finish_forward(attended, top, total, mixed_t, lse)

    def drain_forward(m, carry):
        def one(g, inner):
            j = b - 2 * m

            @pl.when(has_above)
            def _():
                copy(0, j, g).wait_send()

            @pl.when(((m >= 1) & jnp.logical_not(rerouted(j, g))) | ((m == 0) & (y == 0)))
            def _():
                copy(1, j, g).wait_send()

            return inner

        return lax.fori_loop(0, KVH, one, carry)

    lax.fori_loop(0, z + 1, drain_forward, 0)

    @pl.when(has_above & (y == 1))
    def _():
        for g in range(REROUTED):
            copy(0, 0, g).wait_send()


    whole_head = 2 * floors + 1
    end = (KVH - 1) * blocks + whole_head + 2
    main_slots, late_slots, lags = tables(count, depth, blocks)
    lead = count + 1
    rows_of_main = list(enumerate(main_slots))
    plan = (
        (tail_cube, late, list(enumerate(late_slots))),
        (cube, main, [(i, row) for i, row in rows_of_main if i not in Z_FIRST]),
        (z_cube, main, [(i, row) for i, row in rows_of_main if i in Z_FIRST]),
    )

    def part_out(i):
        return pltpu.make_async_copy(parts.at[i], parts_hbm.at[i], out_sem.at[i])


    def serve_now(n):
        for k in range(cube.steps - 1, -1, -1):
            for exchange, block_of, slots in plan:
                for i, row in slots:
                    if row[k] == n or (n == end + cube.steps - 3 and row[k] > n):
                        exchange.step(*block_of(i), k)
                        if block_of is main and n >= end and k == cube.steps - 1:
                            part_out(i).start()

    for load in loads:
        load.wait()
    bs = keep_mask[0].astype(F32) * keep_rate[0]
    gain = column(gain2[...])
    hidden = tokens[...].astype(F32) + bs * nn(wo[...].T, mixed_t[...])
    r2 = inverse_rms(hidden)
    normed2_t = (hidden * r2 * gain).astype(BF16)
    normed2 = normed2_t.T

    def seed():
        by_group = jnp.where(groups[...] == 1, exit_scales[1], exit_scales[0])
        return cotangent[...].astype(F32) * by_group

    d_down_t = (bs * seed()).astype(BF16)
    d_down = d_down_t.T
    width, rows = hidden.shape
    for i in range(count):
        filled = 3 * width if i < chunks else 5 * width // 2
        for half in range(2 if filled < parts.shape[2] else 0):
            parts[i, half, filled:] = jnp.zeros((parts.shape[2] - filled, LANES), BF16)
    down = d_hidden = input_grad
    down[...] = jnp.zeros_like(down)
    d_normed2[...] = jnp.zeros_like(d_normed2)

    def chunk(f, carry):
        for load in weights(f):
            load.wait()

        @pl.when(f + 1 < chunks)
        def _():
            for load in weights(f + 1):
                load.start()

        wg, wu, wd = (stream.at[f % 2, k] for k in range(3))
        gate = nn(normed2, wg[...])
        up = nn(normed2, wu[...])
        d_act = nn(d_down, wd[...])
        sig = 1.0 / (1.0 + jnp.exp(-gate))
        silu = gate * sig
        act = (silu * up).astype(BF16)
        down[...] += nt(wd[...], act)
        down_grad = nn(d_down_t, act)
        d_up = (d_act * silu).astype(BF16)
        up_grad = nn(normed2_t, d_up)
        d_gate = (d_act * up * (sig + silu * (1.0 - sig))).astype(BF16)
        gate_grad = nn(normed2_t, d_gate)
        d_normed2[...] += nt(wu[...], d_up) + nt(wg[...], d_gate)
        for k, value in enumerate((gate_grad, up_grad, down_grad)):
            for half in range(2):
                parts[f, half, k * width : (k + 1) * width] = value[
                    :, half * LANES : (half + 1) * LANES
                ].astype(BF16)
        cube.begin(*main(f), 0)
        by_slot(f, 0, chunks, lambda m: serve_now(m - lead))
        return carry

    lax.fori_loop(0, chunks, chunk, 0)
    layer_out[...] = (hidden + bs * down[...]).astype(BF16)
    whole_out = pltpu.make_async_copy(layer_out, layer_out_hbm, out_sem.at[count])
    whole_out.start()
    dn = d_normed2[...]
    gain2_grad = jnp.sum(dn * hidden * r2, axis=1, keepdims=True)
    gained = gain * dn
    dh = seed() + r2 * gained - hidden * (r2 * r2 * r2) * jnp.mean(gained * hidden, axis=0, keepdims=True)
    d_hidden[...] = dh
    d_branch = (bs * dh).astype(BF16)
    out_grad = nt(mixed_t[...], d_branch)
    half_rows = width // 2
    last = parts.at[chunks]
    last[0, :width] = out_grad[:, :LANES].astype(BF16)
    last[0, width : 2 * width] = out_grad[:, LANES : 2 * LANES].astype(BF16)
    middle = out_grad[:, 2 * LANES : 3 * LANES].astype(BF16)
    last[0, 2 * width : 2 * width + half_rows] = middle[:half_rows]
    last[1, :half_rows] = middle[half_rows:]
    last[1, half_rows : half_rows + width] = out_grad[:, 3 * LANES : 4 * LANES].astype(BF16)
    last[1, half_rows + width : half_rows + 2 * width] = last_block(out_grad)
    cube.begin(*main(chunks), 0)
    serve_now(-2)
    d_mixed = nn(wo[...], d_branch).astype(BF16)
    delta = total
    for h in range(H):
        g, r = h // GROUP, h % GROUP
        head = d_mixed[h * HD : (h + 1) * HD]
        d_out[h * PAIR : h * PAIR + HD] = jnp.zeros((HD, rows), BF16)
        d_out[h * PAIR + HD : (h + 1) * PAIR] = head
        delta[g, r] = jnp.sum(head.astype(F32) * attended[g, r], axis=0, keepdims=True)
    dq = attended
    dq[...] = jnp.zeros_like(dq)
    normed_kept = mixed_t
    normed_kept[...] = normalize(tokens, gain1)
    serve_now(-1)

    def kv_down(j, g):
        return pltpu.make_async_remote_copy(
            src_ref=kv_all.at[j, g],
            dst_ref=chain.at[j // 2, g],
            send_sem=kv_send.at[j, g],
            recv_sem=chain_recv.at[j // 2, g],
            device_id=below,
            device_id_type=MESH,
        )

    def kv_across(j, g):
        return pltpu.make_async_remote_copy(
            src_ref=kv_all.at[j, g],
            dst_ref=cross.at[j // 2, g],
            send_sem=kv_send.at[j, g],
            recv_sem=cross_recv.at[j // 2, g],
            device_id=across,
            device_id_type=MESH,
        )

    d_kv = d_normed2
    lag = lags[0]
    for i in range(1, floors):
        lag = jnp.where(z == i, lags[i], lag)
    nq, nk = H * HD, KVH * HD
    span = GROUP * PAIR

    def finish_head(g):
        at = pl.multiple_of(g * span, PAIR)
        c, sn = cos[...], -sin[...]
        for r in range(GROUP):
            piece = turn(dq[g, r] * HD**-0.5, c, sn)
            d_out[pl.ds(at + r * HD, HD)] = piece.astype(BF16)
        pair = d_kv[pl.ds(pl.multiple_of(g * PAIR, PAIR), PAIR)]
        d_out[pl.ds(at + GROUP * HD, HD)] = turn(pair[:HD], c, sn).astype(BF16)
        d_out[pl.ds(at + (GROUP + 1) * HD, HD)] = pair[HD:].astype(BF16)
        high = (GROUP + 2) * HD
        grad = nt(d_out[pl.ds(at, high)], normed_kept[...]).astype(BF16)
        tails[g, 0, :high] = grad[:, :LANES]
        tails[g, 0, high : 2 * high] = grad[:, LANES : 2 * LANES]
        tails[g, 0, 2 * high : 5 * high // 2] = grad[: high // 2, 2 * LANES : 3 * LANES]
        tails[g, 1, : high // 2] = grad[high // 2 :, 2 * LANES : 3 * LANES]
        tails[g, 1, high // 2 : 3 * high // 2] = grad[:, 3 * LANES : 4 * LANES]
        tails[g, 1, 3 * high // 2 : 5 * high // 2] = jnp.concatenate(
            [grad[:, 4 * LANES :], jnp.zeros((high, HD), BF16)], axis=1
        )
        for half in range(2):
            rest = tails.shape[2] - 5 * high // 2
            tails[g, half, 5 * high // 2 :] = jnp.zeros((rest, LANES), BF16)
        tail_cube.begin(*late(g), 0)

    def slot(n, carry):
        g, j = n // blocks, n % blocks
        busy = n < KVH * blocks

        def unit(masked):
            d_keys, d_vals = grad_unit(g, queries, d_out, lse, delta, kv_all[j, g], dq, masked)
            kv_all[j, g, :HD] = d_keys.astype(BF16)
            kv_all[j, g, HD:] = d_vals.astype(BF16)

        @pl.when(busy & (j < b))
        def _():
            unit(False)

        @pl.when(busy & (j == b))
        def _():
            unit(True)

        @pl.when(busy & (j <= b) & (j % 2 != y))
        def _():
            kv_across(j, g).start()

        ready = n - lag
        at = jnp.maximum(ready, 0)
        gg, jj = at // blocks, at % blocks
        due = (ready >= 0) & (ready < KVH * blocks) & (jj % 2 == y)
        rows_of = pl.ds(pl.multiple_of(jnp.minimum(gg, KVH - 1) * PAIR, PAIR), PAIR)

        @pl.when(due & (jj < b))
        def _():
            kv_across(jj, gg).wait_recv()
            both = kv_all[jj, gg].astype(F32) + cross[jj // 2, gg].astype(F32)

            @pl.when(has_above)
            def _():
                kv_down(jj, gg).wait_recv()
                kv_all[jj, gg] = (both + chain[jj // 2, gg].astype(F32)).astype(BF16)

            @pl.when(jnp.logical_not(has_above))
            def _():
                kv_all[jj, gg] = both.astype(BF16)

            kv_down(jj, gg).start()

        @pl.when(due & (jj == b))
        def _():
            d_kv[rows_of] = kv_all[jj, gg].astype(F32)

            @pl.when(y == 0)
            def _():
                kv_across(jj, gg).wait_recv()
                d_kv[rows_of] = d_kv[rows_of] + cross[jj // 2, gg].astype(F32)

            @pl.when(has_above)
            def _():
                kv_down(jj, gg).wait_recv()
                d_kv[rows_of] = d_kv[rows_of] + chain[jj // 2, gg].astype(F32)

        settled = n - whole_head

        @pl.when((settled >= 0) & (settled % blocks == 0) & (settled // blocks < KVH))
        def _():
            finish_head(settled // blocks)

        by_slot(n, 0, end, serve_now)

        @pl.when(n == end - 1)
        def _():
            tail_cube.step(*late(KVH - 1), 0)

        return carry

    lax.fori_loop(0, end, slot, 0)

    def drain_backward(n, carry):
        j, g = n // KVH, n % KVH

        @pl.when(j % 2 != y)
        def _():
            kv_across(j, g).wait_send()

        @pl.when((j % 2 == y) & (j < b))
        def _():
            kv_down(j, g).wait_send()

        return carry

    lax.fori_loop(0, KVH * (b + 1), drain_backward, 0)

    x = tokens[...].astype(F32)
    r1 = inverse_rms(x)
    weight = column(gain1[...])
    d_normed = jnp.zeros_like(x)
    for g in range(KVH):
        first = g * span
        middle, last_row = first + GROUP * HD, first + (GROUP + 1) * HD
        heads = slice(g * GROUP * HD, (g + 1) * GROUP * HD)
        own_head = slice(g * HD, (g + 1) * HD)
        d_normed = (
            d_normed
            + nn(wq[:, heads], d_out[first:middle])
            + nn(wk[own_head].T, d_out[middle:last_row])
            + nn(wv[own_head].T, d_out[last_row : last_row + HD])
        )
    pads = jnp.zeros((1, gains.shape[1] - width), F32)
    for i, values in enumerate((jnp.sum(d_normed * x * r1, axis=1, keepdims=True), gain2_grad)):
        gains[i : i + 1] = jnp.concatenate([as_row(values), pads], axis=1)
    gains[2:] = jnp.zeros((gains.shape[0] - 2, gains.shape[1]), F32)

    def gain_swap(d):
        return pltpu.make_async_remote_copy(
            src_ref=gains,
            dst_ref=gain_landing.at[d],
            send_sem=gain_send.at[d],
            recv_sem=gain_recv.at[d],
            device_id=cube.partners[d],
            device_id_type=MESH,
        )

    gain_swap(0).start()
    for i, row in rows_of_main:
        if row[-1] < end:
            part_out(i).start()
    tail_cube.step(*late(KVH - 1), 1)
    gained = weight * d_normed
    input_grad[...] = (
        d_hidden[...] + r1 * gained - x * (r1 * r1 * r1) * jnp.mean(gained * x, axis=0, keepdims=True)
    )
    grad_out = pltpu.make_async_copy(input_grad, input_grad_hbm, out_sem.at[count + 1])
    grad_out.start()
    for k in range(2, cube.steps):
        serve_now(end + k - 2)
        if k - 2 < depth:
            gain_swap(k - 2).wait()
            gains[...] = gains[...] + gain_landing[k - 2]
            if k - 1 < depth:
                gain_swap(k - 1).start()
        tail_cube.step(*late(KVH - 1), k)
    for i in range(count):
        (z_cube if i in Z_FIRST else cube).drain(*main(i))
        part_out(i).wait()
    whole_out.wait()
    grad_out.wait()
    for i in range(KVH):
        tail_cube.drain(*late(i))


def unpack_kernel(
    chunks, parts, tails, gains, late_out, late_grad,
    gate, up, down, output_hbm, query_hbm, key_hbm, value_hbm, gain1, gain2, layer_out, input_grad,
    output, query, key, value, sems,
):
    i = pl.program_id(0)
    width = gate.shape[0]
    layer_out[...] = late_out[...]
    input_grad[...] = late_grad[...]
    small = ((output, output_hbm), (query, query_hbm), (key, key_hbm), (value, value_hbm))
    copies = [pltpu.make_async_copy(a, b, sems.at[n]) for n, (a, b) in enumerate(small)]

    @pl.when(i > 0)
    def _():
        for k, out in enumerate((gate, up, down)):
            for half in range(2):
                piece = parts[0, half, k * width : (k + 1) * width]
                out[:, half * LANES : (half + 1) * LANES] = piece.astype(F32)

    def five(ref, at, rows):
        half = rows // 2
        yield ref[at + (0, slice(0, rows))]
        yield ref[at + (0, slice(rows, 2 * rows))]
        yield jnp.concatenate(
            [ref[at + (0, slice(2 * rows, 2 * rows + half))], ref[at + (1, slice(0, half))]], axis=0
        )
        yield ref[at + (1, slice(half, half + rows))]
        yield ref[at + (1, slice(half + rows, half + 2 * rows))]

    @pl.when(i == 0)
    def _():
        for k, block in enumerate(five(parts, (0,), width)):
            size = min(LANES, width - k * LANES)
            output[:, k * LANES : k * LANES + size] = block.astype(F32)[:, :size]
        high = GROUP * HD
        for k in range(5):
            size = min(LANES, width - k * LANES)
            lanes = slice(k * LANES, k * LANES + size)
            columns = []
            for g in range(KVH):
                block = list(five(tails, (g,), high + PAIR))[k].astype(F32)[:, :size]
                own = slice(g * HD, (g + 1) * HD)
                key[own, lanes] = block[high : high + HD]
                value[own, lanes] = block[high + HD :]
                columns.append(block[:high])
            query[lanes, :] = jnp.concatenate(columns, axis=0).T
        gain1[...] = gains[0, :width]
        gain2[...] = gains[1, :width]
        for copy in copies:
            copy.start()

    @pl.when(i == chunks)
    def _():
        for copy in copies:
            copy.wait()


def last_block(grad):
    return jnp.concatenate(
        [grad[:, 4 * LANES :], jnp.zeros((grad.shape[0], LANES - HD), F32)], axis=1
    ).astype(BF16)


def body(sizes, tokens, positions, groups, keep_mask, exit_scales, keep_rate, wq, wk, wv, wo, wg, wu, wd, gain1, gain2, cotangent):
    seqs, blocks = sizes
    depth = log2(seqs) + log2(blocks)
    tokens, cotangent = tokens[0].T, cotangent[0].T
    wk, wv, wd = wk.T, wv.T, wd.T
    width, rows = tokens.shape
    ff = wg.shape[1]
    nq, nk = H * HD, KVH * HD
    frequency = 1.0 / ROPE_BASE ** (jnp.arange(HALF, dtype=F32) * (2.0 / HD))
    angle = frequency[:, None] * positions[0].astype(F32)[None, :]
    cos, sin = jnp.cos(angle), jnp.sin(angle)

    chunks = ff // (2 * LANES)
    count = chunks + 1
    part_rows = padded_rows(3 * width)
    tail_rows = padded_rows(5 * (GROUP + 2) * HD // 2)
    gain_shape = (8, 5 * LANES)
    vmem, smem, hbm = (pl.BlockSpec(memory_space=m) for m in (pltpu.VMEM, pltpu.SMEM, pl.ANY))
    head_t = (KVH, GROUP, PAIR, rows)
    head_o = (KVH, GROUP, HD, rows)
    head_1 = (KVH, GROUP, 1, rows)
    dma = pltpu.SemaphoreType.DMA
    scratch = [
        pltpu.VMEM((width, rows), BF16),
        pltpu.VMEM((width, rows), F32),
        pltpu.VMEM((count, 2, part_rows, LANES), BF16),
        pltpu.VMEM(wo.shape, BF16),
        pltpu.VMEM((2, 3, width, 2 * LANES), BF16),
        pltpu.VMEM(cotangent.shape, BF16),
        pltpu.VMEM(head_t, BF16),
        pltpu.VMEM((blocks, KVH, PAIR, rows), BF16),
        pltpu.VMEM(head_o, F32),
        pltpu.VMEM((nq, rows), BF16),
        pltpu.VMEM(head_1, F32),
        pltpu.VMEM(head_1, F32),
        pltpu.VMEM((width, rows), F32),
        pltpu.VMEM((H * PAIR, rows), BF16),
        pltpu.VMEM((blocks // 2, KVH, PAIR, rows), BF16),
        pltpu.VMEM((blocks // 2, KVH, PAIR, rows), BF16),
        dma((2,)),
        dma((2, 3)),
        dma((count + 2,)),
        dma((2, blocks, KVH)),
        dma((blocks, KVH)),
        dma((count, depth + HALVINGS)),
        dma((count, depth + HALVINGS)),
        pltpu.SemaphoreType.REGULAR((count, HALVINGS)),
        dma((KVH, depth + HALVINGS)),
        dma((KVH, depth + HALVINGS)),
        pltpu.SemaphoreType.REGULAR((KVH, HALVINGS)),
        dma((depth,)),
        dma((depth,)),
        dma((blocks, KVH)),
        dma((blocks // 2, KVH)),
        dma((blocks // 2, KVH)),
    ]
    scratch += [pltpu.VMEM((depth,) + gain_shape, F32)]
    scratch += [pltpu.VMEM((count, n, LANES), BF16) for n in row_counts(part_rows, depth)]
    scratch += [pltpu.VMEM((KVH, n, LANES), BF16) for n in row_counts(tail_rows, depth)]
    layer_out, input_grad, parts, tails, gains = pl.pallas_call(
        functools.partial(mega_kernel, sizes),
        out_shape=[
            jax.ShapeDtypeStruct((width, rows), BF16),
            jax.ShapeDtypeStruct((width, rows), F32),
            jax.ShapeDtypeStruct((count, 2, part_rows, LANES), BF16),
            jax.ShapeDtypeStruct((KVH, 2, tail_rows, LANES), BF16),
            jax.ShapeDtypeStruct(gain_shape, F32),
        ],
        in_specs=[smem] * 3 + [vmem] * 9 + [hbm] * 5,
        out_specs=[hbm] * 3 + [vmem] * 2,
        scratch_shapes=scratch,
        compiler_params=pltpu.CompilerParams(
            vmem_limit_bytes=VMEM_LIMIT, collective_id=0, has_side_effects=True
        ),
    )(
        keep_mask, keep_rate, exit_scales,
        tokens, groups, gain1, gain2, wk, wv, wq, cos, sin,
        wo, wg, wu, wd, cotangent,
    )

    wide = pl.BlockSpec((width, 2 * LANES), lambda i: (0, jnp.maximum(i - 1, 0)))
    lines = pl.BlockSpec((width // chunks, rows), lambda i: (jnp.maximum(i - 1, 0), 0))
    line = pl.BlockSpec((width,), lambda i: (0,))
    small = [(nq, width), (width, nq), (nk, width), (nk, width)]
    (gate_grad, up_grad, down_grad, output_grad, query_grad, key_grad, value_grad, gain1_grad, gain2_grad, layer_out, input_grad) = pl.pallas_call(
        functools.partial(unpack_kernel, chunks),
        grid=(count,),
        out_shape=[jax.ShapeDtypeStruct((width, ff), F32)] * 3
        + [jax.ShapeDtypeStruct(shape, F32) for shape in small + [(width,), (width,)]]
        + [jax.ShapeDtypeStruct((width, rows), t) for t in (BF16, F32)],
        in_specs=[
            pl.BlockSpec((1, 2, part_rows, LANES), lambda i: ((i + chunks) % count, 0, 0, 0)),
            pl.BlockSpec(tails.shape, lambda i: (0,) * 4),
            pl.BlockSpec(gain_shape, lambda i: (0, 0)),
            lines,
            lines,
        ],
        out_specs=[wide] * 3 + [hbm] * 4 + [line] * 2 + [lines] * 2,
        scratch_shapes=[pltpu.VMEM(shape, F32) for shape in small] + [dma((4,))],
        compiler_params=pltpu.CompilerParams(vmem_limit_bytes=VMEM_LIMIT),
    )(parts, tails, gains, layer_out, input_grad)
    return (
        layer_out.T[None],
        input_grad.T[None],
        query_grad,
        key_grad.T,
        value_grad.T,
        output_grad,
        gate_grad,
        up_grad,
        down_grad.T,
        gain1_grad,
        gain2_grad,
    )


def solution(mesh):
    local = P("seq", "blk", None)
    pair = P("seq", "blk")
    placed = (local, pair, pair, P("seq")) + (P(),) * 11 + (local,)
    return jax.shard_map(
        functools.partial(body, (mesh.shape["seq"], mesh.shape["blk"])),
        mesh=mesh,
        in_specs=placed,
        out_specs=(local, local) + (P(),) * 9,
        check_vma=False,
    )
```

```python
import functools

import jax
import jax.numpy as jnp
from jax import lax
from jax.experimental import pallas as pl
from jax.experimental.pallas import tpu as pltpu
from jax.sharding import PartitionSpec as P

H = 9
KVH = 3
HD = 64
GROUP = H // KVH
HALF = HD // 2
PAIR = 2 * HD

EPSILON = 1e-05
ROPE_BASE = 100000.0
MASKED = -1e30
LOG2E = 1.4426950408889634
LN2 = 0.6931471805599453
F32 = jnp.float32
BF16 = jnp.bfloat16
VMEM_LIMIT = 61 * 1024 * 1024
MESH = pl.DeviceIdType.MESH
LANES = 128
REROUTED = 1


def nn(a, b):
    return lax.dot_general(a, b, (((1,), (0,)), ((), ())), preferred_element_type=F32)


def nt(a, b):
    return lax.dot_general(a, b, (((1,), (1,)), ((), ())), preferred_element_type=F32)


def column(values):
    return jnp.broadcast_to(values[None, :], (8, values.shape[0])).T[:, :1]


def as_row(values):
    return jnp.broadcast_to(values, (values.shape[0], 8)).T[:1]


def inverse_rms(values):
    return lax.rsqrt(jnp.mean(values * values, axis=0, keepdims=True) + EPSILON)


def turn(rows, cos, sin):
    u, w = rows[:HALF], rows[HALF:]
    return jnp.concatenate([u * cos - w * sin, w * cos + u * sin], axis=0)


def normalize(tokens, gain):
    x = tokens[...].astype(F32)
    return (x * inverse_rms(x) * column(gain[...])).astype(BF16)


def project_kv(normed, wk, wv, cos, sin, kv):
    keys = nn(wk[...], normed)
    vals = nn(wv[...], normed)
    for g in range(KVH):
        span = slice(g * HD, (g + 1) * HD)
        kv[g, :HD, :] = turn(keys[span], cos, sin).astype(BF16)
        kv[g, HD:, :] = vals[span].astype(BF16)


def project_q(normed, wq, cos, sin, queries):
    raw = nn(wq[...].T, normed)
    factor = HD**-0.5 * LOG2E
    for h in range(H):
        turned = turn(raw[h * HD : (h + 1) * HD], cos, sin) * factor
        queries[h // GROUP, h % GROUP, :HD, :] = turned.astype(BF16)
        queries[h // GROUP, h % GROUP, HD:, :] = jnp.zeros((HD, raw.shape[1]), BF16)


def values_and_ones(packed):
    ones = jnp.ones((16, packed.shape[1]), BF16)
    return jnp.concatenate([packed[HD:], ones], axis=0)


def first_unit(g, queries, packed, out, top, total):
    rows = queries.shape[-1]
    part = rows // 2
    natural = packed.T
    values = values_and_ones(packed)
    items = [(r, c) for r in range(GROUP) for c in range(2)]

    def scores_of(i):
        r, c = items[i]
        return nn(natural[: (c + 1) * part], queries[g, r, :, c * part : (c + 1) * part])

    scores = scores_of(0)
    done = []
    for i, (r, c) in enumerate(items):
        later = scores_of(i + 1) if i + 1 < len(items) else None
        key_at = lax.broadcasted_iota(jnp.int32, scores.shape, 0)
        query_at = lax.broadcasted_iota(jnp.int32, scores.shape, 1) + c * part
        scores = jnp.where(key_at <= query_at, scores, MASKED)
        high = jnp.max(scores, axis=0, keepdims=True)
        probs = jnp.exp2(scores - high)
        done.append((high, nn(values[:, : (c + 1) * part], probs.astype(BF16))))
        scores = later
    for (r, c), (high, summed) in zip(items, done):
        cols = slice(c * part, (c + 1) * part)
        top[g, r, :, cols] = high
        total[g, r, :, cols] = summed[HD : HD + 1]
        out[g, r, :, cols] = summed[:HD]


def next_unit(g, queries, packed, out, top, total):
    natural = packed.T
    values = values_and_ones(packed)
    before = [(top[g, r], total[g, r], out[g, r]) for r in range(GROUP)]
    scores = [nn(natural, queries[g, r]) for r in range(2)]
    done = []
    for r in range(GROUP):
        if r + 2 < GROUP:
            scores.append(nn(natural, queries[g, r + 2]))
        old, count, acc = before[r]
        high = jnp.maximum(old, jnp.max(scores[r], axis=0, keepdims=True))
        probs = jnp.exp2(scores[r] - high)
        fade = jnp.exp2(old - high)
        summed = nn(values, probs.astype(BF16))
        done.append((high, count * fade + summed[HD : HD + 1], acc * fade + summed[:HD]))
    for r, (high, count, acc) in enumerate(done):
        top[g, r] = high
        total[g, r] = count
        out[g, r] = acc


def finish_forward(out, top, total, mixed_t, lse):
    for h in range(H):
        g, r = h // GROUP, h % GROUP
        scaled = out[g, r] * (1.0 / total[g, r])
        out[g, r] = scaled
        mixed_t[h * HD : (h + 1) * HD, :] = scaled.astype(BF16)
        lse[g, r] = top[g, r] + jnp.log2(total[g, r])


def grad_unit(g, queries, d_out, lse, delta, packed, dq, masked):
    rows = queries.shape[-1]
    part = rows // 2
    natural = packed.T
    items = [(r, c) for r in range(GROUP) for c in range(2)]
    columns = [slice(c * part, (c + 1) * part) for c in range(2)]
    before = [dq[g, r, :, columns[c]] for r, c in items]

    def seen(c):
        return (c + 1) * part if masked else rows

    def d_head(r, c, first=0):
        start = pl.multiple_of((g * GROUP + r) * PAIR + first, HD)
        return d_out[pl.ds(start, PAIR - first), columns[c]]

    def products(r, c):
        keys = natural[: seen(c)]
        return nn(keys, queries[g, r, :, columns[c]]), nn(keys, d_head(r, c))

    ahead = products(*items[0])
    done = []
    totals = [None] * 4
    for i, (r, c) in enumerate(items):
        scores, d_probs = ahead
        if i + 1 < len(items):
            ahead = products(*items[i + 1])
        probs = jnp.exp2(scores - lse[g, r, :, columns[c]])
        if masked:
            key_at = lax.broadcasted_iota(jnp.int32, scores.shape, 0)
            query_at = lax.broadcasted_iota(jnp.int32, scores.shape, 1) + c * part
            probs = jnp.where(key_at <= query_at, probs, 0.0)
        d_scores = (probs * (d_probs - delta[g, r, :, columns[c]])).astype(BF16)
        terms = (
            nt(d_head(r, c, HD), probs.astype(BF16)),
            nt(queries[g, r, :HD, columns[c]], d_scores),
        )
        kind = c if masked else 0
        for n, term in enumerate(terms):
            at = 2 * kind + n
            totals[at] = term if totals[at] is None else totals[at] + term
        done.append(before[i] + nn(packed[:HD, : seen(c)], d_scores))
    for i, (r, c) in enumerate(items):
        dq[g, r, :, columns[c]] = done[i]
    d_vals, d_keys = totals[:2]
    if masked:
        rest = jnp.zeros((HD, rows - part), F32)
        d_vals = totals[2] + jnp.concatenate([d_vals, rest], axis=1)
        d_keys = totals[3] + jnp.concatenate([d_keys, rest], axis=1)
    return d_keys * LN2, d_vals


def log2(n):
    return n.bit_length() - 1


HALVINGS = 3


class Cube:
    def __init__(self, links, send_sem, recv_sem, credit):
        self.send_sem, self.recv_sem, self.credit = send_sem, recv_sem, credit
        self.bits = [bit for bit, _ in links]
        self.partners = [partner for _, partner in links]
        self.depth = len(links)
        self.steps = self.depth + HALVINGS

    def span(self, rows, d):
        lo, size = 0, rows
        for e in range(1, d + 1):
            size = size // 2
            lo = lo + self.bits[e] * size
        return lo, size

    def owned(self, part, d):
        lo, size = self.span(part.shape[1], d)
        return part.at[self.bits[0], pl.ds(pl.multiple_of(lo, 16), size)]

    def transfer(self, part, landing, i, k):
        mine, d = self.bits[0], k
        if k == 0:
            src, dst = part.at[1 - mine], landing[0]
        elif k < HALVINGS:
            before, _ = self.span(part.shape[1], k - 1)
            _, size = self.span(part.shape[1], k)
            start = pl.multiple_of(before + (1 - self.bits[k]) * size, 16)
            src, dst = part.at[mine, pl.ds(start, size)], landing[k]
        elif k < self.depth:
            src, dst = self.owned(part, HALVINGS - 1), landing[k]
        else:
            d = self.steps - 1 - k
            src = dst = self.owned(part, d)
        return pltpu.make_async_remote_copy(
            src_ref=src,
            dst_ref=dst,
            send_sem=self.send_sem.at[i, k],
            recv_sem=self.recv_sem.at[i, k],
            device_id=self.partners[d],
            device_id_type=MESH,
        )

    def begin(self, part, landing, i, k):
        if k >= self.depth:
            pl.semaphore_wait(self.credit.at[i, self.steps - 1 - k], 1)
        self.transfer(part, landing, i, k).start()

    def step(self, part, landing, i, k):
        moved = self.transfer(part, landing, i, k)
        if k < self.depth:
            moved.wait_send()
            if k < HALVINGS:
                pl.semaphore_signal(
                    self.credit.at[i, k], inc=1, device_id=self.partners[k], device_id_type=MESH
                )
        moved.wait_recv()
        if k < self.depth:
            rows = self.owned(part, min(k, HALVINGS - 1))
            rows[...] = rows[...] + landing[k][...]
        if k + 1 < self.steps:
            self.begin(part, landing, i, k + 1)

    def drain(self, part, landing, i):
        for k in range(self.depth, self.steps):
            self.transfer(part, landing, i, k).wait_send()


MAIN_SLOTS = [
    [-7, -5, -4, -2, 0, 7, 22, 28],
    [-6, -4, -2, 0, 2, 3, 7, 25],
    [-5, -2, 0, 2, 7, 10, 31, 32],
    [-4, -1, 2, 6, 10, 16, 25, 32],
    [-3, 1, 2, 4, 9, 12, 23, 25],
    [-1, 2, 4, 7, 14, 18, 25, 30],
    [1, 3, 6, 11, 18, 22, 27, 29],
]
LATE_SLOTS = [[12, 14, 17, 19, 23, 24, 27, 31], [21, 23, 26, 27, 29, 30, 31, 32]]
LAGS = [8, 6, 4, 2]
Z_FIRST = [3]


def tables(count, depth, blocks):
    if (count, depth, blocks) == (len(MAIN_SLOTS), 5, 8):
        return MAIN_SLOTS, LATE_SLOTS, LAGS
    floors = blocks // 2
    main = []
    for i in range(count):
        row = [i - count, 2 * i - count + 2]
        row += [2 * (i + k) - count for k in range(HALVINGS - 1, depth + 1)]
        main.append(row + [row[-1] + 3 + i // 2, row[-1] + 4 + i // 2])
    waits = [1, 3, 4] + list(range(5, 2 * depth - 1, 2))
    waits += [waits[-1] + 1, waits[-1] + 3, waits[-1] + 4]
    late = [[g * blocks + blocks + 1 + w for w in waits] for g in range(KVH - 1)]
    return main, late, [2 * (floors - z) for z in range(floors)]


def by_slot(n, first, last, act):
    if last - first == 1:
        act(first)
        return
    middle = (first + last) // 2
    for wanted, lo, hi in ((n < middle, first, middle), (n >= middle, middle, last)):
        pl.when(wanted)(functools.partial(by_slot, n, lo, hi, act))


def cube_links(s, b, sizes):
    seqs, blocks = sizes
    links = []
    for bit in range(log2(seqs)):
        mine = (s // 2**bit) % 2
        links.append((mine, (s + 2**bit * (1 - 2 * mine), b)))
    for bit in range(log2(blocks)):
        mine = (b // 2**bit) % 2
        links.append((mine, (s, b + 2**bit * (1 - 2 * mine))))
    return links


def row_counts(rows, depth):
    return [rows >> min(k, HALVINGS - 1) for k in range(depth)]


def padded_rows(rows):
    return (rows + 63) // 64 * 64


def mega_kernel(
    sizes,
    keep_mask, keep_rate, exit_scales,
    tokens, groups, gain1, gain2, wk, wv, wq, cos, sin,
    wo_hbm, wg_hbm, wu_hbm, wd_hbm, cot_hbm,
    layer_out_hbm, input_grad_hbm, parts_hbm, tails, gains,
    layer_out, input_grad, parts,
    wo, stream, cotangent,
    queries, kv_all, attended, mixed_t, top, total,
    d_normed2, d_out,
    chain, cross,
    load_sem, stream_sem, out_sem, send_sem, recv_sem, cube_send, cube_recv, credit, tail_send, tail_recv, tail_credit,
    gain_send, gain_recv, kv_send, chain_recv, cross_recv, gain_landing,
    *landings,
):
    seqs, blocks = sizes
    s, b = lax.axis_index("seq"), lax.axis_index("blk")
    z, y, floors = b // 2, b % 2, blocks // 2
    above, below, across = (s, b + 2), (s, b - 2), (s, b + 1 - 2 * y)
    has_above, has_below = z < floors - 1, z > 0
    links = cube_links(s, b, sizes)
    cube = Cube(links, cube_send, cube_recv, credit)
    z_links = links[:1] + links[3:] + links[1:3]
    z_cube = Cube(z_links, cube_send, cube_recv, credit)
    tail_cube = Cube(links, tail_send, tail_recv, tail_credit)
    depth = cube.depth
    count = parts.shape[0]

    def main(i):
        return parts.at[i], [r.at[i] for r in landings[:depth]], i

    def late(i):
        return tails.at[i], [r.at[i] for r in landings[depth:]], i

    loads = [
        pltpu.make_async_copy(src, dst, load_sem.at[i])
        for i, (src, dst) in enumerate(
            [(wo_hbm, wo), (cot_hbm, cotangent)]
        )
    ]
    step = 2 * LANES
    chunks = wg_hbm.shape[1] // step

    def weights(f):
        at = pl.ds(pl.multiple_of(f * step, step), step)
        return [
            pltpu.make_async_copy(ref.at[:, at], stream.at[f % 2, k], stream_sem.at[f % 2, k])
            for k, ref in enumerate((wg_hbm, wu_hbm, wd_hbm))
        ]

    for load in loads + weights(0):
        load.start()

    barrier = pltpu.get_barrier_semaphore()

    def greet(device):
        pl.semaphore_signal(barrier, inc=1, device_id=device, device_id_type=MESH)

    for device in cube.partners:
        greet(device)
    odd = z % 2
    extra_below = has_below & (odd == 0)
    extra_above = has_above & (odd == 1)

    @pl.when(extra_below)
    def _():
        greet(below)

    @pl.when(extra_above)
    def _():
        greet(above)

    extra = extra_below.astype(jnp.int32) + extra_above.astype(jnp.int32)

    def copy(kind, j, g):
        return pltpu.make_async_remote_copy(
            src_ref=kv_all.at[j, g],
            dst_ref=kv_all.at[j, g],
            send_sem=send_sem.at[kind, j, g],
            recv_sem=recv_sem.at[j, g],
            device_id=above if kind == 0 else across,
            device_id_type=MESH,
        )

    def rerouted(j, g):
        return (j == 0) & (g < REROUTED)

    normed = normalize(tokens, gain1)
    c, sn = cos[...], sin[...]
    project_kv(normed, wk, wv, c, sn, kv_all.at[b])
    pl.semaphore_wait(barrier, depth + extra)

    def send_own(g, carry):
        @pl.when(has_above)
        def _():
            copy(0, b, g).start()

        @pl.when(y == 0)
        def _():
            copy(1, b, g).start()

        return carry

    lax.fori_loop(0, KVH, send_own, 0)
    project_q(normed, wq, c, sn, queries)

    def own(g, carry):
        first_unit(g, queries, kv_all[b, g], attended, top, total)
        return carry

    lax.fori_loop(0, KVH, own, 0)

    def level(m, carry):
        def one(g, inner):
            @pl.when(m <= z)
            def _():
                j = b - 2 * m
                copy(0, j, g).wait_recv()

                @pl.when(has_above)
                def _():
                    copy(0, j, g).start()

                @pl.when(jnp.logical_not(rerouted(j, g)))
                def _():
                    copy(1, j, g).start()

                next_unit(g, queries, kv_all[j, g], attended, top, total)

            @pl.when((m >= 2) | (y == 1))
            def _():
                j = b - 2 * m + 3 - 2 * y
                copy(1, j, g).wait_recv()

                @pl.when(has_above & rerouted(j, g))
                def _():
                    copy(0, j, g).start()

                next_unit(g, queries, kv_all[j, g], attended, top, total)

            return inner

        return lax.fori_loop(0, KVH, one, carry)

    lax.fori_loop(1, z + 2, level, 0)
    lse = top
    finish_forward(attended, top, total, mixed_t, lse)

    def drain_forward(m, carry):
        def one(g, inner):
            j = b - 2 * m

            @pl.when(has_above)
            def _():
                copy(0, j, g).wait_send()

            @pl.when(((m >= 1) & jnp.logical_not(rerouted(j, g))) | ((m == 0) & (y == 0)))
            def _():
                copy(1, j, g).wait_send()

            return inner

        return lax.fori_loop(0, KVH, one, carry)

    lax.fori_loop(0, z + 1, drain_forward, 0)

    @pl.when(has_above & (y == 1))
    def _():
        for g in range(REROUTED):
            copy(0, 0, g).wait_send()


    whole_head = 2 * floors + 1
    end = (KVH - 1) * blocks + whole_head + 2
    main_slots, late_slots, lags = tables(count, depth, blocks)
    lead = count + 1
    rows_of_main = list(enumerate(main_slots))
    plan = (
        (tail_cube, late, list(enumerate(late_slots))),
        (cube, main, [(i, row) for i, row in rows_of_main if i not in Z_FIRST]),
        (z_cube, main, [(i, row) for i, row in rows_of_main if i in Z_FIRST]),
    )

    def part_out(i):
        return pltpu.make_async_copy(parts.at[i], parts_hbm.at[i], out_sem.at[i])


    def serve_now(n):
        for k in range(cube.steps - 1, -1, -1):
            for exchange, block_of, slots in plan:
                for i, row in slots:
                    if row[k] == n or (n == end + cube.steps - 3 and row[k] > n):
                        exchange.step(*block_of(i), k)
                        if block_of is main and n >= end and k == cube.steps - 1:
                            part_out(i).start()

    for load in loads:
        load.wait()
    bs = keep_mask[0].astype(F32) * keep_rate[0]
    gain = column(gain2[...])
    hidden = tokens[...].astype(F32) + bs * nn(wo[...].T, mixed_t[...])
    r2 = inverse_rms(hidden)
    normed2_t = (hidden * r2 * gain).astype(BF16)
    normed2 = normed2_t.T

    def seed():
        by_group = jnp.where(groups[...] == 1, exit_scales[1], exit_scales[0])
        return cotangent[...].astype(F32) * by_group

    d_down_t = (bs * seed()).astype(BF16)
    d_down = d_down_t.T
    width, rows = hidden.shape
    for i in range(count):
        filled = 3 * width if i < chunks else 5 * width // 2
        for half in range(2 if filled < parts.shape[2] else 0):
            parts[i, half, filled:] = jnp.zeros((parts.shape[2] - filled, LANES), BF16)
    down = d_hidden = input_grad
    down[...] = jnp.zeros_like(down)
    d_normed2[...] = jnp.zeros_like(d_normed2)

    def chunk(f, carry):
        for load in weights(f):
            load.wait()

        @pl.when(f + 1 < chunks)
        def _():
            for load in weights(f + 1):
                load.start()

        wg, wu, wd = (stream.at[f % 2, k] for k in range(3))
        gate = nn(normed2, wg[...])
        up = nn(normed2, wu[...])
        d_act = nn(d_down, wd[...])
        sig = 1.0 / (1.0 + jnp.exp(-gate))
        silu = gate * sig
        act = (silu * up).astype(BF16)
        down[...] += nt(wd[...], act)
        down_grad = nn(d_down_t, act)
        d_up = (d_act * silu).astype(BF16)
        up_grad = nn(normed2_t, d_up)
        d_gate = (d_act * up * (sig + silu * (1.0 - sig))).astype(BF16)
        gate_grad = nn(normed2_t, d_gate)
        d_normed2[...] += nt(wu[...], d_up) + nt(wg[...], d_gate)
        for k, value in enumerate((gate_grad, up_grad, down_grad)):
            for half in range(2):
                parts[f, half, k * width : (k + 1) * width] = value[
                    :, half * LANES : (half + 1) * LANES
                ].astype(BF16)
        cube.begin(*main(f), 0)
        by_slot(f, 0, chunks, lambda m: serve_now(m - lead))
        return carry

    lax.fori_loop(0, chunks, chunk, 0)
    layer_out[...] = (hidden + bs * down[...]).astype(BF16)
    whole_out = pltpu.make_async_copy(layer_out, layer_out_hbm, out_sem.at[count])
    whole_out.start()
    dn = d_normed2[...]
    gain2_grad = jnp.sum(dn * hidden * r2, axis=1, keepdims=True)
    gained = gain * dn
    dh = seed() + r2 * gained - hidden * (r2 * r2 * r2) * jnp.mean(gained * hidden, axis=0, keepdims=True)
    d_hidden[...] = dh
    d_branch = (bs * dh).astype(BF16)
    out_grad = nt(mixed_t[...], d_branch)
    half_rows = width // 2
    last = parts.at[chunks]
    last[0, :width] = out_grad[:, :LANES].astype(BF16)
    last[0, width : 2 * width] = out_grad[:, LANES : 2 * LANES].astype(BF16)
    middle = out_grad[:, 2 * LANES : 3 * LANES].astype(BF16)
    last[0, 2 * width : 2 * width + half_rows] = middle[:half_rows]
    last[1, :half_rows] = middle[half_rows:]
    last[1, half_rows : half_rows + width] = out_grad[:, 3 * LANES : 4 * LANES].astype(BF16)
    last[1, half_rows + width : half_rows + 2 * width] = last_block(out_grad)
    cube.begin(*main(chunks), 0)
    serve_now(-2)
    d_mixed = nn(wo[...], d_branch).astype(BF16)
    delta = total
    for h in range(H):
        g, r = h // GROUP, h % GROUP
        head = d_mixed[h * HD : (h + 1) * HD]
        d_out[h * PAIR : h * PAIR + HD] = jnp.zeros((HD, rows), BF16)
        d_out[h * PAIR + HD : (h + 1) * PAIR] = head
        delta[g, r] = jnp.sum(head.astype(F32) * attended[g, r], axis=0, keepdims=True)
    dq = attended
    dq[...] = jnp.zeros_like(dq)
    normed_kept = mixed_t
    normed_kept[...] = normalize(tokens, gain1)
    serve_now(-1)

    def kv_down(j, g):
        return pltpu.make_async_remote_copy(
            src_ref=kv_all.at[j, g],
            dst_ref=chain.at[j // 2, g],
            send_sem=kv_send.at[j, g],
            recv_sem=chain_recv.at[j // 2, g],
            device_id=below,
            device_id_type=MESH,
        )

    def kv_across(j, g):
        return pltpu.make_async_remote_copy(
            src_ref=kv_all.at[j, g],
            dst_ref=cross.at[j // 2, g],
            send_sem=kv_send.at[j, g],
            recv_sem=cross_recv.at[j // 2, g],
            device_id=across,
            device_id_type=MESH,
        )

    d_kv = d_normed2
    lag = lags[0]
    for i in range(1, floors):
        lag = jnp.where(z == i, lags[i], lag)
    nq, nk = H * HD, KVH * HD
    span = GROUP * PAIR

    def finish_head(g):
        at = pl.multiple_of(g * span, PAIR)
        c, sn = cos[...], -sin[...]
        for r in range(GROUP):
            piece = turn(dq[g, r] * HD**-0.5, c, sn)
            d_out[pl.ds(at + r * HD, HD)] = piece.astype(BF16)
        pair = d_kv[pl.ds(pl.multiple_of(g * PAIR, PAIR), PAIR)]
        d_out[pl.ds(at + GROUP * HD, HD)] = turn(pair[:HD], c, sn).astype(BF16)
        d_out[pl.ds(at + (GROUP + 1) * HD, HD)] = pair[HD:].astype(BF16)
        high = (GROUP + 2) * HD
        grad = nt(d_out[pl.ds(at, high)], normed_kept[...]).astype(BF16)
        tails[g, 0, :high] = grad[:, :LANES]
        tails[g, 0, high : 2 * high] = grad[:, LANES : 2 * LANES]
        tails[g, 0, 2 * high : 5 * high // 2] = grad[: high // 2, 2 * LANES : 3 * LANES]
        tails[g, 1, : high // 2] = grad[high // 2 :, 2 * LANES : 3 * LANES]
        tails[g, 1, high // 2 : 3 * high // 2] = grad[:, 3 * LANES : 4 * LANES]
        tails[g, 1, 3 * high // 2 : 5 * high // 2] = jnp.concatenate(
            [grad[:, 4 * LANES :], jnp.zeros((high, HD), BF16)], axis=1
        )
        for half in range(2):
            rest = tails.shape[2] - 5 * high // 2
            tails[g, half, 5 * high // 2 :] = jnp.zeros((rest, LANES), BF16)
        tail_cube.begin(*late(g), 0)

    def slot(n, carry):
        g, j = n // blocks, n % blocks
        busy = n < KVH * blocks

        def unit(masked):
            d_keys, d_vals = grad_unit(g, queries, d_out, lse, delta, kv_all[j, g], dq, masked)
            kv_all[j, g, :HD] = d_keys.astype(BF16)
            kv_all[j, g, HD:] = d_vals.astype(BF16)

        @pl.when(busy & (j < b))
        def _():
            unit(False)

        @pl.when(busy & (j == b))
        def _():
            unit(True)

        @pl.when(busy & (j <= b) & (j % 2 != y))
        def _():
            kv_across(j, g).start()

        ready = n - lag
        at = jnp.maximum(ready, 0)
        gg, jj = at // blocks, at % blocks
        due = (ready >= 0) & (ready < KVH * blocks) & (jj % 2 == y)
        rows_of = pl.ds(pl.multiple_of(jnp.minimum(gg, KVH - 1) * PAIR, PAIR), PAIR)

        @pl.when(due & (jj < b))
        def _():
            kv_across(jj, gg).wait_recv()
            both = kv_all[jj, gg].astype(F32) + cross[jj // 2, gg].astype(F32)

            @pl.when(has_above)
            def _():
                kv_down(jj, gg).wait_recv()
                kv_all[jj, gg] = (both + chain[jj // 2, gg].astype(F32)).astype(BF16)

            @pl.when(jnp.logical_not(has_above))
            def _():
                kv_all[jj, gg] = both.astype(BF16)

            kv_down(jj, gg).start()

        @pl.when(due & (jj == b))
        def _():
            d_kv[rows_of] = kv_all[jj, gg].astype(F32)

            @pl.when(y == 0)
            def _():
                kv_across(jj, gg).wait_recv()
                d_kv[rows_of] = d_kv[rows_of] + cross[jj // 2, gg].astype(F32)

            @pl.when(has_above)
            def _():
                kv_down(jj, gg).wait_recv()
                d_kv[rows_of] = d_kv[rows_of] + chain[jj // 2, gg].astype(F32)

        settled = n - whole_head

        @pl.when((settled >= 0) & (settled % blocks == 0) & (settled // blocks < KVH))
        def _():
            finish_head(settled // blocks)

        by_slot(n, 0, end, serve_now)

        @pl.when(n == end - 1)
        def _():
            tail_cube.step(*late(KVH - 1), 0)

        return carry

    lax.fori_loop(0, end, slot, 0)

    def drain_backward(n, carry):
        j, g = n // KVH, n % KVH

        @pl.when(j % 2 != y)
        def _():
            kv_across(j, g).wait_send()

        @pl.when((j % 2 == y) & (j < b))
        def _():
            kv_down(j, g).wait_send()

        return carry

    lax.fori_loop(0, KVH * (b + 1), drain_backward, 0)

    x = tokens[...].astype(F32)
    r1 = inverse_rms(x)
    weight = column(gain1[...])
    d_normed = jnp.zeros_like(x)
    for g in range(KVH):
        first = g * span
        middle, last_row = first + GROUP * HD, first + (GROUP + 1) * HD
        heads = slice(g * GROUP * HD, (g + 1) * GROUP * HD)
        own_head = slice(g * HD, (g + 1) * HD)
        d_normed = (
            d_normed
            + nn(wq[:, heads], d_out[first:middle])
            + nn(wk[own_head].T, d_out[middle:last_row])
            + nn(wv[own_head].T, d_out[last_row : last_row + HD])
        )
    pads = jnp.zeros((1, gains.shape[1] - width), F32)
    for i, values in enumerate((jnp.sum(d_normed * x * r1, axis=1, keepdims=True), gain2_grad)):
        gains[i : i + 1] = jnp.concatenate([as_row(values), pads], axis=1)
    gains[2:] = jnp.zeros((gains.shape[0] - 2, gains.shape[1]), F32)

    def gain_swap(d):
        return pltpu.make_async_remote_copy(
            src_ref=gains,
            dst_ref=gain_landing.at[d],
            send_sem=gain_send.at[d],
            recv_sem=gain_recv.at[d],
            device_id=cube.partners[d],
            device_id_type=MESH,
        )

    gain_swap(0).start()
    for i, row in rows_of_main:
        if row[-1] < end:
            part_out(i).start()
    tail_cube.step(*late(KVH - 1), 1)
    gained = weight * d_normed
    input_grad[...] = (
        d_hidden[...] + r1 * gained - x * (r1 * r1 * r1) * jnp.mean(gained * x, axis=0, keepdims=True)
    )
    grad_out = pltpu.make_async_copy(input_grad, input_grad_hbm, out_sem.at[count + 1])
    grad_out.start()
    for k in range(2, cube.steps):
        serve_now(end + k - 2)
        if k - 2 < depth:
            gain_swap(k - 2).wait()
            gains[...] = gains[...] + gain_landing[k - 2]
            if k - 1 < depth:
                gain_swap(k - 1).start()
        tail_cube.step(*late(KVH - 1), k)
    for i in range(count):
        (z_cube if i in Z_FIRST else cube).drain(*main(i))
        part_out(i).wait()
    whole_out.wait()
    grad_out.wait()
    for i in range(KVH):
        tail_cube.drain(*late(i))


def unpack_kernel(
    chunks, parts, tails, gains, late_out, late_grad,
    gate, up, down, output_hbm, query_hbm, key_hbm, value_hbm, gain1, gain2, layer_out, input_grad,
    output, query, key, value, sems,
):
    i = pl.program_id(0)
    width = gate.shape[0]
    layer_out[...] = late_out[...]
    input_grad[...] = late_grad[...]
    small = ((output, output_hbm), (query, query_hbm), (key, key_hbm), (value, value_hbm))
    copies = [pltpu.make_async_copy(a, b, sems.at[n]) for n, (a, b) in enumerate(small)]

    @pl.when(i > 0)
    def _():
        for k, out in enumerate((gate, up, down)):
            for half in range(2):
                piece = parts[0, half, k * width : (k + 1) * width]
                out[:, half * LANES : (half + 1) * LANES] = piece.astype(F32)

    def five(ref, at, rows):
        half = rows // 2
        yield ref[at + (0, slice(0, rows))]
        yield ref[at + (0, slice(rows, 2 * rows))]
        yield jnp.concatenate(
            [ref[at + (0, slice(2 * rows, 2 * rows + half))], ref[at + (1, slice(0, half))]], axis=0
        )
        yield ref[at + (1, slice(half, half + rows))]
        yield ref[at + (1, slice(half + rows, half + 2 * rows))]

    @pl.when(i == 0)
    def _():
        for k, block in enumerate(five(parts, (0,), width)):
            size = min(LANES, width - k * LANES)
            output[:, k * LANES : k * LANES + size] = block.astype(F32)[:, :size]
        high = GROUP * HD
        for k in range(5):
            size = min(LANES, width - k * LANES)
            lanes = slice(k * LANES, k * LANES + size)
            columns = []
            for g in range(KVH):
                block = list(five(tails, (g,), high + PAIR))[k].astype(F32)[:, :size]
                own = slice(g * HD, (g + 1) * HD)
                key[own, lanes] = block[high : high + HD]
                value[own, lanes] = block[high + HD :]
                columns.append(block[:high])
            query[lanes, :] = jnp.concatenate(columns, axis=0).T
        gain1[...] = gains[0, :width]
        gain2[...] = gains[1, :width]
        for copy in copies:
            copy.start()

    @pl.when(i == chunks)
    def _():
        for copy in copies:
            copy.wait()


def last_block(grad):
    return jnp.concatenate(
        [grad[:, 4 * LANES :], jnp.zeros((grad.shape[0], LANES - HD), F32)], axis=1
    ).astype(BF16)


def body(sizes, tokens, positions, groups, keep_mask, exit_scales, keep_rate, wq, wk, wv, wo, wg, wu, wd, gain1, gain2, cotangent):
    seqs, blocks = sizes
    depth = log2(seqs) + log2(blocks)
    tokens, cotangent = tokens[0].T, cotangent[0].T
    wk, wv, wd = wk.T, wv.T, wd.T
    width, rows = tokens.shape
    ff = wg.shape[1]
    nq, nk = H * HD, KVH * HD
    frequency = 1.0 / ROPE_BASE ** (jnp.arange(HALF, dtype=F32) * (2.0 / HD))
    angle = frequency[:, None] * positions[0].astype(F32)[None, :]
    cos, sin = jnp.cos(angle), jnp.sin(angle)

    chunks = ff // (2 * LANES)
    count = chunks + 1
    part_rows = padded_rows(3 * width)
    tail_rows = padded_rows(5 * (GROUP + 2) * HD // 2)
    gain_shape = (8, 5 * LANES)
    vmem, smem, hbm = (pl.BlockSpec(memory_space=m) for m in (pltpu.VMEM, pltpu.SMEM, pl.ANY))
    head_t = (KVH, GROUP, PAIR, rows)
    head_o = (KVH, GROUP, HD, rows)
    head_1 = (KVH, GROUP, 1, rows)
    dma = pltpu.SemaphoreType.DMA
    scratch = [
        pltpu.VMEM((width, rows), BF16),
        pltpu.VMEM((width, rows), F32),
        pltpu.VMEM((count, 2, part_rows, LANES), BF16),
        pltpu.VMEM(wo.shape, BF16),
        pltpu.VMEM((2, 3, width, 2 * LANES), BF16),
        pltpu.VMEM(cotangent.shape, BF16),
        pltpu.VMEM(head_t, BF16),
        pltpu.VMEM((blocks, KVH, PAIR, rows), BF16),
        pltpu.VMEM(head_o, F32),
        pltpu.VMEM((nq, rows), BF16),
        pltpu.VMEM(head_1, F32),
        pltpu.VMEM(head_1, F32),
        pltpu.VMEM((width, rows), F32),
        pltpu.VMEM((H * PAIR, rows), BF16),
        pltpu.VMEM((blocks // 2, KVH, PAIR, rows), BF16),
        pltpu.VMEM((blocks // 2, KVH, PAIR, rows), BF16),
        dma((2,)),
        dma((2, 3)),
        dma((count + 2,)),
        dma((2, blocks, KVH)),
        dma((blocks, KVH)),
        dma((count, depth + HALVINGS)),
        dma((count, depth + HALVINGS)),
        pltpu.SemaphoreType.REGULAR((count, HALVINGS)),
        dma((KVH, depth + HALVINGS)),
        dma((KVH, depth + HALVINGS)),
        pltpu.SemaphoreType.REGULAR((KVH, HALVINGS)),
        dma((depth,)),
        dma((depth,)),
        dma((blocks, KVH)),
        dma((blocks // 2, KVH)),
        dma((blocks // 2, KVH)),
    ]
    scratch += [pltpu.VMEM((depth,) + gain_shape, F32)]
    scratch += [pltpu.VMEM((count, n, LANES), BF16) for n in row_counts(part_rows, depth)]
    scratch += [pltpu.VMEM((KVH, n, LANES), BF16) for n in row_counts(tail_rows, depth)]
    layer_out, input_grad, parts, tails, gains = pl.pallas_call(
        functools.partial(mega_kernel, sizes),
        out_shape=[
            jax.ShapeDtypeStruct((width, rows), BF16),
            jax.ShapeDtypeStruct((width, rows), F32),
            jax.ShapeDtypeStruct((count, 2, part_rows, LANES), BF16),
            jax.ShapeDtypeStruct((KVH, 2, tail_rows, LANES), BF16),
            jax.ShapeDtypeStruct(gain_shape, F32),
        ],
        in_specs=[smem] * 3 + [vmem] * 9 + [hbm] * 5,
        out_specs=[hbm] * 3 + [vmem] * 2,
        scratch_shapes=scratch,
        compiler_params=pltpu.CompilerParams(
            vmem_limit_bytes=VMEM_LIMIT, collective_id=0, has_side_effects=True
        ),
    )(
        keep_mask, keep_rate, exit_scales,
        tokens, groups, gain1, gain2, wk, wv, wq, cos, sin,
        wo, wg, wu, wd, cotangent,
    )

    wide = pl.BlockSpec((width, 2 * LANES), lambda i: (0, jnp.maximum(i - 1, 0)))
    lines = pl.BlockSpec((width // chunks, rows), lambda i: (jnp.maximum(i - 1, 0), 0))
    line = pl.BlockSpec((width,), lambda i: (0,))
    small = [(nq, width), (width, nq), (nk, width), (nk, width)]
    (gate_grad, up_grad, down_grad, output_grad, query_grad, key_grad, value_grad, gain1_grad, gain2_grad, layer_out, input_grad) = pl.pallas_call(
        functools.partial(unpack_kernel, chunks),
        grid=(count,),
        out_shape=[jax.ShapeDtypeStruct((width, ff), F32)] * 3
        + [jax.ShapeDtypeStruct(shape, F32) for shape in small + [(width,), (width,)]]
        + [jax.ShapeDtypeStruct((width, rows), t) for t in (BF16, F32)],
        in_specs=[
            pl.BlockSpec((1, 2, part_rows, LANES), lambda i: ((i + chunks) % count, 0, 0, 0)),
            pl.BlockSpec(tails.shape, lambda i: (0,) * 4),
            pl.BlockSpec(gain_shape, lambda i: (0, 0)),
            lines,
            lines,
        ],
        out_specs=[wide] * 3 + [hbm] * 4 + [line] * 2 + [lines] * 2,
        scratch_shapes=[pltpu.VMEM(shape, F32) for shape in small] + [dma((4,))],
        compiler_params=pltpu.CompilerParams(vmem_limit_bytes=VMEM_LIMIT),
    )(parts, tails, gains, layer_out, input_grad)
    return (
        layer_out.T[None],
        input_grad.T[None],
        query_grad,
        key_grad.T,
        value_grad.T,
        output_grad,
        gate_grad,
        up_grad,
        down_grad.T,
        gain1_grad,
        gain2_grad,
    )


def solution(mesh):
    local = P("seq", "blk", None)
    pair = P("seq", "blk")
    placed = (local, pair, pair, P("seq")) + (P(),) * 11 + (local,)
    return jax.shard_map(
        functools.partial(body, (mesh.shape["seq"], mesh.shape["blk"])),
        mesh=mesh,
        in_specs=placed,
        out_specs=(local, local) + (P(),) * 9,
        check_vma=False,
    )
```

```python
import functools

import jax
import jax.numpy as jnp
from jax import lax
from jax.experimental import pallas as pl
from jax.experimental.pallas import tpu as pltpu
from jax.sharding import PartitionSpec as P

H = 9
KVH = 3
HD = 64
GROUP = H // KVH
HALF = HD // 2
PAIR = 2 * HD

EPSILON = 1e-05
ROPE_BASE = 100000.0
MASKED = -1e30
LOG2E = 1.4426950408889634
LN2 = 0.6931471805599453
F32 = jnp.float32
BF16 = jnp.bfloat16
VMEM_LIMIT = 61 * 1024 * 1024
MESH = pl.DeviceIdType.MESH
LANES = 128
REROUTED = 1


def nn(a, b):
    return lax.dot_general(a, b, (((1,), (0,)), ((), ())), preferred_element_type=F32)


def nt(a, b):
    return lax.dot_general(a, b, (((1,), (1,)), ((), ())), preferred_element_type=F32)


def column(values):
    return jnp.broadcast_to(values[None, :], (8, values.shape[0])).T[:, :1]


def as_row(values):
    return jnp.broadcast_to(values, (values.shape[0], 8)).T[:1]


def inverse_rms(values):
    return lax.rsqrt(jnp.mean(values * values, axis=0, keepdims=True) + EPSILON)


def turn(rows, cos, sin):
    u, w = rows[:HALF], rows[HALF:]
    return jnp.concatenate([u * cos - w * sin, w * cos + u * sin], axis=0)


def normalize(tokens, gain):
    x = tokens[...].astype(F32)
    return (x * inverse_rms(x) * column(gain[...])).astype(BF16)


def project_kv(normed, wk, wv, cos, sin, kv):
    keys = nn(wk[...], normed)
    vals = nn(wv[...], normed)
    for g in range(KVH):
        span = slice(g * HD, (g + 1) * HD)
        kv[g, :HD, :] = turn(keys[span], cos, sin).astype(BF16)
        kv[g, HD:, :] = vals[span].astype(BF16)


def project_q(normed, wq, cos, sin, queries):
    raw = nn(wq[...].T, normed)
    factor = HD**-0.5 * LOG2E
    for h in range(H):
        turned = turn(raw[h * HD : (h + 1) * HD], cos, sin) * factor
        queries[h // GROUP, h % GROUP, :HD, :] = turned.astype(BF16)
        queries[h // GROUP, h % GROUP, HD:, :] = jnp.zeros((HD, raw.shape[1]), BF16)


def values_and_ones(packed):
    ones = jnp.ones((16, packed.shape[1]), BF16)
    return jnp.concatenate([packed[HD:], ones], axis=0)


def first_unit(g, queries, packed, out, top, total):
    rows = queries.shape[-1]
    part = rows // 2
    natural = packed.T
    values = values_and_ones(packed)
    items = [(r, c) for r in range(GROUP) for c in range(2)]

    def scores_of(i):
        r, c = items[i]
        return nn(natural[: (c + 1) * part], queries[g, r, :, c * part : (c + 1) * part])

    scores = scores_of(0)
    done = []
    for i, (r, c) in enumerate(items):
        later = scores_of(i + 1) if i + 1 < len(items) else None
        key_at = lax.broadcasted_iota(jnp.int32, scores.shape, 0)
        query_at = lax.broadcasted_iota(jnp.int32, scores.shape, 1) + c * part
        scores = jnp.where(key_at <= query_at, scores, MASKED)
        high = jnp.max(scores, axis=0, keepdims=True)
        probs = jnp.exp2(scores - high)
        done.append((high, nn(values[:, : (c + 1) * part], probs.astype(BF16))))
        scores = later
    for (r, c), (high, summed) in zip(items, done):
        cols = slice(c * part, (c + 1) * part)
        top[g, r, :, cols] = high
        total[g, r, :, cols] = summed[HD : HD + 1]
        out[g, r, :, cols] = summed[:HD]


def next_unit(g, queries, packed, out, top, total):
    natural = packed.T
    values = values_and_ones(packed)
    before = [(top[g, r], total[g, r], out[g, r]) for r in range(GROUP)]
    scores = [nn(natural, queries[g, r]) for r in range(2)]
    done = []
    for r in range(GROUP):
        if r + 2 < GROUP:
            scores.append(nn(natural, queries[g, r + 2]))
        old, count, acc = before[r]
        high = jnp.maximum(old, jnp.max(scores[r], axis=0, keepdims=True))
        probs = jnp.exp2(scores[r] - high)
        fade = jnp.exp2(old - high)
        summed = nn(values, probs.astype(BF16))
        done.append((high, count * fade + summed[HD : HD + 1], acc * fade + summed[:HD]))
    for r, (high, count, acc) in enumerate(done):
        top[g, r] = high
        total[g, r] = count
        out[g, r] = acc


def finish_forward(out, top, total, mixed_t, lse):
    for h in range(H):
        g, r = h // GROUP, h % GROUP
        scaled = out[g, r] * (1.0 / total[g, r])
        out[g, r] = scaled
        mixed_t[h * HD : (h + 1) * HD, :] = scaled.astype(BF16)
        lse[g, r] = top[g, r] + jnp.log2(total[g, r])


def grad_unit(g, queries, d_out, lse, delta, packed, dq, masked):
    rows = queries.shape[-1]
    part = rows // 2
    natural = packed.T
    items = [(r, c) for r in range(GROUP) for c in range(2)]
    columns = [slice(c * part, (c + 1) * part) for c in range(2)]
    before = [dq[g, r, :, columns[c]] for r, c in items]

    def seen(c):
        return (c + 1) * part if masked else rows

    def d_head(r, c, first=0):
        start = pl.multiple_of((g * GROUP + r) * PAIR + first, HD)
        return d_out[pl.ds(start, PAIR - first), columns[c]]

    def products(r, c):
        keys = natural[: seen(c)]
        return nn(keys, queries[g, r, :, columns[c]]), nn(keys, d_head(r, c))

    ahead = products(*items[0])
    done = []
    totals = [None] * 4
    for i, (r, c) in enumerate(items):
        scores, d_probs = ahead
        if i + 1 < len(items):
            ahead = products(*items[i + 1])
        probs = jnp.exp2(scores - lse[g, r, :, columns[c]])
        if masked:
            key_at = lax.broadcasted_iota(jnp.int32, scores.shape, 0)
            query_at = lax.broadcasted_iota(jnp.int32, scores.shape, 1) + c * part
            probs = jnp.where(key_at <= query_at, probs, 0.0)
        d_scores = (probs * (d_probs - delta[g, r, :, columns[c]])).astype(BF16)
        terms = (
            nt(d_head(r, c, HD), probs.astype(BF16)),
            nt(queries[g, r, :HD, columns[c]], d_scores),
        )
        kind = c if masked else 0
        for n, term in enumerate(terms):
            at = 2 * kind + n
            totals[at] = term if totals[at] is None else totals[at] + term
        done.append(before[i] + nn(packed[:HD, : seen(c)], d_scores))
    for i, (r, c) in enumerate(items):
        dq[g, r, :, columns[c]] = done[i]
    d_vals, d_keys = totals[:2]
    if masked:
        rest = jnp.zeros((HD, rows - part), F32)
        d_vals = totals[2] + jnp.concatenate([d_vals, rest], axis=1)
        d_keys = totals[3] + jnp.concatenate([d_keys, rest], axis=1)
    return d_keys * LN2, d_vals


def log2(n):
    return n.bit_length() - 1


HALVINGS = 3


class Cube:
    def __init__(self, links, send_sem, recv_sem, credit):
        self.send_sem, self.recv_sem, self.credit = send_sem, recv_sem, credit
        self.bits = [bit for bit, _ in links]
        self.partners = [partner for _, partner in links]
        self.depth = len(links)
        self.steps = self.depth + HALVINGS

    def span(self, rows, d):
        lo, size = 0, rows
        for e in range(1, d + 1):
            size = size // 2
            lo = lo + self.bits[e] * size
        return lo, size

    def owned(self, part, d):
        lo, size = self.span(part.shape[1], d)
        return part.at[self.bits[0], pl.ds(pl.multiple_of(lo, 16), size)]

    def transfer(self, part, landing, i, k):
        mine, d = self.bits[0], k
        if k == 0:
            src, dst = part.at[1 - mine], landing[0]
        elif k < HALVINGS:
            before, _ = self.span(part.shape[1], k - 1)
            _, size = self.span(part.shape[1], k)
            start = pl.multiple_of(before + (1 - self.bits[k]) * size, 16)
            src, dst = part.at[mine, pl.ds(start, size)], landing[k]
        elif k < self.depth:
            src, dst = self.owned(part, HALVINGS - 1), landing[k]
        else:
            d = self.steps - 1 - k
            src = dst = self.owned(part, d)
        return pltpu.make_async_remote_copy(
            src_ref=src,
            dst_ref=dst,
            send_sem=self.send_sem.at[i, k],
            recv_sem=self.recv_sem.at[i, k],
            device_id=self.partners[d],
            device_id_type=MESH,
        )

    def begin(self, part, landing, i, k):
        if k >= self.depth:
            pl.semaphore_wait(self.credit.at[i, self.steps - 1 - k], 1)
        self.transfer(part, landing, i, k).start()

    def step(self, part, landing, i, k):
        moved = self.transfer(part, landing, i, k)
        if k < self.depth:
            moved.wait_send()
            if k < HALVINGS:
                pl.semaphore_signal(
                    self.credit.at[i, k], inc=1, device_id=self.partners[k], device_id_type=MESH
                )
        moved.wait_recv()
        if k < self.depth:
            rows = self.owned(part, min(k, HALVINGS - 1))
            rows[...] = rows[...] + landing[k][...]
        if k + 1 < self.steps:
            self.begin(part, landing, i, k + 1)

    def drain(self, part, landing, i):
        for k in range(self.depth, self.steps):
            self.transfer(part, landing, i, k).wait_send()


MAIN_SLOTS = [
    [-7, -5, -4, -2, 0, 7, 22, 28],
    [-6, -4, -2, 0, 2, 3, 7, 25],
    [-5, -2, 0, 2, 7, 10, 31, 32],
    [-4, -1, 2, 6, 10, 16, 25, 32],
    [-3, 1, 2, 4, 9, 12, 23, 25],
    [-1, 2, 4, 7, 14, 18, 25, 30],
    [1, 3, 6, 11, 18, 22, 27, 29],
]
LATE_SLOTS = [[12, 14, 17, 19, 23, 24, 27, 31], [21, 23, 26, 27, 29, 30, 31, 32]]
LAGS = [8, 6, 4, 2]
Z_FIRST = [3]


def tables(count, depth, blocks):
    if (count, depth, blocks) == (len(MAIN_SLOTS), 5, 8):
        return MAIN_SLOTS, LATE_SLOTS, LAGS
    floors = blocks // 2
    main = []
    for i in range(count):
        row = [i - count, 2 * i - count + 2]
        row += [2 * (i + k) - count for k in range(HALVINGS - 1, depth + 1)]
        main.append(row + [row[-1] + 3 + i // 2, row[-1] + 4 + i // 2])
    waits = [1, 3, 4] + list(range(5, 2 * depth - 1, 2))
    waits += [waits[-1] + 1, waits[-1] + 3, waits[-1] + 4]
    late = [[g * blocks + blocks + 1 + w for w in waits] for g in range(KVH - 1)]
    return main, late, [2 * (floors - z) for z in range(floors)]


def by_slot(n, first, last, act):
    if last - first == 1:
        act(first)
        return
    middle = (first + last) // 2
    for wanted, lo, hi in ((n < middle, first, middle), (n >= middle, middle, last)):
        pl.when(wanted)(functools.partial(by_slot, n, lo, hi, act))


def cube_links(s, b, sizes):
    seqs, blocks = sizes
    links = []
    for bit in range(log2(seqs)):
        mine = (s // 2**bit) % 2
        links.append((mine, (s + 2**bit * (1 - 2 * mine), b)))
    for bit in range(log2(blocks)):
        mine = (b // 2**bit) % 2
        links.append((mine, (s, b + 2**bit * (1 - 2 * mine))))
    return links


def row_counts(rows, depth):
    return [rows >> min(k, HALVINGS - 1) for k in range(depth)]


def padded_rows(rows):
    return (rows + 63) // 64 * 64


def mega_kernel(
    sizes,
    keep_mask, keep_rate, exit_scales,
    tokens, groups, gain1, gain2, wk, wv, wq, cos, sin,
    wo_hbm, wg_hbm, wu_hbm, wd_hbm, cot_hbm,
    layer_out_hbm, input_grad_hbm, parts_hbm, tails, gains,
    layer_out, input_grad, parts,
    wo, stream, cotangent,
    queries, kv_all, attended, mixed_t, top, total,
    d_normed2, d_out,
    chain, cross,
    load_sem, stream_sem, out_sem, send_sem, recv_sem, cube_send, cube_recv, credit, tail_send, tail_recv, tail_credit,
    gain_send, gain_recv, kv_send, chain_recv, cross_recv, gain_landing,
    *landings,
):
    seqs, blocks = sizes
    s, b = lax.axis_index("seq"), lax.axis_index("blk")
    z, y, floors = b // 2, b % 2, blocks // 2
    above, below, across = (s, b + 2), (s, b - 2), (s, b + 1 - 2 * y)
    has_above, has_below = z < floors - 1, z > 0
    links = cube_links(s, b, sizes)
    cube = Cube(links, cube_send, cube_recv, credit)
    z_links = links[:1] + links[3:] + links[1:3]
    z_cube = Cube(z_links, cube_send, cube_recv, credit)
    tail_cube = Cube(links, tail_send, tail_recv, tail_credit)
    depth = cube.depth
    count = parts.shape[0]

    def main(i):
        return parts.at[i], [r.at[i] for r in landings[:depth]], i

    def late(i):
        return tails.at[i], [r.at[i] for r in landings[depth:]], i

    loads = [
        pltpu.make_async_copy(src, dst, load_sem.at[i])
        for i, (src, dst) in enumerate(
            [(wo_hbm, wo), (cot_hbm, cotangent)]
        )
    ]
    step = 2 * LANES
    chunks = wg_hbm.shape[1] // step

    def weights(f):
        at = pl.ds(pl.multiple_of(f * step, step), step)
        return [
            pltpu.make_async_copy(ref.at[:, at], stream.at[f % 2, k], stream_sem.at[f % 2, k])
            for k, ref in enumerate((wg_hbm, wu_hbm, wd_hbm))
        ]

    for load in loads + weights(0):
        load.start()

    barrier = pltpu.get_barrier_semaphore()

    def greet(device):
        pl.semaphore_signal(barrier, inc=1, device_id=device, device_id_type=MESH)

    for device in cube.partners:
        greet(device)
    odd = z % 2
    extra_below = has_below & (odd == 0)
    extra_above = has_above & (odd == 1)

    @pl.when(extra_below)
    def _():
        greet(below)

    @pl.when(extra_above)
    def _():
        greet(above)

    extra = extra_below.astype(jnp.int32) + extra_above.astype(jnp.int32)

    def copy(kind, j, g):
        return pltpu.make_async_remote_copy(
            src_ref=kv_all.at[j, g],
            dst_ref=kv_all.at[j, g],
            send_sem=send_sem.at[kind, j, g],
            recv_sem=recv_sem.at[j, g],
            device_id=above if kind == 0 else across,
            device_id_type=MESH,
        )

    def rerouted(j, g):
        return (j == 0) & (g >= KVH - REROUTED)

    normed = normalize(tokens, gain1)
    c, sn = cos[...], sin[...]
    project_kv(normed, wk, wv, c, sn, kv_all.at[b])
    pl.semaphore_wait(barrier, depth + extra)

    def send_own(g, carry):
        @pl.when(has_above)
        def _():
            copy(0, b, g).start()

        @pl.when(y == 0)
        def _():
            copy(1, b, g).start()

        return carry

    lax.fori_loop(0, KVH, send_own, 0)
    project_q(normed, wq, c, sn, queries)

    def own(g, carry):
        first_unit(g, queries, kv_all[b, g], attended, top, total)
        return carry

    lax.fori_loop(0, KVH, own, 0)

    def level(m, carry):
        def one(g, inner):
            @pl.when(m <= z)
            def _():
                j = b - 2 * m
                copy(0, j, g).wait_recv()

                @pl.when(has_above)
                def _():
                    copy(0, j, g).start()

                @pl.when(jnp.logical_not(rerouted(j, g)))
                def _():
                    copy(1, j, g).start()

                next_unit(g, queries, kv_all[j, g], attended, top, total)

            @pl.when((m >= 2) | (y == 1))
            def _():
                j = b - 2 * m + 3 - 2 * y
                copy(1, j, g).wait_recv()

                @pl.when(has_above & rerouted(j, g))
                def _():
                    copy(0, j, g).start()

                next_unit(g, queries, kv_all[j, g], attended, top, total)

            return inner

        return lax.fori_loop(0, KVH, one, carry)

    lax.fori_loop(1, z + 2, level, 0)
    lse = top
    finish_forward(attended, top, total, mixed_t, lse)

    def drain_forward(m, carry):
        def one(g, inner):
            j = b - 2 * m

            @pl.when(has_above)
            def _():
                copy(0, j, g).wait_send()

            @pl.when(((m >= 1) & jnp.logical_not(rerouted(j, g))) | ((m == 0) & (y == 0)))
            def _():
                copy(1, j, g).wait_send()

            return inner

        return lax.fori_loop(0, KVH, one, carry)

    lax.fori_loop(0, z + 1, drain_forward, 0)

    @pl.when(has_above & (y == 1))
    def _():
        for g in range(KVH - REROUTED, KVH):
            copy(0, 0, g).wait_send()


    whole_head = 2 * floors + 1
    end = (KVH - 1) * blocks + whole_head + 2
    main_slots, late_slots, lags = tables(count, depth, blocks)
    lead = count + 1
    rows_of_main = list(enumerate(main_slots))
    plan = (
        (tail_cube, late, list(enumerate(late_slots))),
        (cube, main, [(i, row) for i, row in rows_of_main if i not in Z_FIRST]),
        (z_cube, main, [(i, row) for i, row in rows_of_main if i in Z_FIRST]),
    )

    def part_out(i):
        return pltpu.make_async_copy(parts.at[i], parts_hbm.at[i], out_sem.at[i])


    def serve_now(n):
        for k in range(cube.steps - 1, -1, -1):
            for exchange, block_of, slots in plan:
                for i, row in slots:
                    if row[k] == n or (n == end + cube.steps - 3 and row[k] > n):
                        exchange.step(*block_of(i), k)
                        if block_of is main and n >= end and k == cube.steps - 1:
                            part_out(i).start()

    for load in loads:
        load.wait()
    bs = keep_mask[0].astype(F32) * keep_rate[0]
    gain = column(gain2[...])
    hidden = tokens[...].astype(F32) + bs * nn(wo[...].T, mixed_t[...])
    r2 = inverse_rms(hidden)
    normed2_t = (hidden * r2 * gain).astype(BF16)
    normed2 = normed2_t.T

    def seed():
        by_group = jnp.where(groups[...] == 1, exit_scales[1], exit_scales[0])
        return cotangent[...].astype(F32) * by_group

    d_down_t = (bs * seed()).astype(BF16)
    d_down = d_down_t.T
    width, rows = hidden.shape
    for i in range(count):
        filled = 3 * width if i < chunks else 5 * width // 2
        for half in range(2 if filled < parts.shape[2] else 0):
            parts[i, half, filled:] = jnp.zeros((parts.shape[2] - filled, LANES), BF16)
    down = d_hidden = input_grad
    down[...] = jnp.zeros_like(down)
    d_normed2[...] = jnp.zeros_like(d_normed2)

    def chunk(f, carry):
        for load in weights(f):
            load.wait()

        @pl.when(f + 1 < chunks)
        def _():
            for load in weights(f + 1):
                load.start()

        wg, wu, wd = (stream.at[f % 2, k] for k in range(3))
        gate = nn(normed2, wg[...])
        up = nn(normed2, wu[...])
        d_act = nn(d_down, wd[...])
        sig = 1.0 / (1.0 + jnp.exp(-gate))
        silu = gate * sig
        act = (silu * up).astype(BF16)
        down[...] += nt(wd[...], act)
        down_grad = nn(d_down_t, act)
        d_up = (d_act * silu).astype(BF16)
        up_grad = nn(normed2_t, d_up)
        d_gate = (d_act * up * (sig + silu * (1.0 - sig))).astype(BF16)
        gate_grad = nn(normed2_t, d_gate)
        d_normed2[...] += nt(wu[...], d_up) + nt(wg[...], d_gate)
        for k, value in enumerate((gate_grad, up_grad, down_grad)):
            for half in range(2):
                parts[f, half, k * width : (k + 1) * width] = value[
                    :, half * LANES : (half + 1) * LANES
                ].astype(BF16)
        cube.begin(*main(f), 0)
        by_slot(f, 0, chunks, lambda m: serve_now(m - lead))
        return carry

    lax.fori_loop(0, chunks, chunk, 0)
    layer_out[...] = (hidden + bs * down[...]).astype(BF16)
    whole_out = pltpu.make_async_copy(layer_out, layer_out_hbm, out_sem.at[count])
    whole_out.start()
    dn = d_normed2[...]
    gain2_grad = jnp.sum(dn * hidden * r2, axis=1, keepdims=True)
    gained = gain * dn
    dh = seed() + r2 * gained - hidden * (r2 * r2 * r2) * jnp.mean(gained * hidden, axis=0, keepdims=True)
    d_hidden[...] = dh
    d_branch = (bs * dh).astype(BF16)
    out_grad = nt(mixed_t[...], d_branch)
    half_rows = width // 2
    last = parts.at[chunks]
    last[0, :width] = out_grad[:, :LANES].astype(BF16)
    last[0, width : 2 * width] = out_grad[:, LANES : 2 * LANES].astype(BF16)
    middle = out_grad[:, 2 * LANES : 3 * LANES].astype(BF16)
    last[0, 2 * width : 2 * width + half_rows] = middle[:half_rows]
    last[1, :half_rows] = middle[half_rows:]
    last[1, half_rows : half_rows + width] = out_grad[:, 3 * LANES : 4 * LANES].astype(BF16)
    last[1, half_rows + width : half_rows + 2 * width] = last_block(out_grad)
    cube.begin(*main(chunks), 0)
    serve_now(-2)
    d_mixed = nn(wo[...], d_branch).astype(BF16)
    delta = total
    for h in range(H):
        g, r = h // GROUP, h % GROUP
        head = d_mixed[h * HD : (h + 1) * HD]
        d_out[h * PAIR : h * PAIR + HD] = jnp.zeros((HD, rows), BF16)
        d_out[h * PAIR + HD : (h + 1) * PAIR] = head
        delta[g, r] = jnp.sum(head.astype(F32) * attended[g, r], axis=0, keepdims=True)
    dq = attended
    dq[...] = jnp.zeros_like(dq)
    normed_kept = mixed_t
    normed_kept[...] = normalize(tokens, gain1)
    serve_now(-1)

    def kv_down(j, g):
        return pltpu.make_async_remote_copy(
            src_ref=kv_all.at[j, g],
            dst_ref=chain.at[j // 2, g],
            send_sem=kv_send.at[j, g],
            recv_sem=chain_recv.at[j // 2, g],
            device_id=below,
            device_id_type=MESH,
        )

    def kv_across(j, g):
        return pltpu.make_async_remote_copy(
            src_ref=kv_all.at[j, g],
            dst_ref=cross.at[j // 2, g],
            send_sem=kv_send.at[j, g],
            recv_sem=cross_recv.at[j // 2, g],
            device_id=across,
            device_id_type=MESH,
        )

    d_kv = d_normed2
    lag = lags[0]
    for i in range(1, floors):
        lag = jnp.where(z == i, lags[i], lag)
    nq, nk = H * HD, KVH * HD
    span = GROUP * PAIR

    def finish_head(g):
        at = pl.multiple_of(g * span, PAIR)
        c, sn = cos[...], -sin[...]
        for r in range(GROUP):
            piece = turn(dq[g, r] * HD**-0.5, c, sn)
            d_out[pl.ds(at + r * HD, HD)] = piece.astype(BF16)
        pair = d_kv[pl.ds(pl.multiple_of(g * PAIR, PAIR), PAIR)]
        d_out[pl.ds(at + GROUP * HD, HD)] = turn(pair[:HD], c, sn).astype(BF16)
        d_out[pl.ds(at + (GROUP + 1) * HD, HD)] = pair[HD:].astype(BF16)
        high = (GROUP + 2) * HD
        grad = nt(d_out[pl.ds(at, high)], normed_kept[...]).astype(BF16)
        tails[g, 0, :high] = grad[:, :LANES]
        tails[g, 0, high : 2 * high] = grad[:, LANES : 2 * LANES]
        tails[g, 0, 2 * high : 5 * high // 2] = grad[: high // 2, 2 * LANES : 3 * LANES]
        tails[g, 1, : high // 2] = grad[high // 2 :, 2 * LANES : 3 * LANES]
        tails[g, 1, high // 2 : 3 * high // 2] = grad[:, 3 * LANES : 4 * LANES]
        tails[g, 1, 3 * high // 2 : 5 * high // 2] = jnp.concatenate(
            [grad[:, 4 * LANES :], jnp.zeros((high, HD), BF16)], axis=1
        )
        for half in range(2):
            rest = tails.shape[2] - 5 * high // 2
            tails[g, half, 5 * high // 2 :] = jnp.zeros((rest, LANES), BF16)
        tail_cube.begin(*late(g), 0)

    def slot(n, carry):
        g, j = n // blocks, n % blocks
        busy = n < KVH * blocks

        def unit(masked):
            d_keys, d_vals = grad_unit(g, queries, d_out, lse, delta, kv_all[j, g], dq, masked)
            kv_all[j, g, :HD] = d_keys.astype(BF16)
            kv_all[j, g, HD:] = d_vals.astype(BF16)

        @pl.when(busy & (j < b))
        def _():
            unit(False)

        @pl.when(busy & (j == b))
        def _():
            unit(True)

        @pl.when(busy & (j <= b) & (j % 2 != y))
        def _():
            kv_across(j, g).start()

        ready = n - lag
        at = jnp.maximum(ready, 0)
        gg, jj = at // blocks, at % blocks
        due = (ready >= 0) & (ready < KVH * blocks) & (jj % 2 == y)
        rows_of = pl.ds(pl.multiple_of(jnp.minimum(gg, KVH - 1) * PAIR, PAIR), PAIR)

        @pl.when(due & (jj < b))
        def _():
            kv_across(jj, gg).wait_recv()
            both = kv_all[jj, gg].astype(F32) + cross[jj // 2, gg].astype(F32)

            @pl.when(has_above)
            def _():
                kv_down(jj, gg).wait_recv()
                kv_all[jj, gg] = (both + chain[jj // 2, gg].astype(F32)).astype(BF16)

            @pl.when(jnp.logical_not(has_above))
            def _():
                kv_all[jj, gg] = both.astype(BF16)

            kv_down(jj, gg).start()

        @pl.when(due & (jj == b))
        def _():
            d_kv[rows_of] = kv_all[jj, gg].astype(F32)

            @pl.when(y == 0)
            def _():
                kv_across(jj, gg).wait_recv()
                d_kv[rows_of] = d_kv[rows_of] + cross[jj // 2, gg].astype(F32)

            @pl.when(has_above)
            def _():
                kv_down(jj, gg).wait_recv()
                d_kv[rows_of] = d_kv[rows_of] + chain[jj // 2, gg].astype(F32)

        settled = n - whole_head

        @pl.when((settled >= 0) & (settled % blocks == 0) & (settled // blocks < KVH))
        def _():
            finish_head(settled // blocks)

        by_slot(n, 0, end, serve_now)

        @pl.when(n == end - 1)
        def _():
            tail_cube.step(*late(KVH - 1), 0)

        return carry

    lax.fori_loop(0, end, slot, 0)

    def drain_backward(n, carry):
        j, g = n // KVH, n % KVH

        @pl.when(j % 2 != y)
        def _():
            kv_across(j, g).wait_send()

        @pl.when((j % 2 == y) & (j < b))
        def _():
            kv_down(j, g).wait_send()

        return carry

    lax.fori_loop(0, KVH * (b + 1), drain_backward, 0)

    x = tokens[...].astype(F32)
    r1 = inverse_rms(x)
    weight = column(gain1[...])
    d_normed = jnp.zeros_like(x)
    for g in range(KVH):
        first = g * span
        middle, last_row = first + GROUP * HD, first + (GROUP + 1) * HD
        heads = slice(g * GROUP * HD, (g + 1) * GROUP * HD)
        own_head = slice(g * HD, (g + 1) * HD)
        d_normed = (
            d_normed
            + nn(wq[:, heads], d_out[first:middle])
            + nn(wk[own_head].T, d_out[middle:last_row])
            + nn(wv[own_head].T, d_out[last_row : last_row + HD])
        )
    pads = jnp.zeros((1, gains.shape[1] - width), F32)
    for i, values in enumerate((jnp.sum(d_normed * x * r1, axis=1, keepdims=True), gain2_grad)):
        gains[i : i + 1] = jnp.concatenate([as_row(values), pads], axis=1)
    gains[2:] = jnp.zeros((gains.shape[0] - 2, gains.shape[1]), F32)

    def gain_swap(d):
        return pltpu.make_async_remote_copy(
            src_ref=gains,
            dst_ref=gain_landing.at[d],
            send_sem=gain_send.at[d],
            recv_sem=gain_recv.at[d],
            device_id=cube.partners[d],
            device_id_type=MESH,
        )

    gain_swap(0).start()
    for i, row in rows_of_main:
        if row[-1] < end:
            part_out(i).start()
    tail_cube.step(*late(KVH - 1), 1)
    gained = weight * d_normed
    input_grad[...] = (
        d_hidden[...] + r1 * gained - x * (r1 * r1 * r1) * jnp.mean(gained * x, axis=0, keepdims=True)
    )
    grad_out = pltpu.make_async_copy(input_grad, input_grad_hbm, out_sem.at[count + 1])
    grad_out.start()
    for k in range(2, cube.steps):
        serve_now(end + k - 2)
        if k - 2 < depth:
            gain_swap(k - 2).wait()
            gains[...] = gains[...] + gain_landing[k - 2]
            if k - 1 < depth:
                gain_swap(k - 1).start()
        tail_cube.step(*late(KVH - 1), k)
    for i in range(count):
        (z_cube if i in Z_FIRST else cube).drain(*main(i))
        part_out(i).wait()
    whole_out.wait()
    grad_out.wait()
    for i in range(KVH):
        tail_cube.drain(*late(i))


def unpack_kernel(
    chunks, parts, tails, gains, late_out, late_grad,
    gate, up, down, output_hbm, query_hbm, key_hbm, value_hbm, gain1, gain2, layer_out, input_grad,
    output, query, key, value, sems,
):
    i = pl.program_id(0)
    width = gate.shape[0]
    layer_out[...] = late_out[...]
    input_grad[...] = late_grad[...]
    small = ((output, output_hbm), (query, query_hbm), (key, key_hbm), (value, value_hbm))
    copies = [pltpu.make_async_copy(a, b, sems.at[n]) for n, (a, b) in enumerate(small)]

    @pl.when(i > 0)
    def _():
        for k, out in enumerate((gate, up, down)):
            for half in range(2):
                piece = parts[0, half, k * width : (k + 1) * width]
                out[:, half * LANES : (half + 1) * LANES] = piece.astype(F32)

    def five(ref, at, rows):
        half = rows // 2
        yield ref[at + (0, slice(0, rows))]
        yield ref[at + (0, slice(rows, 2 * rows))]
        yield jnp.concatenate(
            [ref[at + (0, slice(2 * rows, 2 * rows + half))], ref[at + (1, slice(0, half))]], axis=0
        )
        yield ref[at + (1, slice(half, half + rows))]
        yield ref[at + (1, slice(half + rows, half + 2 * rows))]

    @pl.when(i == 0)
    def _():
        for k, block in enumerate(five(parts, (0,), width)):
            size = min(LANES, width - k * LANES)
            output[:, k * LANES : k * LANES + size] = block.astype(F32)[:, :size]
        high = GROUP * HD
        for k in range(5):
            size = min(LANES, width - k * LANES)
            lanes = slice(k * LANES, k * LANES + size)
            columns = []
            for g in range(KVH):
                block = list(five(tails, (g,), high + PAIR))[k].astype(F32)[:, :size]
                own = slice(g * HD, (g + 1) * HD)
                key[own, lanes] = block[high : high + HD]
                value[own, lanes] = block[high + HD :]
                columns.append(block[:high])
            query[lanes, :] = jnp.concatenate(columns, axis=0).T
        gain1[...] = gains[0, :width]
        gain2[...] = gains[1, :width]
        for copy in copies:
            copy.start()

    @pl.when(i == chunks)
    def _():
        for copy in copies:
            copy.wait()


def last_block(grad):
    return jnp.concatenate(
        [grad[:, 4 * LANES :], jnp.zeros((grad.shape[0], LANES - HD), F32)], axis=1
    ).astype(BF16)


def body(sizes, tokens, positions, groups, keep_mask, exit_scales, keep_rate, wq, wk, wv, wo, wg, wu, wd, gain1, gain2, cotangent):
    seqs, blocks = sizes
    depth = log2(seqs) + log2(blocks)
    tokens, cotangent = tokens[0].T, cotangent[0].T
    wk, wv, wd = wk.T, wv.T, wd.T
    width, rows = tokens.shape
    ff = wg.shape[1]
    nq, nk = H * HD, KVH * HD
    frequency = 1.0 / ROPE_BASE ** (jnp.arange(HALF, dtype=F32) * (2.0 / HD))
    angle = frequency[:, None] * positions[0].astype(F32)[None, :]
    cos, sin = jnp.cos(angle), jnp.sin(angle)

    chunks = ff // (2 * LANES)
    count = chunks + 1
    part_rows = padded_rows(3 * width)
    tail_rows = padded_rows(5 * (GROUP + 2) * HD // 2)
    gain_shape = (8, 5 * LANES)
    vmem, smem, hbm = (pl.BlockSpec(memory_space=m) for m in (pltpu.VMEM, pltpu.SMEM, pl.ANY))
    head_t = (KVH, GROUP, PAIR, rows)
    head_o = (KVH, GROUP, HD, rows)
    head_1 = (KVH, GROUP, 1, rows)
    dma = pltpu.SemaphoreType.DMA
    scratch = [
        pltpu.VMEM((width, rows), BF16),
        pltpu.VMEM((width, rows), F32),
        pltpu.VMEM((count, 2, part_rows, LANES), BF16),
        pltpu.VMEM(wo.shape, BF16),
        pltpu.VMEM((2, 3, width, 2 * LANES), BF16),
        pltpu.VMEM(cotangent.shape, BF16),
        pltpu.VMEM(head_t, BF16),
        pltpu.VMEM((blocks, KVH, PAIR, rows), BF16),
        pltpu.VMEM(head_o, F32),
        pltpu.VMEM((nq, rows), BF16),
        pltpu.VMEM(head_1, F32),
        pltpu.VMEM(head_1, F32),
        pltpu.VMEM((width, rows), F32),
        pltpu.VMEM((H * PAIR, rows), BF16),
        pltpu.VMEM((blocks // 2, KVH, PAIR, rows), BF16),
        pltpu.VMEM((blocks // 2, KVH, PAIR, rows), BF16),
        dma((2,)),
        dma((2, 3)),
        dma((count + 2,)),
        dma((2, blocks, KVH)),
        dma((blocks, KVH)),
        dma((count, depth + HALVINGS)),
        dma((count, depth + HALVINGS)),
        pltpu.SemaphoreType.REGULAR((count, HALVINGS)),
        dma((KVH, depth + HALVINGS)),
        dma((KVH, depth + HALVINGS)),
        pltpu.SemaphoreType.REGULAR((KVH, HALVINGS)),
        dma((depth,)),
        dma((depth,)),
        dma((blocks, KVH)),
        dma((blocks // 2, KVH)),
        dma((blocks // 2, KVH)),
    ]
    scratch += [pltpu.VMEM((depth,) + gain_shape, F32)]
    scratch += [pltpu.VMEM((count, n, LANES), BF16) for n in row_counts(part_rows, depth)]
    scratch += [pltpu.VMEM((KVH, n, LANES), BF16) for n in row_counts(tail_rows, depth)]
    layer_out, input_grad, parts, tails, gains = pl.pallas_call(
        functools.partial(mega_kernel, sizes),
        out_shape=[
            jax.ShapeDtypeStruct((width, rows), BF16),
            jax.ShapeDtypeStruct((width, rows), F32),
            jax.ShapeDtypeStruct((count, 2, part_rows, LANES), BF16),
            jax.ShapeDtypeStruct((KVH, 2, tail_rows, LANES), BF16),
            jax.ShapeDtypeStruct(gain_shape, F32),
        ],
        in_specs=[smem] * 3 + [vmem] * 9 + [hbm] * 5,
        out_specs=[hbm] * 3 + [vmem] * 2,
        scratch_shapes=scratch,
        compiler_params=pltpu.CompilerParams(
            vmem_limit_bytes=VMEM_LIMIT, collective_id=0, has_side_effects=True
        ),
    )(
        keep_mask, keep_rate, exit_scales,
        tokens, groups, gain1, gain2, wk, wv, wq, cos, sin,
        wo, wg, wu, wd, cotangent,
    )

    wide = pl.BlockSpec((width, 2 * LANES), lambda i: (0, jnp.maximum(i - 1, 0)))
    lines = pl.BlockSpec((width // chunks, rows), lambda i: (jnp.maximum(i - 1, 0), 0))
    line = pl.BlockSpec((width,), lambda i: (0,))
    small = [(nq, width), (width, nq), (nk, width), (nk, width)]
    (gate_grad, up_grad, down_grad, output_grad, query_grad, key_grad, value_grad, gain1_grad, gain2_grad, layer_out, input_grad) = pl.pallas_call(
        functools.partial(unpack_kernel, chunks),
        grid=(count,),
        out_shape=[jax.ShapeDtypeStruct((width, ff), F32)] * 3
        + [jax.ShapeDtypeStruct(shape, F32) for shape in small + [(width,), (width,)]]
        + [jax.ShapeDtypeStruct((width, rows), t) for t in (BF16, F32)],
        in_specs=[
            pl.BlockSpec((1, 2, part_rows, LANES), lambda i: ((i + chunks) % count, 0, 0, 0)),
            pl.BlockSpec(tails.shape, lambda i: (0,) * 4),
            pl.BlockSpec(gain_shape, lambda i: (0, 0)),
            lines,
            lines,
        ],
        out_specs=[wide] * 3 + [hbm] * 4 + [line] * 2 + [lines] * 2,
        scratch_shapes=[pltpu.VMEM(shape, F32) for shape in small] + [dma((4,))],
        compiler_params=pltpu.CompilerParams(vmem_limit_bytes=VMEM_LIMIT),
    )(parts, tails, gains, layer_out, input_grad)
    return (
        layer_out.T[None],
        input_grad.T[None],
        query_grad,
        key_grad.T,
        value_grad.T,
        output_grad,
        gate_grad,
        up_grad,
        down_grad.T,
        gain1_grad,
        gain2_grad,
    )


def solution(mesh):
    local = P("seq", "blk", None)
    pair = P("seq", "blk")
    placed = (local, pair, pair, P("seq")) + (P(),) * 11 + (local,)
    return jax.shard_map(
        functools.partial(body, (mesh.shape["seq"], mesh.shape["blk"])),
        mesh=mesh,
        in_specs=placed,
        out_specs=(local, local) + (P(),) * 9,
        check_vma=False,
    )
```
